256 devices in a mesh: section: 8 (over z_hi, y), seq: 32 (over z_lo, x, core).
Axes of the slice: x: 4, y: 4, z: 8 (z_hi: 2, z_lo: 4; z = z_hi * 4 + z_lo), core: 2. Of those that a mesh axis runs over, the one named last changes fastest.
Arguments:
- latents: bfloat16 [8, 4096, 1408], P('section', 'seq'), may hold values from -6 to 6
- skip_weight: bfloat16 [8, 1408, 1408], P('section'), may hold values from -0.109375 to 0.109375
- project_in: bfloat16 [8, 1408, 2112], P('section'), as said below
- project_out: bfloat16 [8, 704, 1408], P('section'), may hold values from -0.21875 to 0.21875
- upstream: bfloat16 [8, 4096, 1408], P('section', 'seq'), may hold values from -6 to 6
Outputs:
- block_out: bfloat16 [8, 4096, 1408], P('section', 'seq')
- grad_latents: bfloat16 [8, 4096, 1408], P('section', 'seq')
The draws below stay inside these ranges and needn't reach their ends.
Inputs may be any that keep to these rules, and one draw needn't show every extreme that they name: project_in is a dense projection matrix.
All inputs are finite; a program needn't handle non-finite values.
Results may differ from the reference program's by a relative error of at most 0.028.
Values may be sent and summed in bfloat16 or wider, within the bound.
A program may use at most 192 MiB of HBM per device.

```python
import math
import jax
import jax.numpy as jnp
from jax import lax

D = 1408
HEADS = 8
HEAD_DIM = 88
TOK_DEV = 128
TOKENS = 4096
N_SECTION = 8


def draw_project_in(key, part):
    key = jax.random.fold_in(key, 11)
    head_width = HEADS * HEAD_DIM
    matrix = jax.random.normal(key, (N_SECTION, D, 3 * head_width), jnp.float32) * (1.6 / math.sqrt(D))
    return matrix.astype(jnp.bfloat16)


def block_scale(stream_key, extent, shards, least, largest):
    loudness = 1.0
    for position, parts in shards:
        draws = jax.random.uniform(jax.random.fold_in(jax.random.fold_in(stream_key, 6), position), (parts,), jnp.float32, least / len(shards), largest / len(shards))
        loudness = loudness * jnp.repeat(jnp.exp(draws), extent[position] // parts).reshape((-1,) + (1,) * (len(extent) - 1 - position))
    return loudness


def scatter_about(stream_key, dims, deviation, bound, cuts=(), held_as=jnp.bfloat16):
    entries = jax.random.normal(stream_key, dims, jnp.float32) * deviation
    if len(cuts) > 0:
        entries = block_scale(stream_key, dims, cuts, -0.22, 0.18) * entries
    return jnp.clip(entries, min=-bound, max=bound).astype(held_as)


def setup_inputs(seed: int = 0) -> dict:
    key_of = jax.random.split(jax.random.key(seed), 6)
    return {
        "latents": scatter_about(key_of[0], (N_SECTION, TOKENS, D), 1.0, 6.0, ((0, 8), (1, 32))),
        "skip_weight": scatter_about(key_of[1], (N_SECTION, D, D), (2 * D) ** -0.5, 0.109375, ((0, 8),)),
        "project_in": draw_project_in(jax.random.fold_in(key_of[5], 71), 0),
        "project_out": scatter_about(key_of[3], (N_SECTION, HEADS * HEAD_DIM, D), (HEADS * HEAD_DIM) ** -0.5, 0.21875, ((0, 8),)),
        "upstream": scatter_about(key_of[4], (N_SECTION, TOKENS, D), 1.0, 6.0, ((0, 8), (1, 32))),
    }


EPSILON = 1e-06

def layer_norm(vector):
    center = vector - lax.optimization_barrier(jnp.mean(vector, -1, keepdims=True))
    spread = lax.optimization_barrier(jnp.mean(center * center, -1, keepdims=True))
    return center * lax.rsqrt(spread + EPSILON)

def softmax_rows(queries, gathered_keys, score_scale):
    scores = jnp.einsum('rhd,lhd->hrl', queries.astype(jnp.float32), gathered_keys.astype(jnp.float32)) * score_scale
    row_top = lax.optimization_barrier(jnp.max(scores, -1, keepdims=True))
    lifted_rows = jnp.exp(scores - row_top)
    return lifted_rows / lax.optimization_barrier(jnp.sum(lifted_rows, -1, keepdims=True))

def block_pass(block_input, weight_in, weight_out, gradient):
    length = block_input.shape[0]
    head_width = HEADS * HEAD_DIM
    score_scale = 1.0 / math.sqrt(HEAD_DIM)
    normed, norm_back = jax.vjp(layer_norm, block_input.astype(jnp.float32))
    projections = jnp.dot(normed.astype(jnp.bfloat16), weight_in, preferred_element_type=jnp.float32).astype(jnp.bfloat16)
    queries = projections[:, :head_width].reshape(length, HEADS, HEAD_DIM)
    all_keys = projections[:, head_width:2 * head_width].reshape(length, HEADS, HEAD_DIM)
    all_values = projections[:, 2 * head_width:].reshape(length, HEADS, HEAD_DIM)
    block_list = length // TOK_DEV
    query_blocks = queries.reshape(block_list, TOK_DEV, HEADS, HEAD_DIM)

    def forward_block(query_rows):
        attention = softmax_rows(query_rows, all_keys, score_scale)
        mixed = jnp.einsum('hrl,lhd->rhd', attention.astype(jnp.bfloat16).astype(jnp.float32), all_values.astype(jnp.float32))
        return mixed.astype(jnp.bfloat16)
    attended = lax.map(forward_block, query_blocks).reshape(length, head_width)
    block_out = (block_input.astype(jnp.float32) + jnp.dot(attended, weight_out, preferred_element_type=jnp.float32)).astype(jnp.bfloat16)
    grad_att = jnp.dot(gradient, weight_out.T, preferred_element_type=jnp.float32).astype(jnp.bfloat16)
    grad_heads = grad_att.reshape(length, HEADS, HEAD_DIM)
    row_delta = lax.optimization_barrier(jnp.sum(grad_heads.astype(jnp.float32) * attended.reshape(length, HEADS, HEAD_DIM).astype(jnp.float32), -1))

    def backward_block(running, pieces):
        query_rows, grad_rows, delta_rows = pieces
        attention = softmax_rows(query_rows, all_keys, score_scale)
        rounded = attention.astype(jnp.bfloat16)
        grad_prob = jnp.einsum('rhd,lhd->hrl', grad_rows.astype(jnp.float32), all_values.astype(jnp.float32))
        grad_score = (attention * (grad_prob - delta_rows.T[:, :, None]) * score_scale).astype(jnp.bfloat16)
        grad_q = jnp.einsum('hrl,lhd->rhd', grad_score.astype(jnp.float32), all_keys.astype(jnp.float32)).astype(jnp.bfloat16)
        key_term = jnp.einsum('hrl,rhd->lhd', grad_score.astype(jnp.float32), query_rows.astype(jnp.float32)).astype(jnp.bfloat16)
        value_term = jnp.einsum('hrl,rhd->lhd', rounded.astype(jnp.float32), grad_rows.astype(jnp.float32)).astype(jnp.bfloat16)
        key_term, value_term = lax.optimization_barrier((key_term, value_term))
        return ((running[0] + key_term.astype(jnp.float32), running[1] + value_term.astype(jnp.float32)), grad_q)
    zeros = jnp.zeros((length, HEADS, HEAD_DIM), jnp.float32)
    pieces = (query_blocks, grad_heads.reshape(block_list, TOK_DEV, HEADS, HEAD_DIM), row_delta.reshape(block_list, TOK_DEV, HEADS))
    (key_sum, value_sum), grad_q = lax.scan(backward_block, (zeros, zeros), pieces)
    grad_proj = jnp.concatenate([grad_q.reshape(length, head_width), key_sum.astype(jnp.bfloat16).reshape(length, head_width), value_sum.astype(jnp.bfloat16).reshape(length, head_width)], axis=1)
    grad_normed = jnp.dot(grad_proj, weight_in.T, preferred_element_type=jnp.float32)
    grad_input = gradient.astype(jnp.float32) + norm_back(grad_normed)[0]
    return (block_out, grad_input)

def reference(latents, skip_weight, project_in, project_out, upstream):
    half_count = N_SECTION // 2
    skips = [jnp.dot(latents[section_id], skip_weight[section_id], preferred_element_type=jnp.float32).astype(jnp.bfloat16) for section_id in range(half_count)]
    outputs = [None] * N_SECTION
    gradients = [None] * N_SECTION
    returned = [None] * N_SECTION
    for section_id in range(half_count, N_SECTION):
        partner = N_SECTION - 1 - section_id
        mixed_sum = jnp.dot(latents[section_id], skip_weight[section_id], preferred_element_type=jnp.float32) + skips[partner].astype(jnp.float32)
        joined_value, mix_back = jax.vjp(layer_norm, mixed_sum)
        block_out, grad_input = block_pass(joined_value.astype(jnp.bfloat16), project_in[section_id], project_out[section_id], upstream[section_id])
        grad_mixed = mix_back(grad_input)[0].astype(jnp.bfloat16)
        returned[partner] = grad_mixed
        outputs[section_id] = block_out
        gradients[section_id] = jnp.dot(grad_mixed, skip_weight[section_id].T, preferred_element_type=jnp.float32).astype(jnp.bfloat16)
    for section_id in range(half_count):
        block_out, grad_input = block_pass(latents[section_id], project_in[section_id], project_out[section_id], upstream[section_id])
        outputs[section_id] = block_out
        through = jnp.dot(returned[section_id], skip_weight[section_id].T, preferred_element_type=jnp.float32)
        gradients[section_id] = (grad_input + through).astype(jnp.bfloat16)
    return (jnp.stack(outputs), jnp.stack(gradients))
```

```python
import functools
import math

import jax
import jax.numpy as jnp
from jax import lax
from jax.experimental import pallas as pl
from jax.experimental.pallas import tpu as pltpu
from jax.sharding import PartitionSpec as P

HEADS = 8
EPSILON = 1e-06
CORES = 2
CHUNK = 128
PAD = 8

MESH = pl.DeviceIdType.MESH
F32 = jnp.float32
BF16 = jnp.bfloat16

GRAD, KV, QUERY, OUT, DKV, DQ = range(6)


def dot(a, b):
    return jnp.dot(a, b, preferred_element_type=F32)


def spans(extent, width):
    return [(at, min(width, extent - at)) for at in range(0, extent, width)]


def stats(value):
    center = value - jnp.mean(value, -1, keepdims=True)
    rate = lax.rsqrt(jnp.mean(center * center, -1, keepdims=True) + EPSILON)
    return center * rate, rate


def norm_back(hat, rate, grad):
    inner = jnp.mean(grad * hat, -1, keepdims=True)
    return rate * (grad - jnp.mean(grad, -1, keepdims=True) - hat * inner)


def kernel(
    rows_z,
    rows_x,
    lat_hbm,
    skipw_hbm,
    win_hbm,
    wout_hbm,
    ups_hbm,
    out_hbm,
    glat_hbm,
    lat,
    skipw,
    win,
    wout,
    ups,
    skip_send,
    skip_recv,
    mixed,
    binput,
    normed,
    flip,
    projt,
    gsend,
    kvsend,
    qsend,
    gt,
    qt,
    kv,
    knat,
    vnat,
    qnat,
    gnat,
    exps,
    tops,
    facs,
    delta,
    oacc,
    qacc,
    kvacc,
    ot,
    dqt,
    dkvpart,
    dkvrecv,
    dkvown,
    ofin,
    dqfin,
    dkvfin,
    gpt,
    gnt,
    ginput,
    gm_send,
    gm_recv,
    outv,
    load_sem,
    store_sem,
    col_send,
    col_recv,
    kvx_send,
    kvx_recv,
    dkvx_send,
    dkvx_recv,
    skip_ssem,
    skip_rsem,
    gm_ssem,
    gm_rsem,
):
    sections = lax.axis_size("section")
    section = lax.axis_index("section")
    place = lax.axis_index("seq")
    zl = place // (rows_x * CORES)
    x = lax.rem(place // CORES, rows_x)
    core = lax.rem(place, CORES)
    is_upper = section >= sections // 2
    is_lower = jnp.logical_not(is_upper)
    column = rows_z * CORES
    me = zl * CORES + core

    tok, width = lat.shape
    head_width = wout.shape[0]
    depth = head_width // column
    padded = depth + PAD
    span = column * CHUNK
    scale = 1.0 / math.sqrt(depth)
    rate2 = scale * math.log2(math.e)
    q_tile = 256

    def col_dev(index):
        return {
            "section": section,
            "seq": ((index // CORES) * rows_x + x) * CORES + lax.rem(index, CORES),
        }

    def x_dev(offset):
        there = lax.rem(x + offset + rows_x, rows_x)
        return {"section": section, "seq": (zl * rows_x + there) * CORES + core}

    partner = {"section": sections - 1 - section, "seq": place}

    def remote(src, dst, send, recv, device):
        return pltpu.make_async_remote_copy(
            src_ref=src,
            dst_ref=dst,
            send_sem=send,
            recv_sem=recv,
            device_id=device,
            device_id_type=MESH,
        )

    def lanes(index):
        return pl.ds(pl.multiple_of(index * CHUNK, CHUNK), CHUNK)

    def col_copy(kind, step, src, dst):
        there = lax.rem(me + step, column)
        return remote(
            src(there),
            dst(me),
            col_send.at[kind, step],
            col_recv.at[kind, step],
            col_dev(there),
        )

    def col_own(kind, src, dst):
        return pltpu.make_async_copy(src(me), dst(me), col_recv.at[kind, 0])

    def col_start(kind, src, dst):
        col_own(kind, src, dst).start()

        @pl.loop(1, column)
        def _(step):
            col_copy(kind, step, src, dst).start()

    def col_arrived(kind, src, dst):
        col_own(kind, src, dst).wait()

        @pl.loop(1, column)
        def _(step):
            col_copy(kind, step, src, dst).wait_recv()

    def col_sent(kind, src, dst):
        @pl.loop(1, column)
        def _(step):
            col_copy(kind, step, src, dst).wait_send()

    g_pair = (lambda j: gsend.at[j], lambda j: gt.at[:, lanes(j)])
    kv_pair = (lambda j: kvsend.at[j], lambda j: kv.at[0, :, lanes(j)])
    q_pair = (lambda j: qsend.at[j], lambda j: qt.at[:, lanes(j)])
    o_pair = (lambda j: ot.at[:, lanes(j)], lambda j: ofin.at[j])
    dkv_pair = (lambda j: dkvown.at[:, lanes(j)], lambda j: dkvfin.at[j])
    dq_pair = (lambda j: dqt.at[:, lanes(j)], lambda j: dqfin.at[j])

    loads = [
        pltpu.make_async_copy(src, dst, load_sem.at[i])
        for i, (src, dst) in enumerate(
            [
                (lat_hbm, lat),
                (skipw_hbm, skipw),
                (ups_hbm, ups),
                (wout_hbm, wout),
                (win_hbm, win),
            ]
        )
    ]
    for load in loads:
        load.start()

    barrier = pltpu.get_barrier_semaphore()
    peers = [col_dev(lax.rem(me + step, column)) for step in range(1, column)]
    peers += [x_dev(offset) for offset in range(1, rows_x)]
    peers.append(partner)
    for peer in peers:
        pl.semaphore_signal(barrier, inc=1, device_id=peer, device_id_type=MESH)

    skip_spans = spans(width, 512)

    def skip_copy(i):
        at, size = skip_spans[i]
        cols = pl.ds(at, size)
        return remote(
            skip_send.at[:, cols],
            skip_recv.at[:, cols],
            skip_ssem.at[i],
            skip_rsem.at[i],
            partner,
        )

    loads[0].wait()
    loads[1].wait()
    for i, (at, size) in enumerate(skip_spans):
        product = dot(lat[...], skipw[:, pl.ds(at, size)])
        mixed[:, pl.ds(at, size)] = product
        skip_send[:, pl.ds(at, size)] = product.astype(BF16)
        if i == 0:
            pl.semaphore_wait(barrier, len(peers))

        @pl.when(is_lower)
        def _():
            skip_copy(i).start()

    def turn(source, i):
        block = source[:, pl.ds(i * CHUNK, CHUNK)]
        flip[pl.ds(i * CHUNK, CHUNK), :] = block.astype(F32).T.astype(BF16)

    loads[2].wait()
    for i in range(width // CHUNK):
        turn(ups, i)
    loads[3].wait()
    blank = jnp.zeros((PAD, CHUNK), F32)

    @pl.loop(0, column // 2)
    def _(i):
        rows = pl.ds(pl.multiple_of(i * 2 * depth, 16), 2 * depth)
        pair = dot(wout[rows, :], flip[...])
        gsend[2 * i] = jnp.concatenate([blank, pair[:depth]], 0).astype(BF16)
        gsend[2 * i + 1] = jnp.concatenate([blank, pair[depth:]], 0).astype(BF16)

    col_start(GRAD, *g_pair)

    row_spans = spans(tok, 32)

    @pl.when(is_upper)
    def _():
        for i in range(len(skip_spans)):
            skip_copy(i).wait_recv()
        for at, size in row_spans:
            rows = pl.ds(at, size)
            total = mixed[rows, :] + skip_recv[rows, :].astype(F32)
            mixed[rows, :] = total
            binput[rows, :] = stats(total)[0].astype(BF16)

    @pl.when(is_lower)
    def _():
        binput[...] = lat[...]

    for at, size in row_spans:
        rows = pl.ds(at, size)
        normed[rows, :] = stats(binput[rows, :].astype(F32))[0].astype(BF16)

    loads[4].wait()
    step_cols = 256
    full = 3 * head_width // step_cols
    first = head_width // step_cols

    def project(at, size):
        product = dot(normed[...], win[:, pl.ds(at, size)])
        projt[pl.ds(at, size), :] = product.T

    @pl.loop(first, full)
    def _(i):
        project(pl.multiple_of(i * step_cols, step_cols), step_cols)

    if full * step_cols < 3 * head_width:
        project(full * step_cols, 3 * head_width - full * step_cols)
    for head in range(column):
        keys = projt[pl.ds(head_width + head * depth, depth), :]
        values = projt[pl.ds(2 * head_width + head * depth, depth), :]
        kvsend[head] = jnp.concatenate([keys, values], 0).astype(BF16)
    col_start(KV, *kv_pair)

    @pl.loop(0, first)
    def _(i):
        project(pl.multiple_of(i * step_cols, step_cols), step_cols)

    for head in range(column):
        queries = projt[pl.ds(head * depth, depth), :]
        qsend[head] = jnp.concatenate([queries, blank], 0).astype(BF16)
    col_start(QUERY, *q_pair)

    def kvx_copy(offset, step):
        piece = lanes(lax.rem(me + column - step, column))
        return remote(
            kv.at[0, :, piece],
            kv.at[offset, :, piece],
            kvx_send.at[offset - 1, step],
            kvx_recv.at[offset - 1, step],
            x_dev(offset),
        )

    col_own(KV, *kv_pair).wait()
    for offset in range(1, rows_x):
        kvx_copy(offset, 0).start()

    @pl.loop(1, column)
    def _(step):
        col_copy(KV, step, *kv_pair).wait_recv()
        for offset in range(1, rows_x):
            kvx_copy(offset, step).start()

    def natural(block):
        lane = lax.broadcasted_iota(jnp.int32, (q_tile, padded), 1)
        for at, size in spans(span, q_tile):
            cols = pl.ds(at, size)
            keys = kv[block, :padded, cols].astype(F32).T
            values = kv[block, depth - PAD :, cols].astype(F32).T
            knat[block, cols, :] = keys.astype(BF16)
            vnat[block, cols, :] = jnp.where(lane < PAD, 1.0, values).astype(BF16)

    col_arrived(GRAD, *g_pair)
    col_arrived(QUERY, *q_pair)
    for at, size in spans(span, q_tile):
        rows = pl.ds(at, size)
        qnat[rows, :] = qt[:, rows].astype(F32).T.astype(BF16)
        gnat[rows, :] = gt[:, rows].astype(F32).T

    order = [0] + sorted(range(1, rows_x), key=lambda d: min(d, rows_x - d))

    def forward(block, is_first):
        natural(block)

        @pl.loop(0, span // q_tile)
        def _(i):
            rows = pl.ds(pl.multiple_of(i * q_tile, q_tile), q_tile)
            scores = dot(qnat[rows, :], kv[block, :padded, :])
            top = jnp.max(scores, -1, keepdims=True)
            if not is_first:
                before = tops[order[order.index(block) - 1], rows, :]
                top = jnp.maximum(top, before)
            tops[block, rows, :] = top
            lifted = jnp.exp2((scores - top) * rate2).astype(BF16)
            exps[block, rows, :] = lifted
            term = dot(lifted, vnat[block])
            if not is_first:
                term += oacc[rows, :] * jnp.exp2((before - top) * rate2)
            oacc[rows, :] = term

    for n, block in enumerate(order):
        if n > 0:

            @pl.loop(0, column)
            def _(step):
                kvx_copy(block, step).wait_recv()

        forward(block, n == 0)

    for at, size in spans(span, q_tile):
        rows = pl.ds(at, size)
        total = oacc[rows, :]
        inverse = 1.0 / total[:, :1]
        mixed_values = (total * inverse).astype(BF16).astype(F32)
        ot[:, rows] = mixed_values.T.astype(BF16)
        delta[rows, :] = jnp.sum(gnat[rows, :] * mixed_values, -1, keepdims=True)
        last = tops[order[-1], rows, :]
        for block in range(rows_x):
            lift = jnp.exp2((tops[block, rows, :] - last) * rate2)
            facs[block, rows, :] = lift * inverse
        qacc[rows, :] = jnp.zeros((size, padded), F32)
    col_start(OUT, *o_pair)

    def dkvx_copy(offset):
        return remote(
            dkvpart.at[offset - 1],
            dkvrecv.at[offset - 1],
            dkvx_send.at[offset - 1],
            dkvx_recv.at[offset - 1],
            x_dev(-offset),
        )

    def backward(block):
        kvacc[...] = jnp.zeros_like(kvacc)

        @pl.loop(0, span // q_tile)
        def _(i):
            rows = pl.ds(pl.multiple_of(i * q_tile, q_tile), q_tile)
            factor = facs[block, rows, :]
            grads = gnat[rows, :] * factor
            shift = delta[rows, :] * factor
            lifted = exps[block, rows, :]
            back = dot(grads.astype(BF16), kv[block, depth - PAD :, :]) - shift
            gscore = (lifted.astype(F32) * back).astype(BF16)
            qacc[rows, :] += dot(gscore, knat[block])
            kvacc[:padded, :] += dot(qt[:, rows], gscore)
            kvacc[padded:, :] += dot(grads.T.astype(BF16), lifted)

    def joined(at, size):
        cols = pl.ds(at, size)
        keys = kvacc[:padded, cols] * scale
        values = kvacc[padded:, cols]
        middle = keys[depth - PAD :] + values[: 2 * PAD]
        return jnp.concatenate([keys[: depth - PAD], middle, values[2 * PAD :]], 0)

    for block in reversed(order[1:]):
        backward(block)
        for at, size in spans(span, q_tile):
            dkvpart[block - 1, :, pl.ds(at, size)] = joined(at, size).astype(BF16)
        dkvx_copy(block).start()
    backward(0)
    for offset in range(1, rows_x):
        dkvx_copy(offset).wait_recv()
    for at, size in spans(span, q_tile):
        cols = pl.ds(at, size)
        total = joined(at, size)
        for other in range(rows_x - 1):
            total += dkvrecv[other, :, cols].astype(F32)
        dkvown[:, cols] = total.astype(BF16)
    col_start(DKV, *dkv_pair)
    for at, size in spans(span, q_tile):
        rows = pl.ds(at, size)
        dqt[:, rows] = (qacc[rows, :] * scale).T.astype(BF16)
    col_start(DQ, *dq_pair)

    col_arrived(OUT, *o_pair)
    for head in range(column):
        rows = pl.ds(head * depth, depth)
        projt[rows, :] = ofin[head].astype(F32)[PAD:]
    attended = projt[:head_width, :].T.astype(BF16)
    for at, size in spans(width, 512):
        cols = pl.ds(at, size)
        term = dot(attended, wout[:, cols])
        outv[:, cols] = (binput[:, cols].astype(F32) + term).astype(BF16)
    out_store = pltpu.make_async_copy(outv, out_hbm, store_sem.at[0])
    out_store.start()

    col_arrived(DKV, *dkv_pair)
    for head in range(column):
        both = dkvfin[head].astype(F32)
        projt[pl.ds(head_width + head * depth, depth), :] = both[:depth]
        projt[pl.ds(2 * head_width + head * depth, depth), :] = both[depth:]
    col_arrived(DQ, *dq_pair)
    for head in range(column):
        projt[pl.ds(head * depth, depth), :] = dqfin[head].astype(F32)[:depth]
    gpt[...] = projt[...].astype(BF16)
    half = width // 2

    @pl.loop(0, 2)
    def _(i):
        rows = pl.ds(pl.multiple_of(i * half, 16), half)
        gnt[rows, :] = dot(win[rows, :], gpt[...])

    for i in range(width // CHUNK):
        ginput[:, pl.ds(i * CHUNK, CHUNK)] = gnt[pl.ds(i * CHUNK, CHUNK), :].T

    def gm_copy(i):
        rows = pl.ds(*row_spans[i])
        return remote(
            gm_send.at[rows], gm_recv.at[rows], gm_ssem.at[i], gm_rsem.at[i], partner
        )

    for i, (at, size) in enumerate(row_spans):
        rows = pl.ds(at, size)
        hat, rate = stats(binput[rows, :].astype(F32))
        grad = ups[rows, :].astype(F32) + norm_back(hat, rate, ginput[rows, :])
        ginput[rows, :] = grad

        @pl.when(is_upper)
        def _():
            hat, rate = stats(mixed[rows, :])
            gm_send[rows, :] = norm_back(hat, rate, ginput[rows, :]).astype(BF16)
            gm_copy(i).start()

    @pl.when(is_upper)
    def _():
        ginput[...] = jnp.zeros_like(ginput)
        for i in range(width // CHUNK):
            turn(gm_send, i)

    @pl.when(is_lower)
    def _():
        for i in range(len(row_spans)):
            gm_copy(i).wait_recv()
        for i in range(width // CHUNK):
            turn(gm_recv, i)

    @pl.loop(0, 2)
    def _(i):
        rows = pl.ds(pl.multiple_of(i * half, 16), half)
        gnt[rows, :] = dot(skipw[rows, :], flip[...])

    out_store.wait()
    for i in range(width // CHUNK):
        cols = pl.ds(i * CHUNK, CHUNK)
        term = ginput[:, cols] + gnt[pl.ds(i * CHUNK, CHUNK), :].T
        outv[:, cols] = term.astype(BF16)
    glat_store = pltpu.make_async_copy(outv, glat_hbm, store_sem.at[1])
    glat_store.start()

    for kind, pair in (
        (GRAD, g_pair),
        (KV, kv_pair),
        (QUERY, q_pair),
        (OUT, o_pair),
        (DKV, dkv_pair),
        (DQ, dq_pair),
    ):
        col_sent(kind, *pair)
    for offset in range(1, rows_x):

        @pl.loop(0, column)
        def _(step):
            kvx_copy(offset, step).wait_send()

        dkvx_copy(offset).wait_send()

    @pl.when(is_lower)
    def _():
        for i in range(len(skip_spans)):
            skip_copy(i).wait_send()

    @pl.when(is_upper)
    def _():
        for i in range(len(row_spans)):
            gm_copy(i).wait_send()

    glat_store.wait()


def body(rows_z, rows_x, latents, skip_weight, project_in, project_out, upstream):
    tok, width = latents.shape[1:]
    head_width = project_out.shape[1]
    column = rows_z * CORES
    depth = head_width // column
    padded = depth + PAD
    span = column * tok
    n_skip = len(spans(width, 512))
    n_rows = len(spans(tok, 32))
    wide = (tok, width)
    vmem = pltpu.VMEM
    dma = pltpu.SemaphoreType.DMA
    scratch = [
        vmem(wide, BF16),
        vmem((width, width), BF16),
        vmem((width, 3 * head_width), BF16),
        vmem((head_width, width), BF16),
        vmem(wide, BF16),
        vmem(wide, BF16),
        vmem(wide, BF16),
        vmem(wide, F32),
        vmem(wide, BF16),
        vmem(wide, BF16),
        vmem((width, tok), BF16),
        vmem((3 * head_width, tok), F32),
        vmem((column, padded, tok), BF16),
        vmem((column, 2 * depth, tok), BF16),
        vmem((column, padded, tok), BF16),
        vmem((padded, span), BF16),
        vmem((padded, span), BF16),
        vmem((rows_x, 2 * depth, span), BF16),
        vmem((rows_x, span, padded), BF16),
        vmem((rows_x, span, padded), BF16),
        vmem((span, padded), BF16),
        vmem((span, padded), F32),
        vmem((rows_x, span, span), BF16),
        vmem((rows_x, span, 1), F32),
        vmem((rows_x, span, 1), F32),
        vmem((span, 1), F32),
        vmem((span, padded), F32),
        vmem((span, padded), F32),
        vmem((2 * padded, span), F32),
        vmem((padded, span), BF16),
        vmem((padded, span), BF16),
        vmem((rows_x - 1, 2 * depth, span), BF16),
        vmem((rows_x - 1, 2 * depth, span), BF16),
        vmem((2 * depth, span), BF16),
        vmem((column, padded, tok), BF16),
        vmem((column, padded, tok), BF16),
        vmem((column, 2 * depth, tok), BF16),
        vmem((3 * head_width, tok), BF16),
        vmem((width, tok), F32),
        vmem(wide, F32),
        vmem(wide, BF16),
        vmem(wide, BF16),
        vmem(wide, BF16),
        dma((5,)),
        dma((2,)),
        dma((6, column)),
        dma((6, column)),
        dma((rows_x - 1, column)),
        dma((rows_x - 1, column)),
        dma((rows_x - 1,)),
        dma((rows_x - 1,)),
        dma((n_skip,)),
        dma((n_skip,)),
        dma((n_rows,)),
        dma((n_rows,)),
    ]
    out, glat = pl.pallas_call(
        functools.partial(kernel, rows_z, rows_x),
        out_shape=[jax.ShapeDtypeStruct(wide, BF16)] * 2,
        in_specs=[pl.BlockSpec(memory_space=pl.ANY)] * 5,
        out_specs=[pl.BlockSpec(memory_space=pl.ANY)] * 2,
        scratch_shapes=scratch,
        compiler_params=pltpu.CompilerParams(
            collective_id=0, has_side_effects=True, vmem_limit_bytes=56 * 2**20
        ),
    )(latents[0], skip_weight[0], project_in[0], project_out[0], upstream[0])
    return out[None], glat[None]


def solution(mesh):
    rows_z = HEADS // CORES
    rows_x = mesh.shape["seq"] // HEADS
    return jax.shard_map(
        functools.partial(body, rows_z, rows_x),
        mesh=mesh,
        in_specs=(
            P("section", "seq", None),
            P("section", None, None),
            P("section", None, None),
            P("section", None, None),
            P("section", "seq", None),
        ),
        out_specs=(P("section", "seq", None), P("section", "seq", None)),
        check_vma=False,
    )
```

```python
import functools
import math

import jax
import jax.numpy as jnp
from jax import lax
from jax.experimental import pallas as pl
from jax.experimental.pallas import tpu as pltpu
from jax.sharding import PartitionSpec as P

HEADS = 8
EPSILON = 1e-06
CORES = 2
CHUNK = 128
PAD = 8

MESH = pl.DeviceIdType.MESH
F32 = jnp.float32
BF16 = jnp.bfloat16

GRAD, KV, QUERY, OUT, DKV, DQ = range(6)


def dot(a, b):
    return jnp.dot(a, b, preferred_element_type=F32)


def spans(extent, width):
    return [(at, min(width, extent - at)) for at in range(0, extent, width)]


def stats(value):
    center = value - jnp.mean(value, -1, keepdims=True)
    rate = lax.rsqrt(jnp.mean(center * center, -1, keepdims=True) + EPSILON)
    return center * rate, rate


def norm_back(hat, rate, grad):
    inner = jnp.mean(grad * hat, -1, keepdims=True)
    return rate * (grad - jnp.mean(grad, -1, keepdims=True) - hat * inner)


def kernel(
    rows_z,
    rows_x,
    lat_hbm,
    skipw_hbm,
    win_hbm,
    wout_hbm,
    ups_hbm,
    out_hbm,
    glat_hbm,
    lat,
    skipw,
    win,
    wout,
    ups,
    skip_send,
    skip_recv,
    mixed,
    binput,
    normed,
    flip,
    projt,
    gsend,
    kvsend,
    qsend,
    gt,
    qt,
    kv,
    knat,
    vnat,
    qnat,
    gnat,
    exps,
    tops,
    facs,
    delta,
    oacc,
    qacc,
    kvacc,
    ot,
    dqt,
    dkvpart,
    dkvrecv,
    dkvown,
    ofin,
    dqfin,
    dkvfin,
    gproj,
    gnt,
    ginput,
    gm_send,
    gm_recv,
    outv,
    load_sem,
    store_sem,
    col_send,
    col_recv,
    kvx_send,
    kvx_recv,
    dkvx_send,
    dkvx_recv,
    skip_ssem,
    skip_rsem,
    gm_ssem,
    gm_rsem,
):
    sections = lax.axis_size("section")
    section = lax.axis_index("section")
    place = lax.axis_index("seq")
    zl = place // (rows_x * CORES)
    x = lax.rem(place // CORES, rows_x)
    core = lax.rem(place, CORES)
    is_upper = section >= sections // 2
    is_lower = jnp.logical_not(is_upper)
    column = rows_z * CORES
    me = zl * CORES + core

    tok, width = lat.shape
    head_width = wout.shape[0]
    depth = head_width // column
    padded = depth + PAD
    span = column * CHUNK
    scale = 1.0 / math.sqrt(depth)
    rate2 = scale * math.log2(math.e)
    q_tile = 256

    def col_dev(index):
        return {
            "section": section,
            "seq": ((index // CORES) * rows_x + x) * CORES + lax.rem(index, CORES),
        }

    def x_dev(offset):
        there = lax.rem(x + offset + rows_x, rows_x)
        return {"section": section, "seq": (zl * rows_x + there) * CORES + core}

    partner = {"section": sections - 1 - section, "seq": place}

    def remote(src, dst, send, recv, device):
        return pltpu.make_async_remote_copy(
            src_ref=src,
            dst_ref=dst,
            send_sem=send,
            recv_sem=recv,
            device_id=device,
            device_id_type=MESH,
        )

    def lanes(index):
        return pl.ds(pl.multiple_of(index * CHUNK, CHUNK), CHUNK)

    def col_copy(kind, step, src, dst):
        there = lax.rem(me + step, column)
        return remote(
            src(there),
            dst(me),
            col_send.at[kind, step],
            col_recv.at[kind, step],
            col_dev(there),
        )

    def col_own(kind, src, dst):
        return pltpu.make_async_copy(src(me), dst(me), col_recv.at[kind, 0])

    def col_start(kind, src, dst):
        col_own(kind, src, dst).start()

        @pl.loop(1, column)
        def _(step):
            col_copy(kind, step, src, dst).start()

    def col_arrived(kind, src, dst):
        col_own(kind, src, dst).wait()

        @pl.loop(1, column)
        def _(step):
            col_copy(kind, step, src, dst).wait_recv()

    def col_sent(kind, src, dst):
        @pl.loop(1, column)
        def _(step):
            col_copy(kind, step, src, dst).wait_send()

    g_pair = (lambda j: gsend.at[j], lambda j: gt.at[:, lanes(j)])
    kv_pair = (lambda j: kvsend.at[j], lambda j: kv.at[0, :, lanes(j)])
    q_pair = (lambda j: qsend.at[j], lambda j: qt.at[:, lanes(j)])
    o_pair = (lambda j: ot.at[:, lanes(j)], lambda j: ofin.at[j])
    dkv_pair = (lambda j: dkvown.at[:, lanes(j)], lambda j: dkvfin.at[j])
    dq_pair = (lambda j: dqt.at[:, lanes(j)], lambda j: dqfin.at[j])

    loads = [
        pltpu.make_async_copy(src, dst, load_sem.at[i])
        for i, (src, dst) in enumerate(
            [
                (lat_hbm, lat),
                (skipw_hbm, skipw),
                (ups_hbm, ups),
                (wout_hbm, wout),
                (win_hbm, win),
            ]
        )
    ]
    for load in loads:
        load.start()

    barrier = pltpu.get_barrier_semaphore()
    peers = [col_dev(lax.rem(me + step, column)) for step in range(1, column)]
    peers += [x_dev(offset) for offset in range(1, rows_x)]
    peers.append(partner)
    for peer in peers:
        pl.semaphore_signal(barrier, inc=1, device_id=peer, device_id_type=MESH)

    skip_spans = spans(width, 512)

    def skip_copy(i):
        at, size = skip_spans[i]
        cols = pl.ds(at, size)
        return remote(
            skip_send.at[:, cols],
            skip_recv.at[:, cols],
            skip_ssem.at[i],
            skip_rsem.at[i],
            partner,
        )

    loads[0].wait()
    loads[1].wait()
    for i, (at, size) in enumerate(skip_spans):
        product = dot(lat[...], skipw[:, pl.ds(at, size)])
        mixed[:, pl.ds(at, size)] = product
        skip_send[:, pl.ds(at, size)] = product.astype(BF16)
        if i == 0:
            pl.semaphore_wait(barrier, len(peers))

        @pl.when(is_lower)
        def _():
            skip_copy(i).start()

    def turn(source, i):
        block = source[:, pl.ds(i * CHUNK, CHUNK)]
        flip[pl.ds(i * CHUNK, CHUNK), :] = block.astype(F32).T.astype(BF16)

    loads[2].wait()
    for i in range(width // CHUNK):
        turn(ups, i)
    loads[3].wait()
    blank = jnp.zeros((PAD, CHUNK), F32)

    @pl.loop(0, column // 2)
    def _(i):
        rows = pl.ds(pl.multiple_of(i * 2 * depth, 16), 2 * depth)
        pair = dot(wout[rows, :], flip[...])
        gsend[2 * i] = jnp.concatenate([blank, pair[:depth]], 0).astype(BF16)
        gsend[2 * i + 1] = jnp.concatenate([blank, pair[depth:]], 0).astype(BF16)

    col_start(GRAD, *g_pair)

    row_spans = spans(tok, 32)

    @pl.when(is_upper)
    def _():
        for i in range(len(skip_spans)):
            skip_copy(i).wait_recv()
        for at, size in row_spans:
            rows = pl.ds(at, size)
            total = mixed[rows, :] + skip_recv[rows, :].astype(F32)
            mixed[rows, :] = total
            binput[rows, :] = stats(total)[0].astype(BF16)

    @pl.when(is_lower)
    def _():
        binput[...] = lat[...]

    for at, size in row_spans:
        rows = pl.ds(at, size)
        normed[rows, :] = stats(binput[rows, :].astype(F32))[0].astype(BF16)

    for i in range(width // CHUNK):
        turn(normed, i)
    loads[4].wait()

    def project(part):
        rows = pl.ds(pl.multiple_of(part * head_width, 16), head_width)
        projt[rows, :] = dot(win[rows, :], flip[...])

    @pl.loop(1, 3)
    def _(part):
        project(part)

    for head in range(column):
        keys = projt[pl.ds(head_width + head * depth, depth), :]
        values = projt[pl.ds(2 * head_width + head * depth, depth), :]
        kvsend[head] = jnp.concatenate([keys, values], 0).astype(BF16)
    col_start(KV, *kv_pair)
    project(0)
    for head in range(column):
        queries = projt[pl.ds(head * depth, depth), :]
        qsend[head] = jnp.concatenate([queries, blank], 0).astype(BF16)
    col_start(QUERY, *q_pair)

    def kvx_copy(offset, step):
        piece = lanes(lax.rem(me + column - step, column))
        return remote(
            kv.at[0, :, piece],
            kv.at[offset, :, piece],
            kvx_send.at[offset - 1, step],
            kvx_recv.at[offset - 1, step],
            x_dev(offset),
        )

    col_own(KV, *kv_pair).wait()
    for offset in range(1, rows_x):
        kvx_copy(offset, 0).start()

    @pl.loop(1, column)
    def _(step):
        col_copy(KV, step, *kv_pair).wait_recv()
        for offset in range(1, rows_x):
            kvx_copy(offset, step).start()

    def natural(block):
        lane = lax.broadcasted_iota(jnp.int32, (q_tile, padded), 1)
        for at, size in spans(span, q_tile):
            cols = pl.ds(at, size)
            keys = kv[block, :padded, cols].astype(F32).T
            values = kv[block, depth - PAD :, cols].astype(F32).T
            knat[block, cols, :] = keys.astype(BF16)
            vnat[block, cols, :] = jnp.where(lane < PAD, 1.0, values).astype(BF16)

    col_arrived(GRAD, *g_pair)
    col_arrived(QUERY, *q_pair)
    for at, size in spans(span, q_tile):
        rows = pl.ds(at, size)
        qnat[rows, :] = qt[:, rows].astype(F32).T.astype(BF16)
        gnat[rows, :] = gt[:, rows].astype(F32).T

    order = [0] + sorted(range(1, rows_x), key=lambda d: min(d, rows_x - d))

    def forward(block, is_first):
        natural(block)

        @pl.loop(0, span // q_tile)
        def _(i):
            rows = pl.ds(pl.multiple_of(i * q_tile, q_tile), q_tile)
            scores = dot(qnat[rows, :], kv[block, :padded, :])
            top = jnp.max(scores, -1, keepdims=True)
            if not is_first:
                before = tops[order[order.index(block) - 1], rows, :]
                top = jnp.maximum(top, before)
            tops[block, rows, :] = top
            lifted = jnp.exp2((scores - top) * rate2).astype(BF16)
            exps[block, rows, :] = lifted
            term = dot(lifted, vnat[block])
            if not is_first:
                term += oacc[rows, :] * jnp.exp2((before - top) * rate2)
            oacc[rows, :] = term

    for n, block in enumerate(order):
        if n > 0:

            @pl.loop(0, column)
            def _(step):
                kvx_copy(block, step).wait_recv()

        forward(block, n == 0)

    for at, size in spans(span, q_tile):
        rows = pl.ds(at, size)
        total = oacc[rows, :]
        inverse = 1.0 / total[:, :1]
        mixed_values = (total * inverse).astype(BF16).astype(F32)
        ot[:, rows] = mixed_values.T.astype(BF16)
        delta[rows, :] = jnp.sum(gnat[rows, :] * mixed_values, -1, keepdims=True)
        last = tops[order[-1], rows, :]
        for block in range(rows_x):
            lift = jnp.exp2((tops[block, rows, :] - last) * rate2)
            facs[block, rows, :] = lift * inverse
        qacc[rows, :] = jnp.zeros((size, padded), F32)
    col_start(OUT, *o_pair)

    def dkvx_copy(offset):
        return remote(
            dkvpart.at[offset - 1],
            dkvrecv.at[offset - 1],
            dkvx_send.at[offset - 1],
            dkvx_recv.at[offset - 1],
            x_dev(-offset),
        )

    def backward(block):
        kvacc[...] = jnp.zeros_like(kvacc)

        @pl.loop(0, span // q_tile)
        def _(i):
            rows = pl.ds(pl.multiple_of(i * q_tile, q_tile), q_tile)
            factor = facs[block, rows, :]
            grads = gnat[rows, :] * factor
            shift = delta[rows, :] * factor
            lifted = exps[block, rows, :]
            back = dot(grads.astype(BF16), kv[block, depth - PAD :, :]) - shift
            gscore = (lifted.astype(F32) * back).astype(BF16)
            qacc[rows, :] += dot(gscore, knat[block])
            kvacc[:padded, :] += dot(qt[:, rows], gscore)
            kvacc[padded:, :] += dot(grads.T.astype(BF16), lifted)

    def joined(at, size):
        cols = pl.ds(at, size)
        keys = kvacc[:padded, cols] * scale
        values = kvacc[padded:, cols]
        middle = keys[depth - PAD :] + values[: 2 * PAD]
        return jnp.concatenate([keys[: depth - PAD], middle, values[2 * PAD :]], 0)

    for block in reversed(order[1:]):
        backward(block)
        for at, size in spans(span, q_tile):
            dkvpart[block - 1, :, pl.ds(at, size)] = joined(at, size).astype(BF16)
        dkvx_copy(block).start()
    backward(0)
    for offset in range(1, rows_x):
        dkvx_copy(offset).wait_recv()
    for at, size in spans(span, q_tile):
        cols = pl.ds(at, size)
        total = joined(at, size)
        for other in range(rows_x - 1):
            total += dkvrecv[other, :, cols].astype(F32)
        dkvown[:, cols] = total.astype(BF16)
    col_start(DKV, *dkv_pair)
    for at, size in spans(span, q_tile):
        rows = pl.ds(at, size)
        dqt[:, rows] = (qacc[rows, :] * scale).T.astype(BF16)
    col_start(DQ, *dq_pair)

    col_arrived(OUT, *o_pair)
    for head in range(column):
        rows = pl.ds(head * depth, depth)
        projt[rows, :] = ofin[head].astype(F32)[PAD:]
    attended = projt[:head_width, :].T.astype(BF16)
    for at, size in spans(width, 512):
        cols = pl.ds(at, size)
        term = dot(attended, wout[:, cols])
        outv[:, cols] = (binput[:, cols].astype(F32) + term).astype(BF16)
    out_store = pltpu.make_async_copy(outv, out_hbm, store_sem.at[0])
    out_store.start()

    col_arrived(DKV, *dkv_pair)
    for head in range(column):
        both = dkvfin[head].astype(F32)
        projt[pl.ds(head_width + head * depth, depth), :] = both[:depth]
        projt[pl.ds(2 * head_width + head * depth, depth), :] = both[depth:]
    col_arrived(DQ, *dq_pair)
    for head in range(column):
        projt[pl.ds(head * depth, depth), :] = dqfin[head].astype(F32)[:depth]
    for part in range(3):
        gproj[part] = projt[pl.ds(part * head_width, head_width), :].T.astype(BF16)
    for at, size in spans(width, 512):
        cols = pl.ds(at, size)
        ginput[:, cols] = sum(
            dot(gproj[part], win[pl.ds(part * head_width, head_width), cols])
            for part in range(3)
        )

    def gm_copy(i):
        rows = pl.ds(*row_spans[i])
        return remote(
            gm_send.at[rows], gm_recv.at[rows], gm_ssem.at[i], gm_rsem.at[i], partner
        )

    for i, (at, size) in enumerate(row_spans):
        rows = pl.ds(at, size)
        hat, rate = stats(binput[rows, :].astype(F32))
        grad = ups[rows, :].astype(F32) + norm_back(hat, rate, ginput[rows, :])
        ginput[rows, :] = grad

        @pl.when(is_upper)
        def _():
            hat, rate = stats(mixed[rows, :])
            gm_send[rows, :] = norm_back(hat, rate, ginput[rows, :]).astype(BF16)
            gm_copy(i).start()

    @pl.when(is_upper)
    def _():
        ginput[...] = jnp.zeros_like(ginput)
        for i in range(width // CHUNK):
            turn(gm_send, i)

    @pl.when(is_lower)
    def _():
        for i in range(len(row_spans)):
            gm_copy(i).wait_recv()
        for i in range(width // CHUNK):
            turn(gm_recv, i)

    half = width // 2

    @pl.loop(0, 2)
    def _(i):
        rows = pl.ds(pl.multiple_of(i * half, 16), half)
        gnt[rows, :] = dot(skipw[rows, :], flip[...])

    out_store.wait()
    for i in range(width // CHUNK):
        cols = pl.ds(i * CHUNK, CHUNK)
        term = ginput[:, cols] + gnt[pl.ds(i * CHUNK, CHUNK), :].T
        outv[:, cols] = term.astype(BF16)
    glat_store = pltpu.make_async_copy(outv, glat_hbm, store_sem.at[1])
    glat_store.start()

    for kind, pair in (
        (GRAD, g_pair),
        (KV, kv_pair),
        (QUERY, q_pair),
        (OUT, o_pair),
        (DKV, dkv_pair),
        (DQ, dq_pair),
    ):
        col_sent(kind, *pair)
    for offset in range(1, rows_x):

        @pl.loop(0, column)
        def _(step):
            kvx_copy(offset, step).wait_send()

        dkvx_copy(offset).wait_send()

    @pl.when(is_lower)
    def _():
        for i in range(len(skip_spans)):
            skip_copy(i).wait_send()

    @pl.when(is_upper)
    def _():
        for i in range(len(row_spans)):
            gm_copy(i).wait_send()

    glat_store.wait()


def settle(out, glat, out_hbm, glat_hbm, held, sem):
    ins = [
        pltpu.make_async_copy(out, held.at[0], sem.at[0]),
        pltpu.make_async_copy(glat, held.at[1], sem.at[1]),
    ]
    outs = [
        pltpu.make_async_copy(held.at[0], out_hbm, sem.at[2]),
        pltpu.make_async_copy(held.at[1], glat_hbm, sem.at[3]),
    ]
    for copy in ins:
        copy.start()
    for copy, onward in zip(ins, outs):
        copy.wait()
        onward.start()
    for copy in outs:
        copy.wait()


def body(rows_z, rows_x, latents, skip_weight, project_in, project_out, upstream):
    tok, width = latents.shape[1:]
    head_width = project_out.shape[1]
    column = rows_z * CORES
    depth = head_width // column
    padded = depth + PAD
    span = column * tok
    n_skip = len(spans(width, 512))
    n_rows = len(spans(tok, 32))
    wide = (tok, width)
    vmem = pltpu.VMEM
    dma = pltpu.SemaphoreType.DMA
    scratch = [
        vmem(wide, BF16),
        vmem((width, width), BF16),
        vmem((3 * head_width, width), BF16),
        vmem((head_width, width), BF16),
        vmem(wide, BF16),
        vmem(wide, BF16),
        vmem(wide, BF16),
        vmem(wide, F32),
        vmem(wide, BF16),
        vmem(wide, BF16),
        vmem((width, tok), BF16),
        vmem((3 * head_width, tok), F32),
        vmem((column, padded, tok), BF16),
        vmem((column, 2 * depth, tok), BF16),
        vmem((column, padded, tok), BF16),
        vmem((padded, span), BF16),
        vmem((padded, span), BF16),
        vmem((rows_x, 2 * depth, span), BF16),
        vmem((rows_x, span, padded), BF16),
        vmem((rows_x, span, padded), BF16),
        vmem((span, padded), BF16),
        vmem((span, padded), F32),
        vmem((rows_x, span, span), BF16),
        vmem((rows_x, span, 1), F32),
        vmem((rows_x, span, 1), F32),
        vmem((span, 1), F32),
        vmem((span, padded), F32),
        vmem((span, padded), F32),
        vmem((2 * padded, span), F32),
        vmem((padded, span), BF16),
        vmem((padded, span), BF16),
        vmem((rows_x - 1, 2 * depth, span), BF16),
        vmem((rows_x - 1, 2 * depth, span), BF16),
        vmem((2 * depth, span), BF16),
        vmem((column, padded, tok), BF16),
        vmem((column, padded, tok), BF16),
        vmem((column, 2 * depth, tok), BF16),
        vmem((3, tok, head_width), BF16),
        vmem((width, tok), F32),
        vmem(wide, F32),
        vmem(wide, BF16),
        vmem(wide, BF16),
        vmem(wide, BF16),
        dma((5,)),
        dma((2,)),
        dma((6, column)),
        dma((6, column)),
        dma((rows_x - 1, column)),
        dma((rows_x - 1, column)),
        dma((rows_x - 1,)),
        dma((rows_x - 1,)),
        dma((n_skip,)),
        dma((n_skip,)),
        dma((n_rows,)),
        dma((n_rows,)),
    ]
    out, glat = pl.pallas_call(
        functools.partial(kernel, rows_z, rows_x),
        out_shape=[jax.ShapeDtypeStruct(wide, BF16)] * 2,
        in_specs=[pl.BlockSpec(memory_space=pl.ANY)] * 5,
        out_specs=[pl.BlockSpec(memory_space=pl.ANY)] * 2,
        scratch_shapes=scratch,
        compiler_params=pltpu.CompilerParams(
            collective_id=0, has_side_effects=True, vmem_limit_bytes=56 * 2**20
        ),
    )(latents[0], skip_weight[0], project_in[0].T, project_out[0], upstream[0])
    out, glat = pl.pallas_call(
        settle,
        out_shape=[jax.ShapeDtypeStruct(wide, BF16)] * 2,
        in_specs=[pl.BlockSpec(memory_space=pl.ANY)] * 2,
        out_specs=[pl.BlockSpec(memory_space=pl.ANY)] * 2,
        scratch_shapes=[vmem((2,) + wide, BF16), dma((4,))],
        compiler_params=pltpu.CompilerParams(vmem_limit_bytes=56 * 2**20),
    )(out, glat)
    return out[None], glat[None]


def solution(mesh):
    rows_z = HEADS // CORES
    rows_x = mesh.shape["seq"] // HEADS
    return jax.shard_map(
        functools.partial(body, rows_z, rows_x),
        mesh=mesh,
        in_specs=(
            P("section", "seq", None),
            P("section", None, None),
            P("section", None, None),
            P("section", None, None),
            P("section", "seq", None),
        ),
        out_specs=(P("section", "seq", None), P("section", "seq", None)),
        check_vma=False,
    )
```

```python
import functools
import math

import jax
import jax.numpy as jnp
from jax import lax
from jax.experimental import pallas as pl
from jax.experimental.pallas import tpu as pltpu
from jax.sharding import PartitionSpec as P

HEADS = 8
EPSILON = 1e-06
CORES = 2
CHUNK = 128
PAD = 8

MESH = pl.DeviceIdType.MESH
F32 = jnp.float32
BF16 = jnp.bfloat16

GRAD, QUERY, OUT, DQ = range(4)


def dot(a, b):
    return jnp.dot(a, b, preferred_element_type=F32)


def spans(extent, width):
    return [(at, min(width, extent - at)) for at in range(0, extent, width)]


def stats(value):
    center = value - jnp.mean(value, -1, keepdims=True)
    rate = lax.rsqrt(jnp.mean(center * center, -1, keepdims=True) + EPSILON)
    return center * rate, rate


def norm_back(hat, rate, grad):
    inner = jnp.mean(grad * hat, -1, keepdims=True)
    return rate * (grad - jnp.mean(grad, -1, keepdims=True) - hat * inner)


def kernel(
    rows_z,
    rows_x,
    lat_hbm,
    skipw_hbm,
    win_hbm,
    wout_hbm,
    ups_hbm,
    out_hbm,
    glat_hbm,
    lat,
    skipw,
    win,
    wout,
    ups,
    skip_send,
    skip_recv,
    mixed,
    binput,
    normed,
    flip,
    projt,
    gsend,
    kvsend,
    qsend,
    gt,
    qt,
    kv,
    knat,
    vnat,
    qnat,
    gnat,
    exps,
    tops,
    facs,
    delta,
    oacc,
    qacc,
    kvacc,
    ot,
    dqt,
    kvin,
    keep,
    dkvgive,
    dkvtake,
    dkvpart,
    dkvrecv,
    dkvown,
    ofin,
    dqfin,
    dkvfin,
    gproj,
    gnt,
    ginput,
    gm_send,
    gm_recv,
    outv,
    load_sem,
    store_sem,
    col_send,
    col_recv,
    kv_send,
    kv_recv,
    kvx_send,
    kvx_recv,
    kvs_send,
    kvs_recv,
    place_sem,
    dkvs_send,
    dkvs_recv,
    dkv_send,
    dkv_recv,
    dkvx_send,
    dkvx_recv,
    skip_ssem,
    skip_rsem,
    gm_ssem,
    gm_rsem,
):
    sections = lax.axis_size("section")
    section = lax.axis_index("section")
    place = lax.axis_index("seq")
    zl = place // (rows_x * CORES)
    x = lax.rem(place // CORES, rows_x)
    core = lax.rem(place, CORES)
    is_upper = section >= sections // 2
    is_lower = jnp.logical_not(is_upper)
    column = rows_z * CORES
    part_size = column // 2
    me = zl * CORES + core
    even = lax.rem(x, 2)
    pair = x // 2
    own_head = 2 * zl + even
    query_x = 2 * pair + core

    tok, width = lat.shape
    head_width = wout.shape[0]
    depth = head_width // column
    padded = depth + PAD
    span = column * CHUNK
    scale = 1.0 / math.sqrt(depth)
    rate2 = scale * math.log2(math.e)
    q_tile = 256

    def device(z, at_x, at_core):
        return {
            "section": section,
            "seq": (z * rows_x + at_x) * CORES + at_core,
        }

    def owner(index, at_x):
        return device(index // CORES, at_x, lax.rem(index, CORES))

    def across(offset):
        there = (x, x + 1 - 2 * even, lax.rem(x + 2, rows_x), rows_x - 1 - x)[offset]
        return device(zl, there, core)

    sibling = device(zl, x, 1 - core)
    partner = {"section": sections - 1 - section, "seq": place}

    def remote(src, dst, send, recv, device):
        return pltpu.make_async_remote_copy(
            src_ref=src,
            dst_ref=dst,
            send_sem=send,
            recv_sem=recv,
            device_id=device,
            device_id_type=MESH,
        )

    def lanes(index):
        return pl.ds(pl.multiple_of(index * CHUNK, CHUNK), CHUNK)

    def head_copy(kind, head, src, dst):
        there = device(head // 2, 2 * pair + lax.rem(head, 2), even)
        return remote(
            src.at[head],
            dst.at[:, lanes(me)],
            col_send.at[kind, head],
            col_recv.at[kind, me],
            there,
        )

    def back_copy(kind, index, src, dst):
        return remote(
            src.at[:, lanes(index)],
            dst.at[own_head],
            col_send.at[kind, index],
            col_recv.at[kind, own_head],
            owner(index, query_x),
        )

    def head_start(kind, src, dst):
        @pl.loop(0, column)
        def _(step):
            head = lax.rem(own_head + step, column)
            mine = (step == 0) & (even == core)

            @pl.when(mine)
            def _():
                pltpu.make_async_copy(
                    src.at[head], dst.at[:, lanes(me)], col_recv.at[kind, me]
                ).start()

            @pl.when(jnp.logical_not(mine))
            def _():
                head_copy(kind, head, src, dst).start()

    def head_arrived(kind, src, dst):
        @pl.loop(0, column)
        def _(index):
            pltpu.make_async_copy(
                src.at[0], dst.at[:, lanes(index)], col_recv.at[kind, index]
            ).wait()

    def head_sent(kind, src, dst):
        @pl.loop(0, column)
        def _(step):
            head = lax.rem(own_head + step, column)

            @pl.when((step > 0) | (even != core))
            def _():
                head_copy(kind, head, src, dst).wait_send()

    def back_start(kind, src, dst):
        @pl.loop(0, column)
        def _(step):
            index = lax.rem(me + step, column)
            mine = (step == 0) & (even == core)

            @pl.when(mine)
            def _():
                pltpu.make_async_copy(
                    src.at[:, lanes(index)],
                    dst.at[own_head],
                    col_recv.at[kind, own_head],
                ).start()

            @pl.when(jnp.logical_not(mine))
            def _():
                back_copy(kind, index, src, dst).start()

    def back_arrived(kind, src, dst):
        @pl.loop(0, column)
        def _(head):
            pltpu.make_async_copy(
                src.at[:, lanes(0)], dst.at[head], col_recv.at[kind, head]
            ).wait()

    def back_sent(kind, src, dst):
        @pl.loop(0, column)
        def _(step):
            index = lax.rem(me + step, column)

            @pl.when((step > 0) | (even != core))
            def _():
                back_copy(kind, index, src, dst).wait_send()

    half_core = me // part_size
    half_at = lax.rem(me, part_size)
    kv_mine = half_core == core

    def kv_copy(step):
        z = lax.rem(zl + step, rows_z)
        return remote(
            kvsend.at[pl.ds(2 * z, 2)],
            kvin.at[:, :, lanes(half_at)],
            kv_send.at[step],
            kv_recv.at[half_at],
            device(z, x, half_core),
        )

    def kv_own():
        return pltpu.make_async_copy(
            kvsend.at[pl.ds(2 * zl, 2)],
            kvin.at[:, :, lanes(half_at)],
            kv_recv.at[half_at],
        )

    def kv_start():
        @pl.when(kv_mine)
        def _():
            kv_own().start()

        @pl.when(jnp.logical_not(kv_mine))
        def _():
            kv_copy(0).start()

        @pl.loop(1, rows_z)
        def _(step):
            kv_copy(step).start()

    def kv_arrived(at):
        pltpu.make_async_copy(
            kvsend.at[pl.ds(0, 2)], kvin.at[:, :, lanes(at)], kv_recv.at[at]
        ).wait()

    def kv_sent():
        @pl.when(jnp.logical_not(kv_mine))
        def _():
            kv_copy(0).wait_send()

        @pl.loop(1, rows_z)
        def _(step):
            kv_copy(step).wait_send()

    def half_lanes(at):
        return lanes(core * part_size + at)

    def kvx_copy(offset, at):
        head = even if offset == 2 else 1 - even
        return remote(
            kvin.at[head, :, lanes(at)],
            kv.at[offset, :, half_lanes(at)],
            kvx_send.at[offset - 1, at],
            kvx_recv.at[offset - 1, at],
            across(offset),
        )

    def kvs_copy(offset, at):
        there = kv.at[offset, :, half_lanes(at)]
        here = kvin.at[even, :, lanes(at)] if offset == 0 else there
        return remote(
            here, there, kvs_send.at[offset, at], kvs_recv.at[offset, at], sibling
        )

    def kv_place(at):
        return pltpu.make_async_copy(
            kvin.at[even, :, lanes(at)], kv.at[0, :, half_lanes(at)], place_sem.at[at]
        )

    def dkvs_copy(block):
        return remote(
            dkvgive.at[block],
            dkvtake.at[block],
            dkvs_send.at[block],
            dkvs_recv.at[block],
            sibling,
        )

    def dkvx_copy(offset):
        return remote(
            dkvpart.at[offset - 1],
            dkvrecv.at[offset - 1],
            dkvx_send.at[offset - 1],
            dkvx_recv.at[offset - 1],
            across(offset),
        )

    def dkv_copy(which, at):
        head = 2 * zl + (even if which == 0 else 1 - even)
        return remote(
            dkvown.at[which, :, lanes(at)],
            dkvfin.at[head],
            dkv_send.at[which, at],
            dkv_recv.at[head],
            owner(core * part_size + at, x),
        )

    def dkv_start(which):
        head = 2 * zl + (even if which == 0 else 1 - even)

        @pl.loop(0, part_size)
        def _(step):
            at = lax.rem(half_at + step, part_size)
            mine = (step == 0) & kv_mine

            @pl.when(mine)
            def _():
                pltpu.make_async_copy(
                    dkvown.at[which, :, lanes(at)], dkvfin.at[head], dkv_recv.at[head]
                ).start()

            @pl.when(jnp.logical_not(mine))
            def _():
                dkv_copy(which, at).start()

    def dkv_sent(which):
        @pl.loop(0, part_size)
        def _(step):
            at = lax.rem(half_at + step, part_size)

            @pl.when((step > 0) | jnp.logical_not(kv_mine))
            def _():
                dkv_copy(which, at).wait_send()

    def dkv_arrived():
        @pl.loop(0, column)
        def _(head):
            pltpu.make_async_copy(
                dkvown.at[0, :, lanes(0)], dkvfin.at[head], dkv_recv.at[head]
            ).wait()

    g_pair = (gsend, gt)
    q_pair = (qsend, qt)
    o_pair = (ot, ofin)
    dq_pair = (dqt, dqfin)

    skip_spans = spans(width, 512)
    pieces = [(lat_hbm, lat)]
    for at, size in skip_spans:
        cols = pl.ds(at, size)
        pieces.append((skipw_hbm.at[:, cols], skipw.at[:, cols]))
    pieces += [(ups_hbm, ups), (wout_hbm, wout), (win_hbm, win)]
    loads = [
        pltpu.make_async_copy(src, dst, load_sem.at[i])
        for i, (src, dst) in enumerate(pieces)
    ]
    lat_load, *skip_loads, ups_load, wout_load, win_load = loads
    for load in loads:
        load.start()

    barrier = pltpu.get_barrier_semaphore()
    peers = [owner(lax.rem(me + step, column), x) for step in range(1, column)]
    peers += [owner(index, x + 1 - 2 * even) for index in range(column)]
    peers += [across(offset) for offset in range(2, rows_x)]
    peers.append(partner)
    for peer in peers:
        pl.semaphore_signal(barrier, inc=1, device_id=peer, device_id_type=MESH)

    def skip_copy(i):
        at, size = skip_spans[i]
        cols = pl.ds(at, size)
        return remote(
            skip_send.at[:, cols],
            skip_recv.at[:, cols],
            skip_ssem.at[i],
            skip_rsem.at[i],
            partner,
        )

    lat_load.wait()
    for i, (at, size) in enumerate(skip_spans):
        skip_loads[i].wait()
        product = dot(lat[...], skipw[:, pl.ds(at, size)])
        mixed[:, pl.ds(at, size)] = product
        skip_send[:, pl.ds(at, size)] = product.astype(BF16)
        if i == 0:
            pl.semaphore_wait(barrier, len(peers))

        @pl.when(is_lower)
        def _():
            skip_copy(i).start()

    def turn(source, i):
        block = source[:, pl.ds(i * CHUNK, CHUNK)]
        flip[pl.ds(i * CHUNK, CHUNK), :] = block.astype(F32).T.astype(BF16)

    ups_load.wait()
    for i in range(width // CHUNK):
        turn(ups, i)
    wout_load.wait()
    blank = jnp.zeros((PAD, CHUNK), F32)

    @pl.loop(0, column // 2)
    def _(i):
        rows = pl.ds(pl.multiple_of(i * 2 * depth, 16), 2 * depth)
        two = dot(wout[rows, :], flip[...])
        gsend[2 * i] = jnp.concatenate([blank, two[:depth]], 0).astype(BF16)
        gsend[2 * i + 1] = jnp.concatenate([blank, two[depth:]], 0).astype(BF16)

    head_start(GRAD, *g_pair)

    row_spans = spans(tok, 32)

    @pl.when(is_upper)
    def _():
        for i in range(len(skip_spans)):
            skip_copy(i).wait_recv()
        for at, size in row_spans:
            rows = pl.ds(at, size)
            total = mixed[rows, :] + skip_recv[rows, :].astype(F32)
            mixed[rows, :] = total
            binput[rows, :] = stats(total)[0].astype(BF16)

    @pl.when(is_lower)
    def _():
        binput[...] = lat[...]

    for at, size in row_spans:
        rows = pl.ds(at, size)
        normed[rows, :] = stats(binput[rows, :].astype(F32))[0].astype(BF16)

    for i in range(width // CHUNK):
        turn(normed, i)
    win_load.wait()

    def project(part):
        rows = pl.ds(pl.multiple_of(part * head_width, 16), head_width)
        projt[rows, :] = dot(win[rows, :], flip[...])

    @pl.loop(1, 3)
    def _(part):
        project(part)

    for head in range(column):
        keys = projt[pl.ds(head_width + head * depth, depth), :]
        values = projt[pl.ds(2 * head_width + head * depth, depth), :]
        kvsend[head] = jnp.concatenate([keys, values], 0).astype(BF16)
    kv_start()
    project(0)
    for head in range(column):
        queries = projt[pl.ds(head * depth, depth), :]
        qsend[head] = jnp.concatenate([queries, blank], 0).astype(BF16)
    head_start(QUERY, *q_pair)

    @pl.loop(0, part_size)
    def _(at):
        kv_arrived(at)
        for offset in range(1, rows_x):
            kvx_copy(offset, at).start()
        kvs_copy(0, at).start()
        kv_place(at).start()

    @pl.loop(0, part_size)
    def _(at):
        for offset in range(1, rows_x):
            kvx_copy(offset, at).wait_recv()
            kvs_copy(offset, at).start()

    def natural(block):
        lane = lax.broadcasted_iota(jnp.int32, (q_tile, padded), 1)
        for at, size in spans(span, q_tile):
            cols = pl.ds(at, size)
            keys = kv[block, :padded, cols].astype(F32).T
            values = kv[block, depth - PAD :, cols].astype(F32).T
            knat[block, cols, :] = keys.astype(BF16)
            vnat[block, cols, :] = jnp.where(lane < PAD, 1.0, values).astype(BF16)

    head_arrived(GRAD, *g_pair)
    head_arrived(QUERY, *q_pair)
    for at, size in spans(span, q_tile):
        rows = pl.ds(at, size)
        qnat[rows, :] = qt[:, rows].astype(F32).T.astype(BF16)
        gnat[rows, :] = gt[:, rows].astype(F32).T

    order = [0, 1, 3, 2]

    def forward(block, is_first):
        natural(block)

        @pl.loop(0, span // q_tile)
        def _(i):
            rows = pl.ds(pl.multiple_of(i * q_tile, q_tile), q_tile)
            scores = dot(qnat[rows, :], kv[block, :padded, :])
            top = jnp.max(scores, -1, keepdims=True)
            if not is_first:
                before = tops[order[order.index(block) - 1], rows, :]
                top = jnp.maximum(top, before)
            tops[block, rows, :] = top
            lifted = jnp.exp2((scores - top) * rate2).astype(BF16)
            exps[block, rows, :] = lifted
            term = dot(lifted, vnat[block])
            if not is_first:
                term += oacc[rows, :] * jnp.exp2((before - top) * rate2)
            oacc[rows, :] = term

    for n, block in enumerate(order):

        @pl.loop(0, part_size)
        def _(at):
            kvs_copy(block, at).wait_recv()
            if block == 0:
                kv_place(at).wait()

        forward(block, n == 0)

    for at, size in spans(span, q_tile):
        rows = pl.ds(at, size)
        total = oacc[rows, :]
        inverse = 1.0 / total[:, :1]
        mixed_values = (total * inverse).astype(BF16).astype(F32)
        ot[:, rows] = mixed_values.T.astype(BF16)
        delta[rows, :] = jnp.sum(gnat[rows, :] * mixed_values, -1, keepdims=True)
        last = tops[order[-1], rows, :]
        for block in range(rows_x):
            lift = jnp.exp2((tops[block, rows, :] - last) * rate2)
            facs[block, rows, :] = lift * inverse
        qacc[rows, :] = jnp.zeros((size, padded), F32)
    back_start(OUT, *o_pair)

    def backward_rows(block, i):
        rows = pl.ds(i * q_tile, q_tile)
        factor = facs[block, rows, :]
        grads = gnat[rows, :] * factor
        shift = delta[rows, :] * factor
        lifted = exps[block, rows, :]
        back = dot(grads.astype(BF16), kv[block, depth - PAD :, :]) - shift
        gscore = (lifted.astype(F32) * back).astype(BF16)
        qacc[rows, :] += dot(gscore, knat[block])
        keys = dot(qt[:, rows], gscore)
        values = dot(grads.T.astype(BF16), lifted)
        if i > 0:
            keys += kvacc[:padded, :]
            values += kvacc[padded:, :]
        kvacc[:padded, :] = keys
        kvacc[padded:, :] = values

    half_span = span // 2

    def joined(which):
        cols = pl.ds(pl.multiple_of(which * half_span, CHUNK), half_span)
        keys = kvacc[:padded, cols] * scale
        values = kvacc[padded:, cols]
        middle = keys[depth - PAD :] + values[: 2 * PAD]
        return jnp.concatenate([keys[: depth - PAD], middle, values[2 * PAD :]], 0)

    def pass_on(block):
        dkvs_copy(block).wait_recv()
        total = keep[block] + dkvtake[block].astype(F32)
        dkvpart[block - 1] = total.astype(BF16)
        dkvx_copy(block).start()

    turns = [2, 1, 3, 0]
    for n, block in enumerate(turns):
        for i in range(span // q_tile):
            backward_rows(block, i)
            if n > 0 and i == (span // q_tile - 1) // 2:
                pass_on(turns[n - 1])
        dkvgive[block] = joined(1 - core).astype(BF16)
        dkvs_copy(block).start()
        keep[block] = joined(core)

    for offset in (1, 3):
        dkvx_copy(offset).wait_recv()
    dkvown[1] = (dkvrecv[0].astype(F32) + dkvrecv[2].astype(F32)).astype(BF16)
    dkv_start(1)
    dkvs_copy(0).wait_recv()
    dkvx_copy(2).wait_recv()
    total = keep[0] + dkvtake[0].astype(F32) + dkvrecv[1].astype(F32)
    dkvown[0] = total.astype(BF16)
    dkv_start(0)
    for at, size in spans(span, q_tile):
        rows = pl.ds(at, size)
        dqt[:, rows] = (qacc[rows, :] * scale).T.astype(BF16)
    back_start(DQ, *dq_pair)

    back_arrived(OUT, *o_pair)
    for head in range(column):
        rows = pl.ds(head * depth, depth)
        projt[rows, :] = ofin[head].astype(F32)[PAD:]
    attended = projt[:head_width, :].T.astype(BF16)
    for at, size in spans(width, 512):
        cols = pl.ds(at, size)
        term = dot(attended, wout[:, cols])
        outv[:, cols] = (binput[:, cols].astype(F32) + term).astype(BF16)
    out_store = pltpu.make_async_copy(outv, out_hbm, store_sem.at[0])
    out_store.start()

    dkv_arrived()
    for head in range(column):
        both = dkvfin[head].astype(F32)
        projt[pl.ds(head_width + head * depth, depth), :] = both[:depth]
        projt[pl.ds(2 * head_width + head * depth, depth), :] = both[depth:]
    back_arrived(DQ, *dq_pair)
    for head in range(column):
        projt[pl.ds(head * depth, depth), :] = dqfin[head].astype(F32)[:depth]
    for part in range(3):
        gproj[part] = projt[pl.ds(part * head_width, head_width), :].T.astype(BF16)
    for at, size in spans(width, 512):
        cols = pl.ds(at, size)
        ginput[:, cols] = sum(
            dot(gproj[part], win[pl.ds(part * head_width, head_width), cols])
            for part in range(3)
        )

    def gm_copy(i):
        rows = pl.ds(*row_spans[i])
        return remote(
            gm_send.at[rows], gm_recv.at[rows], gm_ssem.at[i], gm_rsem.at[i], partner
        )

    for i, (at, size) in enumerate(row_spans):
        rows = pl.ds(at, size)
        hat, rate = stats(binput[rows, :].astype(F32))
        grad = ups[rows, :].astype(F32) + norm_back(hat, rate, ginput[rows, :])
        ginput[rows, :] = grad

        @pl.when(is_upper)
        def _():
            hat, rate = stats(mixed[rows, :])
            gm_send[rows, :] = norm_back(hat, rate, ginput[rows, :]).astype(BF16)
            gm_copy(i).start()

    @pl.when(is_upper)
    def _():
        ginput[...] = jnp.zeros_like(ginput)
        for i in range(width // CHUNK):
            turn(gm_send, i)

    @pl.when(is_lower)
    def _():
        for i in range(len(row_spans)):
            gm_copy(i).wait_recv()
        for i in range(width // CHUNK):
            turn(gm_recv, i)

    half = width // 2

    @pl.loop(0, 2)
    def _(i):
        rows = pl.ds(pl.multiple_of(i * half, 16), half)
        gnt[rows, :] = dot(skipw[rows, :], flip[...])

    out_store.wait()
    for i in range(width // CHUNK):
        cols = pl.ds(i * CHUNK, CHUNK)
        term = ginput[:, cols] + gnt[pl.ds(i * CHUNK, CHUNK), :].T
        outv[:, cols] = term.astype(BF16)
    glat_store = pltpu.make_async_copy(outv, glat_hbm, store_sem.at[1])
    glat_store.start()

    head_sent(GRAD, *g_pair)
    head_sent(QUERY, *q_pair)
    back_sent(OUT, *o_pair)
    back_sent(DQ, *dq_pair)
    kv_sent()
    dkv_sent(0)
    dkv_sent(1)

    @pl.loop(0, part_size)
    def _(at):
        kvs_copy(0, at).wait_send()
        for offset in range(1, rows_x):
            kvx_copy(offset, at).wait_send()
            kvs_copy(offset, at).wait_send()

    dkvs_copy(0).wait_send()
    for offset in range(1, rows_x):
        dkvx_copy(offset).wait_send()
        dkvs_copy(offset).wait_send()

    @pl.when(is_lower)
    def _():
        for i in range(len(skip_spans)):
            skip_copy(i).wait_send()

    @pl.when(is_upper)
    def _():
        for i in range(len(row_spans)):
            gm_copy(i).wait_send()

    glat_store.wait()


def settle(out, glat, out_hbm, glat_hbm, held, sem):
    ins = [
        pltpu.make_async_copy(out, held.at[0], sem.at[0]),
        pltpu.make_async_copy(glat, held.at[1], sem.at[1]),
    ]
    outs = [
        pltpu.make_async_copy(held.at[0], out_hbm, sem.at[2]),
        pltpu.make_async_copy(held.at[1], glat_hbm, sem.at[3]),
    ]
    for copy in ins:
        copy.start()
    for copy, onward in zip(ins, outs):
        copy.wait()
        onward.start()
    for copy in outs:
        copy.wait()


def body(rows_z, rows_x, latents, skip_weight, project_in, project_out, upstream):
    tok, width = latents.shape[1:]
    head_width = project_out.shape[1]
    column = rows_z * CORES
    depth = head_width // column
    padded = depth + PAD
    span = column * tok
    part = span // 2
    n_skip = len(spans(width, 512))
    n_rows = len(spans(tok, 32))
    wide = (tok, width)
    vmem = pltpu.VMEM
    dma = pltpu.SemaphoreType.DMA
    scratch = [
        vmem(wide, BF16),
        vmem((width, width), BF16),
        vmem((3 * head_width, width), BF16),
        vmem((head_width, width), BF16),
        vmem(wide, BF16),
        vmem(wide, BF16),
        vmem(wide, BF16),
        vmem(wide, F32),
        vmem(wide, BF16),
        vmem(wide, BF16),
        vmem((width, tok), BF16),
        vmem((3 * head_width, tok), F32),
        vmem((column, padded, tok), BF16),
        vmem((column, 2 * depth, tok), BF16),
        vmem((column, padded, tok), BF16),
        vmem((padded, span), BF16),
        vmem((padded, span), BF16),
        vmem((rows_x, 2 * depth, span), BF16),
        vmem((rows_x, span, padded), BF16),
        vmem((rows_x, span, padded), BF16),
        vmem((span, padded), BF16),
        vmem((span, padded), F32),
        vmem((rows_x, span, span), BF16),
        vmem((rows_x, span, 1), F32),
        vmem((rows_x, span, 1), F32),
        vmem((span, 1), F32),
        vmem((span, padded), F32),
        vmem((span, padded), F32),
        vmem((2 * padded, span), F32),
        vmem((padded, span), BF16),
        vmem((padded, span), BF16),
        vmem((2, 2 * depth, part), BF16),
        vmem((rows_x, 2 * depth, part), F32),
        vmem((rows_x, 2 * depth, part), BF16),
        vmem((rows_x, 2 * depth, part), BF16),
        vmem((rows_x - 1, 2 * depth, part), BF16),
        vmem((rows_x - 1, 2 * depth, part), BF16),
        vmem((2, 2 * depth, part), BF16),
        vmem((column, padded, tok), BF16),
        vmem((column, padded, tok), BF16),
        vmem((column, 2 * depth, tok), BF16),
        vmem((3, tok, head_width), BF16),
        vmem((width, tok), F32),
        vmem(wide, F32),
        vmem(wide, BF16),
        vmem(wide, BF16),
        vmem(wide, BF16),
        dma((4 + n_skip,)),
        dma((2,)),
        dma((4, column)),
        dma((4, column)),
        dma((rows_z,)),
        dma((column // 2,)),
        dma((rows_x - 1, column // 2)),
        dma((rows_x - 1, column // 2)),
        dma((rows_x, column // 2)),
        dma((rows_x, column // 2)),
        dma((column // 2,)),
        dma((rows_x,)),
        dma((rows_x,)),
        dma((2, column // 2)),
        dma((column,)),
        dma((rows_x - 1,)),
        dma((rows_x - 1,)),
        dma((n_skip,)),
        dma((n_skip,)),
        dma((n_rows,)),
        dma((n_rows,)),
    ]
    out, glat = pl.pallas_call(
        functools.partial(kernel, rows_z, rows_x),
        out_shape=[jax.ShapeDtypeStruct(wide, BF16)] * 2,
        in_specs=[pl.BlockSpec(memory_space=pl.ANY)] * 5,
        out_specs=[pl.BlockSpec(memory_space=pl.ANY)] * 2,
        scratch_shapes=scratch,
        compiler_params=pltpu.CompilerParams(
            collective_id=0, has_side_effects=True, vmem_limit_bytes=56 * 2**20
        ),
    )(latents[0], skip_weight[0], project_in[0].T, project_out[0], upstream[0])
    out, glat = pl.pallas_call(
        settle,
        out_shape=[jax.ShapeDtypeStruct(wide, BF16)] * 2,
        in_specs=[pl.BlockSpec(memory_space=pl.ANY)] * 2,
        out_specs=[pl.BlockSpec(memory_space=pl.ANY)] * 2,
        scratch_shapes=[vmem((2,) + wide, BF16), dma((4,))],
        compiler_params=pltpu.CompilerParams(vmem_limit_bytes=56 * 2**20),
    )(out, glat)
    return out[None], glat[None]


def solution(mesh):
    rows_z = HEADS // CORES
    rows_x = mesh.shape["seq"] // HEADS
    return jax.shard_map(
        functools.partial(body, rows_z, rows_x),
        mesh=mesh,
        in_specs=(
            P("section", "seq", None),
            P("section", None, None),
            P("section", None, None),
            P("section", None, None),
            P("section", "seq", None),
        ),
        out_specs=(P("section", "seq", None), P("section", "seq", None)),
        check_vma=False,
    )
```

```python
import functools
import math

import jax
import jax.numpy as jnp
from jax import lax
from jax.experimental import pallas as pl
from jax.experimental.pallas import tpu as pltpu
from jax.sharding import PartitionSpec as P

HEADS = 8
EPSILON = 1e-06
CORES = 2
CHUNK = 128
PAD = 8

MESH = pl.DeviceIdType.MESH
F32 = jnp.float32
BF16 = jnp.bfloat16

GRAD, QUERY, OUT, DQ = range(4)


def dot(a, b):
    return jnp.dot(a, b, preferred_element_type=F32)


def spans(extent, width):
    return [(at, min(width, extent - at)) for at in range(0, extent, width)]


def stats(value):
    center = value - jnp.mean(value, -1, keepdims=True)
    rate = lax.rsqrt(jnp.mean(center * center, -1, keepdims=True) + EPSILON)
    return center * rate, rate


def norm_back(hat, rate, grad):
    inner = jnp.mean(grad * hat, -1, keepdims=True)
    return rate * (grad - jnp.mean(grad, -1, keepdims=True) - hat * inner)


def kernel(
    rows_h,
    rows_k,
    lat_hbm,
    skipw_hbm,
    win_hbm,
    wout_hbm,
    ups_hbm,
    out_hbm,
    glat_hbm,
    lat,
    skipw,
    win,
    wout,
    ups,
    skip_send,
    skip_recv,
    mixed,
    binput,
    normed,
    flip,
    projt,
    gsend,
    kvsend,
    qsend,
    gt,
    qt,
    kv,
    knat,
    vnat,
    qnat,
    gnat,
    exps,
    tops,
    facs,
    delta,
    oacc,
    qacc,
    kvacc,
    ot,
    dqt,
    kvin,
    keep,
    dkvgive,
    dkvtake,
    dkvpart,
    dkvrecv,
    dkvown,
    ofin,
    dqfin,
    dkvfin,
    gproj,
    gnt,
    ginput,
    gm_send,
    gm_recv,
    outv,
    load_sem,
    store_sem,
    col_send,
    col_recv,
    kv_send,
    kv_recv,
    kvx_send,
    kvx_recv,
    kvs_send,
    kvs_recv,
    place_sem,
    dkvs_send,
    dkvs_recv,
    dkv_send,
    dkv_recv,
    dkvx_send,
    dkvx_recv,
    skip_ssem,
    skip_rsem,
    gm_ssem,
    gm_rsem,
):
    sections = lax.axis_size("section")
    section = lax.axis_index("section")
    place = lax.axis_index("seq")
    line = place // (rows_h * CORES)
    row = lax.rem(place // CORES, rows_h)
    core = lax.rem(place, CORES)
    is_upper = section >= sections // 2
    is_lower = jnp.logical_not(is_upper)
    column = rows_h * CORES
    part_size = column // 2
    me = row * CORES + core
    even = lax.rem(line, 2)
    pair = line // 2
    own_head = 2 * row + even
    query_line = 2 * pair + core

    tok, width = lat.shape
    head_width = wout.shape[0]
    depth = head_width // column
    padded = depth + PAD
    span = column * CHUNK
    scale = 1.0 / math.sqrt(depth)
    rate2 = scale * math.log2(math.e)
    q_tile = 256

    def device(at_row, at_line, at_core):
        return {
            "section": section,
            "seq": (at_line * rows_h + at_row) * CORES + at_core,
        }

    def owner(index, at_line):
        return device(index // CORES, at_line, lax.rem(index, CORES))

    def across(offset):
        there = (line, line + 1 - 2 * even, lax.rem(line + 2, rows_k), rows_k - 1 - line)[offset]
        return device(row, there, core)

    sibling = device(row, line, 1 - core)
    partner = {"section": sections - 1 - section, "seq": place}

    def remote(src, dst, send, recv, device):
        return pltpu.make_async_remote_copy(
            src_ref=src,
            dst_ref=dst,
            send_sem=send,
            recv_sem=recv,
            device_id=device,
            device_id_type=MESH,
        )

    def lanes(index):
        return pl.ds(pl.multiple_of(index * CHUNK, CHUNK), CHUNK)

    def head_copy(kind, head, src, dst):
        there = device(head // 2, 2 * pair + lax.rem(head, 2), even)
        return remote(
            src.at[head],
            dst.at[:, lanes(me)],
            col_send.at[kind, head],
            col_recv.at[kind, me],
            there,
        )

    def back_copy(kind, index, src, dst):
        return remote(
            src.at[:, lanes(index)],
            dst.at[own_head],
            col_send.at[kind, index],
            col_recv.at[kind, own_head],
            owner(index, query_line),
        )

    def head_start(kind, src, dst):
        @pl.loop(0, column)
        def _(step):
            head = lax.rem(own_head + step, column)
            mine = (step == 0) & (even == core)

            @pl.when(mine)
            def _():
                pltpu.make_async_copy(
                    src.at[head], dst.at[:, lanes(me)], col_recv.at[kind, me]
                ).start()

            @pl.when(jnp.logical_not(mine))
            def _():
                head_copy(kind, head, src, dst).start()

    def head_arrived(kind, src, dst):
        @pl.loop(0, column)
        def _(index):
            pltpu.make_async_copy(
                src.at[0], dst.at[:, lanes(index)], col_recv.at[kind, index]
            ).wait()

    def head_sent(kind, src, dst):
        @pl.loop(0, column)
        def _(step):
            head = lax.rem(own_head + step, column)

            @pl.when((step > 0) | (even != core))
            def _():
                head_copy(kind, head, src, dst).wait_send()

    def back_one(kind, index, src, dst):
        mine = (index == me) & (even == core)

        @pl.when(mine)
        def _():
            pltpu.make_async_copy(
                src.at[:, lanes(index)], dst.at[own_head], col_recv.at[kind, own_head]
            ).start()

        @pl.when(jnp.logical_not(mine))
        def _():
            back_copy(kind, index, src, dst).start()

    def back_start(kind, src, dst):
        @pl.loop(0, column)
        def _(index):
            back_one(kind, index, src, dst)

    def back_arrived(kind, src, dst):
        @pl.loop(0, column)
        def _(head):
            pltpu.make_async_copy(
                src.at[:, lanes(0)], dst.at[head], col_recv.at[kind, head]
            ).wait()

    def back_sent(kind, src, dst):
        @pl.loop(0, column)
        def _(step):
            index = lax.rem(me + step, column)

            @pl.when((step > 0) | (even != core))
            def _():
                back_copy(kind, index, src, dst).wait_send()

    half_core = me // part_size
    half_at = lax.rem(me, part_size)
    kv_mine = half_core == core

    def kv_copy(step):
        at_row = lax.rem(row + step, rows_h)
        return remote(
            kvsend.at[pl.ds(2 * at_row, 2)],
            kvin.at[:, :, lanes(half_at)],
            kv_send.at[step],
            kv_recv.at[half_at],
            device(at_row, line, half_core),
        )

    def kv_own():
        return pltpu.make_async_copy(
            kvsend.at[pl.ds(2 * row, 2)],
            kvin.at[:, :, lanes(half_at)],
            kv_recv.at[half_at],
        )

    def kv_start():
        @pl.when(kv_mine)
        def _():
            kv_own().start()

        @pl.when(jnp.logical_not(kv_mine))
        def _():
            kv_copy(0).start()

        @pl.loop(1, rows_h)
        def _(step):
            kv_copy(step).start()

    def kv_arrived(at):
        pltpu.make_async_copy(
            kvsend.at[pl.ds(0, 2)], kvin.at[:, :, lanes(at)], kv_recv.at[at]
        ).wait()

    def kv_sent():
        @pl.when(jnp.logical_not(kv_mine))
        def _():
            kv_copy(0).wait_send()

        @pl.loop(1, rows_h)
        def _(step):
            kv_copy(step).wait_send()

    def half_lanes(at):
        return lanes(core * part_size + at)

    def kvx_copy(offset, at):
        head = even if offset == 2 else 1 - even
        return remote(
            kvin.at[head, :, lanes(at)],
            kv.at[offset, :, half_lanes(at)],
            kvx_send.at[offset - 1, at],
            kvx_recv.at[offset - 1, at],
            across(offset),
        )

    def kvs_copy(offset, at):
        there = kv.at[offset, :, half_lanes(at)]
        here = kvin.at[even, :, lanes(at)] if offset == 0 else there
        return remote(
            here, there, kvs_send.at[offset, at], kvs_recv.at[offset, at], sibling
        )

    def kv_place(at):
        return pltpu.make_async_copy(
            kvin.at[even, :, lanes(at)], kv.at[0, :, half_lanes(at)], place_sem.at[at]
        )

    def dkvs_copy(block):
        return remote(
            dkvgive.at[block],
            dkvtake.at[block],
            dkvs_send.at[block],
            dkvs_recv.at[block],
            sibling,
        )

    def dkvx_copy(offset):
        return remote(
            dkvpart.at[offset - 1],
            dkvrecv.at[offset - 1],
            dkvx_send.at[offset - 1],
            dkvx_recv.at[offset - 1],
            across(offset),
        )

    def dkv_copy(which, at):
        head = 2 * row + (even if which == 0 else 1 - even)
        return remote(
            dkvown.at[which, :, lanes(at)],
            dkvfin.at[head],
            dkv_send.at[which, at],
            dkv_recv.at[head],
            owner(core * part_size + at, line),
        )

    def dkv_start(which):
        head = 2 * row + (even if which == 0 else 1 - even)

        @pl.loop(0, part_size)
        def _(step):
            at = lax.rem(half_at + step, part_size)
            mine = (step == 0) & kv_mine

            @pl.when(mine)
            def _():
                pltpu.make_async_copy(
                    dkvown.at[which, :, lanes(at)], dkvfin.at[head], dkv_recv.at[head]
                ).start()

            @pl.when(jnp.logical_not(mine))
            def _():
                dkv_copy(which, at).start()

    def dkv_sent(which):
        @pl.loop(0, part_size)
        def _(step):
            at = lax.rem(half_at + step, part_size)

            @pl.when((step > 0) | jnp.logical_not(kv_mine))
            def _():
                dkv_copy(which, at).wait_send()

    def dkv_arrived():
        @pl.loop(0, column)
        def _(head):
            pltpu.make_async_copy(
                dkvown.at[0, :, lanes(0)], dkvfin.at[head], dkv_recv.at[head]
            ).wait()

    g_pair = (gsend, gt)
    q_pair = (qsend, qt)
    o_pair = (ot, ofin)
    dq_pair = (dqt, dqfin)

    skip_spans = spans(width, 512)
    pieces = [(lat_hbm, lat)]
    for at, size in skip_spans:
        cols = pl.ds(at, size)
        pieces.append((skipw_hbm.at[:, cols], skipw.at[:, cols]))
    pieces += [(ups_hbm, ups), (wout_hbm, wout), (win_hbm, win)]
    loads = [
        pltpu.make_async_copy(src, dst, load_sem.at[i])
        for i, (src, dst) in enumerate(pieces)
    ]
    lat_load, *skip_loads, ups_load, wout_load, win_load = loads
    for load in loads:
        load.start()

    barrier = pltpu.get_barrier_semaphore()
    peers = [owner(lax.rem(me + step, column), line) for step in range(1, column)]
    peers += [owner(index, line + 1 - 2 * even) for index in range(column)]
    peers += [across(offset) for offset in range(2, rows_k)]
    peers.append(partner)
    for peer in peers:
        pl.semaphore_signal(barrier, inc=1, device_id=peer, device_id_type=MESH)

    def skip_copy(i):
        at, size = skip_spans[i]
        cols = pl.ds(at, size)
        return remote(
            skip_send.at[:, cols],
            skip_recv.at[:, cols],
            skip_ssem.at[i],
            skip_rsem.at[i],
            partner,
        )

    lat_load.wait()
    for i, (at, size) in enumerate(skip_spans):
        skip_loads[i].wait()
        product = dot(lat[...], skipw[:, pl.ds(at, size)])
        mixed[:, pl.ds(at, size)] = product
        skip_send[:, pl.ds(at, size)] = product.astype(BF16)
        if i == 0:
            pl.semaphore_wait(barrier, len(peers))

        @pl.when(is_lower)
        def _():
            skip_copy(i).start()

    def turn(source, i):
        block = source[:, pl.ds(i * CHUNK, CHUNK)]
        flip[pl.ds(i * CHUNK, CHUNK), :] = block.astype(F32).T.astype(BF16)

    ups_load.wait()
    for i in range(width // CHUNK):
        turn(ups, i)
    wout_load.wait()
    blank = jnp.zeros((PAD, CHUNK), F32)

    @pl.loop(0, column // 2)
    def _(i):
        rows = pl.ds(pl.multiple_of(i * 2 * depth, 16), 2 * depth)
        two = dot(wout[rows, :], flip[...])
        gsend[2 * i] = jnp.concatenate([blank, two[:depth]], 0).astype(BF16)
        gsend[2 * i + 1] = jnp.concatenate([blank, two[depth:]], 0).astype(BF16)

    head_start(GRAD, *g_pair)

    row_spans = spans(tok, 32)

    @pl.when(is_upper)
    def _():
        for i in range(len(skip_spans)):
            skip_copy(i).wait_recv()
        for at, size in row_spans:
            rows = pl.ds(at, size)
            total = mixed[rows, :] + skip_recv[rows, :].astype(F32)
            mixed[rows, :] = total
            binput[rows, :] = stats(total)[0].astype(BF16)

    @pl.when(is_lower)
    def _():
        binput[...] = lat[...]

    for at, size in row_spans:
        rows = pl.ds(at, size)
        normed[rows, :] = stats(binput[rows, :].astype(F32))[0].astype(BF16)

    for i in range(width // CHUNK):
        turn(normed, i)
    win_load.wait()

    def project(part):
        rows = pl.ds(pl.multiple_of(part * head_width, 16), head_width)
        projt[rows, :] = dot(win[rows, :], flip[...])

    @pl.loop(1, 3)
    def _(part):
        project(part)

    for head in range(column):
        keys = projt[pl.ds(head_width + head * depth, depth), :]
        values = projt[pl.ds(2 * head_width + head * depth, depth), :]
        kvsend[head] = jnp.concatenate([keys, values], 0).astype(BF16)
    kv_start()
    project(0)
    for head in range(column):
        queries = projt[pl.ds(head * depth, depth), :]
        qsend[head] = jnp.concatenate([queries, blank], 0).astype(BF16)
    head_start(QUERY, *q_pair)

    @pl.loop(0, part_size)
    def _(at):
        kv_arrived(at)
        kvs_copy(0, at).start()
        kv_place(at).start()

    for offset in range(1, rows_k):

        @pl.loop(0, part_size)
        def _(at):
            kvx_copy(offset, at).start()

    def take(block):
        @pl.loop(0, part_size)
        def _(at):
            kvx_copy(block, at).wait_recv()
            kvs_copy(block, at).start()

    def natural(block):
        lane = lax.broadcasted_iota(jnp.int32, (q_tile, padded), 1)
        for at, size in spans(span, q_tile):
            cols = pl.ds(at, size)
            keys = kv[block, :padded, cols].astype(F32).T
            values = kv[block, depth - PAD :, cols].astype(F32).T
            knat[block, cols, :] = keys.astype(BF16)
            vnat[block, cols, :] = jnp.where(lane < PAD, 1.0, values).astype(BF16)

    head_arrived(GRAD, *g_pair)
    head_arrived(QUERY, *q_pair)
    for at, size in spans(span, q_tile):
        rows = pl.ds(at, size)
        qnat[rows, :] = qt[:, rows].astype(F32).T.astype(BF16)
        gnat[rows, :] = gt[:, rows].astype(F32).T

    order = [0, 1, 2, 3]
    tiles = span // q_tile
    middle_tile = (tiles - 1) // 2

    def forward_rows(block, i):
        rows = pl.ds(i * q_tile, q_tile)
        scores = dot(qnat[rows, :], kv[block, :padded, :])
        top = jnp.max(scores, -1, keepdims=True)
        if block > 0:
            before = tops[block - 1, rows, :]
            top = jnp.maximum(top, before)
        tops[block, rows, :] = top
        lifted = jnp.exp2((scores - top) * rate2).astype(BF16)
        exps[block, rows, :] = lifted
        term = dot(lifted, vnat[block])
        if block > 0:
            term += oacc[rows, :] * jnp.exp2((before - top) * rate2)
        oacc[rows, :] = term

    for block in order:

        @pl.loop(0, part_size)
        def _(at):
            kvs_copy(block, at).wait_recv()
            if block == 0:
                kv_place(at).wait()

        natural(block)
        for i in range(tiles):
            forward_rows(block, i)
            if i == middle_tile and block + 1 < rows_k:
                take(block + 1)

    for at, size in spans(span, q_tile):
        rows = pl.ds(at, size)
        total = oacc[rows, :]
        inverse = 1.0 / total[:, :1]
        mixed_values = (total * inverse).astype(BF16).astype(F32)
        ot[:, rows] = mixed_values.T.astype(BF16)
        delta[rows, :] = jnp.sum(gnat[rows, :] * mixed_values, -1, keepdims=True)
        last = tops[order[-1], rows, :]
        for block in range(rows_k):
            lift = jnp.exp2((tops[block, rows, :] - last) * rate2)
            facs[block, rows, :] = lift * inverse
        qacc[rows, :] = jnp.zeros((size, padded), F32)
    back_start(OUT, *o_pair)

    def backward_rows(block, i):
        rows = pl.ds(i * q_tile, q_tile)
        factor = facs[block, rows, :]
        grads = gnat[rows, :] * factor
        shift = delta[rows, :] * factor
        lifted = exps[block, rows, :]
        back = dot(grads.astype(BF16), kv[block, depth - PAD :, :]) - shift
        gscore = (lifted.astype(F32) * back).astype(BF16)
        qacc[rows, :] += dot(gscore, knat[block])
        keys = dot(qt[:, rows], gscore)
        values = dot(grads.T.astype(BF16), lifted)
        if i > 0:
            keys += kvacc[:padded, :]
            values += kvacc[padded:, :]
        kvacc[:padded, :] = keys
        kvacc[padded:, :] = values

    half_span = span // 2

    def joined(which):
        cols = pl.ds(pl.multiple_of(which * half_span, CHUNK), half_span)
        keys = kvacc[:padded, cols] * scale
        values = kvacc[padded:, cols]
        middle = keys[depth - PAD :] + values[: 2 * PAD]
        return jnp.concatenate([keys[: depth - PAD], middle, values[2 * PAD :]], 0)

    def pass_on(block):
        dkvs_copy(block).wait_recv()
        total = keep[block] + dkvtake[block].astype(F32)
        dkvpart[block - 1] = total.astype(BF16)
        dkvx_copy(block).start()

    turns = [2, 3, 1, 0]
    for n, block in enumerate(turns):
        for i in range(tiles):
            backward_rows(block, i)
            if n > 0 and i == middle_tile:
                pass_on(turns[n - 1])
            if block == 0:
                rows = pl.ds(i * q_tile, q_tile)
                dqt[:, rows] = (qacc[rows, :] * scale).T.astype(BF16)
                for at in range(q_tile // CHUNK):
                    back_one(DQ, i * (q_tile // CHUNK) + at, *dq_pair)
        dkvgive[block] = joined(1 - core).astype(BF16)
        dkvs_copy(block).start()
        keep[block] = joined(core)

    dkvs_copy(0).wait_recv()
    dkvx_copy(2).wait_recv()
    total = keep[0] + dkvtake[0].astype(F32) + dkvrecv[1].astype(F32)
    dkvown[0] = total.astype(BF16)
    dkv_start(0)

    back_arrived(OUT, *o_pair)
    for head in range(column):
        rows = pl.ds(head * depth, depth)
        projt[rows, :] = ofin[head].astype(F32)[PAD:]
    attended = projt[:head_width, :].T.astype(BF16)
    for at, size in spans(width, 512):
        cols = pl.ds(at, size)
        term = dot(attended, wout[:, cols])
        outv[:, cols] = (binput[:, cols].astype(F32) + term).astype(BF16)
    out_store = pltpu.make_async_copy(outv, out_hbm, store_sem.at[0])
    out_store.start()

    for offset in (1, 3):
        dkvx_copy(offset).wait_recv()
    dkvown[1] = (dkvrecv[0].astype(F32) + dkvrecv[2].astype(F32)).astype(BF16)
    dkv_start(1)

    def back_project(part):
        rows = pl.ds(part * head_width, head_width)
        gproj[part] = projt[rows, :].T.astype(BF16)

    back_arrived(DQ, *dq_pair)
    for head in range(column):
        projt[pl.ds(head * depth, depth), :] = dqfin[head].astype(F32)[:depth]
    back_project(0)
    for at, size in spans(width, 512):
        cols = pl.ds(at, size)
        ginput[:, cols] = dot(gproj[0], win[pl.ds(0, head_width), cols])
    dkv_arrived()
    for head in range(column):
        both = dkvfin[head].astype(F32)
        projt[pl.ds(head_width + head * depth, depth), :] = both[:depth]
        projt[pl.ds(2 * head_width + head * depth, depth), :] = both[depth:]
    for part in (1, 2):
        back_project(part)
    for at, size in spans(width, 512):
        cols = pl.ds(at, size)
        ginput[:, cols] += sum(
            dot(gproj[part], win[pl.ds(part * head_width, head_width), cols])
            for part in (1, 2)
        )

    def gm_copy(i):
        rows = pl.ds(*row_spans[i])
        return remote(
            gm_send.at[rows], gm_recv.at[rows], gm_ssem.at[i], gm_rsem.at[i], partner
        )

    for i, (at, size) in enumerate(row_spans):
        rows = pl.ds(at, size)
        hat, rate = stats(binput[rows, :].astype(F32))
        grad = ups[rows, :].astype(F32) + norm_back(hat, rate, ginput[rows, :])
        ginput[rows, :] = grad

        @pl.when(is_upper)
        def _():
            hat, rate = stats(mixed[rows, :])
            gm_send[rows, :] = norm_back(hat, rate, ginput[rows, :]).astype(BF16)
            gm_copy(i).start()

    @pl.when(is_upper)
    def _():
        ginput[...] = jnp.zeros_like(ginput)
        for i in range(width // CHUNK):
            turn(gm_send, i)

    @pl.when(is_lower)
    def _():
        for i in range(len(row_spans)):
            gm_copy(i).wait_recv()
        for i in range(width // CHUNK):
            turn(gm_recv, i)

    half = width // 2

    @pl.loop(0, 2)
    def _(i):
        rows = pl.ds(pl.multiple_of(i * half, 16), half)
        gnt[rows, :] = dot(skipw[rows, :], flip[...])

    out_store.wait()
    for i in range(width // CHUNK):
        cols = pl.ds(i * CHUNK, CHUNK)
        term = ginput[:, cols] + gnt[pl.ds(i * CHUNK, CHUNK), :].T
        outv[:, cols] = term.astype(BF16)
    glat_store = pltpu.make_async_copy(outv, glat_hbm, store_sem.at[1])
    glat_store.start()

    head_sent(GRAD, *g_pair)
    head_sent(QUERY, *q_pair)
    back_sent(OUT, *o_pair)
    back_sent(DQ, *dq_pair)
    kv_sent()
    dkv_sent(0)
    dkv_sent(1)

    @pl.loop(0, part_size)
    def _(at):
        kvs_copy(0, at).wait_send()
        for offset in range(1, rows_k):
            kvx_copy(offset, at).wait_send()
            kvs_copy(offset, at).wait_send()

    dkvs_copy(0).wait_send()
    for offset in range(1, rows_k):
        dkvx_copy(offset).wait_send()
        dkvs_copy(offset).wait_send()

    @pl.when(is_lower)
    def _():
        for i in range(len(skip_spans)):
            skip_copy(i).wait_send()

    @pl.when(is_upper)
    def _():
        for i in range(len(row_spans)):
            gm_copy(i).wait_send()

    glat_store.wait()


def settle(out, glat, out_hbm, glat_hbm, held, sem):
    ins = [
        pltpu.make_async_copy(out, held.at[0], sem.at[0]),
        pltpu.make_async_copy(glat, held.at[1], sem.at[1]),
    ]
    outs = [
        pltpu.make_async_copy(held.at[0], out_hbm, sem.at[2]),
        pltpu.make_async_copy(held.at[1], glat_hbm, sem.at[3]),
    ]
    for copy in ins:
        copy.start()
    for copy, onward in zip(ins, outs):
        copy.wait()
        onward.start()
    for copy in outs:
        copy.wait()


def body(rows_h, rows_k, latents, skip_weight, project_in, project_out, upstream):
    tok, width = latents.shape[1:]
    head_width = project_out.shape[1]
    column = rows_h * CORES
    depth = head_width // column
    padded = depth + PAD
    span = column * tok
    part = span // 2
    n_skip = len(spans(width, 512))
    n_rows = len(spans(tok, 32))
    wide = (tok, width)
    vmem = pltpu.VMEM
    dma = pltpu.SemaphoreType.DMA
    scratch = [
        vmem(wide, BF16),
        vmem((width, width), BF16),
        vmem((3 * head_width, width), BF16),
        vmem((head_width, width), BF16),
        vmem(wide, BF16),
        vmem(wide, BF16),
        vmem(wide, BF16),
        vmem(wide, F32),
        vmem(wide, BF16),
        vmem(wide, BF16),
        vmem((width, tok), BF16),
        vmem((3 * head_width, tok), F32),
        vmem((column, padded, tok), BF16),
        vmem((column, 2 * depth, tok), BF16),
        vmem((column, padded, tok), BF16),
        vmem((padded, span), BF16),
        vmem((padded, span), BF16),
        vmem((rows_k, 2 * depth, span), BF16),
        vmem((rows_k, span, padded), BF16),
        vmem((rows_k, span, padded), BF16),
        vmem((span, padded), BF16),
        vmem((span, padded), F32),
        vmem((rows_k, span, span), BF16),
        vmem((rows_k, span, 1), F32),
        vmem((rows_k, span, 1), F32),
        vmem((span, 1), F32),
        vmem((span, padded), F32),
        vmem((span, padded), F32),
        vmem((2 * padded, span), F32),
        vmem((padded, span), BF16),
        vmem((padded, span), BF16),
        vmem((2, 2 * depth, part), BF16),
        vmem((rows_k, 2 * depth, part), F32),
        vmem((rows_k, 2 * depth, part), BF16),
        vmem((rows_k, 2 * depth, part), BF16),
        vmem((rows_k - 1, 2 * depth, part), BF16),
        vmem((rows_k - 1, 2 * depth, part), BF16),
        vmem((2, 2 * depth, part), BF16),
        vmem((column, padded, tok), BF16),
        vmem((column, padded, tok), BF16),
        vmem((column, 2 * depth, tok), BF16),
        vmem((3, tok, head_width), BF16),
        vmem((width, tok), F32),
        vmem(wide, F32),
        vmem(wide, BF16),
        vmem(wide, BF16),
        vmem(wide, BF16),
        dma((4 + n_skip,)),
        dma((2,)),
        dma((4, column)),
        dma((4, column)),
        dma((rows_h,)),
        dma((column // 2,)),
        dma((rows_k - 1, column // 2)),
        dma((rows_k - 1, column // 2)),
        dma((rows_k, column // 2)),
        dma((rows_k, column // 2)),
        dma((column // 2,)),
        dma((rows_k,)),
        dma((rows_k,)),
        dma((2, column // 2)),
        dma((column,)),
        dma((rows_k - 1,)),
        dma((rows_k - 1,)),
        dma((n_skip,)),
        dma((n_skip,)),
        dma((n_rows,)),
        dma((n_rows,)),
    ]
    out, glat = pl.pallas_call(
        functools.partial(kernel, rows_h, rows_k),
        out_shape=[jax.ShapeDtypeStruct(wide, BF16)] * 2,
        in_specs=[pl.BlockSpec(memory_space=pl.ANY)] * 5,
        out_specs=[pl.BlockSpec(memory_space=pl.ANY)] * 2,
        scratch_shapes=scratch,
        compiler_params=pltpu.CompilerParams(
            collective_id=0, has_side_effects=True, vmem_limit_bytes=56 * 2**20
        ),
    )(latents[0], skip_weight[0], project_in[0].T, project_out[0], upstream[0])
    out, glat = pl.pallas_call(
        settle,
        out_shape=[jax.ShapeDtypeStruct(wide, BF16)] * 2,
        in_specs=[pl.BlockSpec(memory_space=pl.ANY)] * 2,
        out_specs=[pl.BlockSpec(memory_space=pl.ANY)] * 2,
        scratch_shapes=[vmem((2,) + wide, BF16), dma((4,))],
        compiler_params=pltpu.CompilerParams(vmem_limit_bytes=56 * 2**20),
    )(out, glat)
    return out[None], glat[None]


def solution(mesh):
    rows_h = HEADS // 2
    rows_k = mesh.shape["seq"] // HEADS
    return jax.shard_map(
        functools.partial(body, rows_h, rows_k),
        mesh=mesh,
        in_specs=(
            P("section", "seq", None),
            P("section", None, None),
            P("section", None, None),
            P("section", None, None),
            P("section", "seq", None),
        ),
        out_specs=(P("section", "seq", None), P("section", "seq", None)),
        check_vma=False,
    )
```

```python
import functools
import math

import jax
import jax.numpy as jnp
from jax import lax
from jax.experimental import pallas as pl
from jax.experimental.pallas import tpu as pltpu
from jax.sharding import PartitionSpec as P

HEADS = 8
EPSILON = 1e-06
CORES = 2
CHUNK = 128
PAD = 8

MESH = pl.DeviceIdType.MESH
F32 = jnp.float32
BF16 = jnp.bfloat16

GRAD, QUERY, OUT, DQ = range(4)


def dot(a, b):
    return jnp.dot(a, b, preferred_element_type=F32)


def spans(extent, width):
    return [(at, min(width, extent - at)) for at in range(0, extent, width)]


def stats(value):
    center = value - jnp.mean(value, -1, keepdims=True)
    rate = lax.rsqrt(jnp.mean(center * center, -1, keepdims=True) + EPSILON)
    return center * rate, rate


def norm_back(hat, rate, grad):
    inner = jnp.mean(grad * hat, -1, keepdims=True)
    return rate * (grad - jnp.mean(grad, -1, keepdims=True) - hat * inner)


def kernel(
    rows_h,
    rows_k,
    lat_hbm,
    skipw_hbm,
    win_hbm,
    wout_hbm,
    ups_hbm,
    out_hbm,
    glat_hbm,
    lat,
    skipw,
    win,
    wout,
    ups,
    skip_send,
    skip_recv,
    mixed,
    binput,
    normed,
    flip,
    projt,
    gsend,
    kvsend,
    qsend,
    gt,
    qt,
    kv,
    knat,
    vnat,
    qnat,
    gnat,
    exps,
    tops,
    facs,
    delta,
    oacc,
    qacc,
    kvacc,
    ot,
    dqt,
    kvin,
    keep,
    dkvgive,
    dkvtake,
    dkvpart,
    dkvrecv,
    dkvown,
    ofin,
    dqfin,
    dkvfin,
    gproj,
    gnt,
    ginput,
    gm_send,
    gm_recv,
    outv,
    load_sem,
    store_sem,
    col_send,
    col_recv,
    kv_send,
    kv_recv,
    kvx_send,
    kvx_recv,
    kvs_send,
    kvs_recv,
    place_sem,
    dkvs_send,
    dkvs_recv,
    dkv_send,
    dkv_recv,
    dkvx_send,
    dkvx_recv,
    turn_sem,
    skip_ssem,
    skip_rsem,
    gm_ssem,
    gm_rsem,
):
    sections = lax.axis_size("section")
    section = lax.axis_index("section")
    place = lax.axis_index("seq")
    line = place // (rows_h * CORES)
    row = lax.rem(place // CORES, rows_h)
    core = lax.rem(place, CORES)
    is_upper = section >= sections // 2
    is_lower = jnp.logical_not(is_upper)
    column = rows_h * CORES
    me = row * CORES + core
    even = lax.rem(line, 2)
    pair = line // 2
    own_head = 2 * row + even
    query_line = 2 * pair + core

    tok, width = lat.shape
    head_width = wout.shape[0]
    depth = head_width // column
    padded = depth + PAD
    span = column * CHUNK
    scale = 1.0 / math.sqrt(depth)
    rate2 = scale * math.log2(math.e)
    q_tile = 512
    half_span = span // 2

    def device(at_row, at_line, at_core):
        return {
            "section": section,
            "seq": (at_line * rows_h + at_row) * CORES + at_core,
        }

    def owner(index, at_line):
        return device(index // CORES, at_line, lax.rem(index, CORES))

    def across(offset):
        there = (line, line + 1 - 2 * even, lax.rem(line + 2, rows_k), rows_k - 1 - line)[offset]
        return device(row, there, core)

    sibling = device(row, line, 1 - core)
    partner = {"section": sections - 1 - section, "seq": place}

    def remote(src, dst, send, recv, device):
        return pltpu.make_async_remote_copy(
            src_ref=src,
            dst_ref=dst,
            send_sem=send,
            recv_sem=recv,
            device_id=device,
            device_id_type=MESH,
        )

    def lanes(index):
        return pl.ds(pl.multiple_of(index * CHUNK, CHUNK), CHUNK)

    def head_copy(kind, head, src, dst):
        there = device(head // 2, 2 * pair + lax.rem(head, 2), even)
        return remote(
            src.at[head],
            dst.at[:, lanes(me)],
            col_send.at[kind, head],
            col_recv.at[kind, me],
            there,
        )

    def back_copy(kind, index, src, dst):
        return remote(
            src.at[:, lanes(index)],
            dst.at[own_head],
            col_send.at[kind, index],
            col_recv.at[kind, own_head],
            owner(index, query_line),
        )

    def head_start(kind, src, dst):
        @pl.loop(0, column)
        def _(step):
            head = lax.rem(own_head + step, column)
            mine = (step == 0) & (even == core)

            @pl.when(mine)
            def _():
                pltpu.make_async_copy(
                    src.at[head], dst.at[:, lanes(me)], col_recv.at[kind, me]
                ).start()

            @pl.when(jnp.logical_not(mine))
            def _():
                head_copy(kind, head, src, dst).start()

    def head_arrived(kind, src, dst):
        @pl.loop(0, column)
        def _(index):
            pltpu.make_async_copy(
                src.at[0], dst.at[:, lanes(index)], col_recv.at[kind, index]
            ).wait()

    def head_sent(kind, src, dst):
        @pl.loop(0, column)
        def _(step):
            head = lax.rem(own_head + step, column)

            @pl.when((step > 0) | (even != core))
            def _():
                head_copy(kind, head, src, dst).wait_send()

    def back_one(kind, index, src, dst):
        mine = (index == me) & (even == core)

        @pl.when(mine)
        def _():
            pltpu.make_async_copy(
                src.at[:, lanes(index)], dst.at[own_head], col_recv.at[kind, own_head]
            ).start()

        @pl.when(jnp.logical_not(mine))
        def _():
            back_copy(kind, index, src, dst).start()

    def back_start(kind, src, dst):
        @pl.loop(0, column)
        def _(index):
            back_one(kind, index, src, dst)

    def back_arrived(kind, src, dst):
        @pl.loop(0, column)
        def _(head):
            pltpu.make_async_copy(
                src.at[:, lanes(0)], dst.at[head], col_recv.at[kind, head]
            ).wait()

    def back_sent(kind, src, dst):
        @pl.loop(0, column)
        def _(step):
            index = lax.rem(me + step, column)

            @pl.when((step > 0) | (even != core))
            def _():
                back_copy(kind, index, src, dst).wait_send()

    def kv_copy(step):
        there = lax.rem(row + step, rows_h)
        return remote(
            kvsend.at[pl.ds(2 * there, 2)],
            kvin.at[:, :, lanes(row)],
            kv_send.at[step],
            kv_recv.at[row],
            device(there, line, core),
        )

    def kv_start():
        pltpu.make_async_copy(
            kvsend.at[pl.ds(2 * row, 2)], kvin.at[:, :, lanes(row)], kv_recv.at[row]
        ).start()

        @pl.loop(1, rows_h)
        def _(step):
            kv_copy(step).start()

    def kv_arrived(at):
        pltpu.make_async_copy(
            kvsend.at[pl.ds(0, 2)], kvin.at[:, :, lanes(at)], kv_recv.at[at]
        ).wait()

    def kv_sent():
        @pl.loop(1, rows_h)
        def _(step):
            kv_copy(step).wait_send()

    def half_lanes(at):
        return lanes(core * rows_h + at)

    def kvx_copy(offset, at):
        head = even if offset == 2 else 1 - even
        return remote(
            kvin.at[head, :, lanes(at)],
            kv.at[offset, :, half_lanes(at)],
            kvx_send.at[offset - 1, at],
            kvx_recv.at[offset - 1, at],
            across(offset),
        )

    def kvs_copy(offset, at):
        there = kv.at[offset, :, half_lanes(at)]
        here = kvin.at[even, :, lanes(at)] if offset == 0 else there
        return remote(
            here, there, kvs_send.at[offset, at], kvs_recv.at[offset, at], sibling
        )

    def kv_place(at):
        return pltpu.make_async_copy(
            kvin.at[even, :, lanes(at)], kv.at[0, :, half_lanes(at)], place_sem.at[at]
        )

    def dkvs_copy(block):
        return remote(
            dkvgive.at[block],
            dkvtake.at[block],
            dkvs_send.at[block],
            dkvs_recv.at[block],
            sibling,
        )

    def dkvx_copy(offset):
        return remote(
            dkvpart.at[offset - 1],
            dkvrecv.at[offset - 1],
            dkvx_send.at[offset - 1],
            dkvx_recv.at[offset - 1],
            across(offset),
        )

    def dkv_copy(which, step):
        head = 2 * row + (even if which == 0 else 1 - even)
        there = lax.rem(row + step, rows_h)
        return remote(
            dkvown.at[which, :, lanes(there)],
            dkvfin.at[head],
            dkv_send.at[which, step],
            dkv_recv.at[head],
            device(there, line, core),
        )

    def dkv_start(which):
        head = 2 * row + (even if which == 0 else 1 - even)
        pltpu.make_async_copy(
            dkvown.at[which, :, lanes(row)], dkvfin.at[head], dkv_recv.at[head]
        ).start()

        @pl.loop(1, rows_h)
        def _(step):
            dkv_copy(which, step).start()

    def dkv_sent(which):
        @pl.loop(1, rows_h)
        def _(step):
            dkv_copy(which, step).wait_send()

    def dkv_arrived():
        @pl.loop(0, column)
        def _(head):
            pltpu.make_async_copy(
                dkvown.at[0, :, lanes(0)], dkvfin.at[head], dkv_recv.at[head]
            ).wait()

    g_pair = (gsend, gt)
    q_pair = (qsend, qt)
    o_pair = (ot, ofin)
    dq_pair = (dqt, dqfin)

    skip_spans = spans(width, 512)
    pieces = [(lat_hbm, lat)]
    for at, size in skip_spans:
        cols = pl.ds(at, size)
        pieces.append((skipw_hbm.at[:, cols], skipw.at[:, cols]))
    pieces += [(ups_hbm, ups), (wout_hbm, wout), (win_hbm, win)]
    loads = [
        pltpu.make_async_copy(src, dst, load_sem.at[i])
        for i, (src, dst) in enumerate(pieces)
    ]
    lat_load, *skip_loads, ups_load, wout_load, win_load = loads
    for load in loads:
        load.start()

    barrier = pltpu.get_barrier_semaphore()
    peers = [owner(lax.rem(me + step, column), line) for step in range(1, column)]
    peers += [owner(index, line + 1 - 2 * even) for index in range(column)]
    peers += [across(offset) for offset in range(2, rows_k)]
    peers.append(partner)
    for peer in peers:
        pl.semaphore_signal(barrier, inc=1, device_id=peer, device_id_type=MESH)

    def skip_copy(i):
        at, size = skip_spans[i]
        cols = pl.ds(at, size)
        return remote(
            skip_send.at[:, cols],
            skip_recv.at[:, cols],
            skip_ssem.at[i],
            skip_rsem.at[i],
            partner,
        )

    lat_load.wait()
    for i, (at, size) in enumerate(skip_spans):
        skip_loads[i].wait()
        product = dot(lat[...], skipw[:, pl.ds(at, size)])
        mixed[:, pl.ds(at, size)] = product
        skip_send[:, pl.ds(at, size)] = product.astype(BF16)
        if i == 0:
            pl.semaphore_wait(barrier, len(peers))

        @pl.when(is_lower & (core == 0))
        def _():
            skip_copy(i).start()

    def turn(source, i):
        block = source[:, pl.ds(i * CHUNK, CHUNK)]
        flip[pl.ds(i * CHUNK, CHUNK), :] = block.astype(F32).T.astype(BF16)

    ups_load.wait()
    for i in range(width // CHUNK):
        turn(ups, i)
    wout_load.wait()
    blank = jnp.zeros((PAD, CHUNK), F32)

    @pl.loop(0, column // 2)
    def _(i):
        rows = pl.ds(pl.multiple_of(i * 2 * depth, 16), 2 * depth)
        two = dot(wout[rows, :], flip[...])
        gsend[2 * i] = jnp.concatenate([blank, two[:depth]], 0).astype(BF16)
        gsend[2 * i + 1] = jnp.concatenate([blank, two[depth:]], 0).astype(BF16)

    head_start(GRAD, *g_pair)

    @pl.when(is_lower & (core == 0))
    def _():
        for i in range(len(skip_spans) - 1):
            skip_copy(i).wait_send()
        pl.semaphore_signal(turn_sem, inc=1, device_id=sibling, device_id_type=MESH)

    @pl.when(is_lower & (core == 1))
    def _():
        pl.semaphore_wait(turn_sem, 1)
        for i in range(len(skip_spans)):
            skip_copy(i).start()

    row_spans = spans(tok, 32)

    @pl.when(is_upper)
    def _():
        for i in range(len(skip_spans)):
            skip_copy(i).wait_recv()
        for at, size in row_spans:
            rows = pl.ds(at, size)
            total = mixed[rows, :] + skip_recv[rows, :].astype(F32)
            mixed[rows, :] = total
            binput[rows, :] = stats(total)[0].astype(BF16)

    @pl.when(is_lower)
    def _():
        binput[...] = lat[...]

    for at, size in row_spans:
        rows = pl.ds(at, size)
        normed[rows, :] = stats(binput[rows, :].astype(F32))[0].astype(BF16)

    for i in range(width // CHUNK):
        turn(normed, i)
    win_load.wait()

    def project(part):
        rows = pl.ds(pl.multiple_of(part * head_width, 16), head_width)
        projt[rows, :] = dot(win[rows, :], flip[...])

    @pl.loop(1, 3)
    def _(part):
        project(part)

    for head in range(column):
        keys = projt[pl.ds(head_width + head * depth, depth), :]
        values = projt[pl.ds(2 * head_width + head * depth, depth), :]
        kvsend[head] = jnp.concatenate([keys, values], 0).astype(BF16)
    kv_start()
    project(0)
    for head in range(column):
        queries = projt[pl.ds(head * depth, depth), :]
        qsend[head] = jnp.concatenate([queries, blank], 0).astype(BF16)
    head_start(QUERY, *q_pair)

    @pl.loop(0, rows_h)
    def _(at):
        kv_arrived(at)
        kvs_copy(0, at).start()
        kv_place(at).start()
        for offset in range(1, rows_k):
            kvx_copy(offset, at).start()

    def take(block):
        @pl.loop(0, rows_h)
        def _(at):
            kvx_copy(block, at).wait_recv()
            kvs_copy(block, at).start()

    def natural(block, half):
        lane = lax.broadcasted_iota(jnp.int32, (half_span, padded), 1)
        cols = pl.ds(half * half_span, half_span)
        keys = kv[block, :padded, cols].astype(F32).T
        values = kv[block, depth - PAD :, cols].astype(F32).T
        knat[block, cols, :] = keys.astype(BF16)
        vnat[block, cols, :] = jnp.where(lane < PAD, 1.0, values).astype(BF16)

    head_arrived(GRAD, *g_pair)
    head_arrived(QUERY, *q_pair)
    for at, size in spans(span, q_tile):
        rows = pl.ds(at, size)
        qnat[rows, :] = qt[:, rows].astype(F32).T.astype(BF16)
        gnat[rows, :] = gt[:, rows].astype(F32).T

    tiles = span // q_tile
    middle_tile = (tiles - 1) // 2
    units = [(half, block) for half in range(2) for block in range(rows_k)]

    def forward_rows(unit, i):
        half, block = units[unit]
        rows = pl.ds(i * q_tile, q_tile)
        cols = pl.ds(half * half_span, half_span)
        scores = dot(qnat[rows, :], kv[block, :padded, cols])
        top = jnp.max(scores, -1, keepdims=True)
        if unit > 0:
            before = tops[unit - 1, rows, :]
            top = jnp.maximum(top, before)
        tops[unit, rows, :] = top
        lifted = jnp.exp2((scores - top) * rate2).astype(BF16)
        exps[block, rows, cols] = lifted
        term = dot(lifted, vnat[block, cols, :])
        if unit > 0:
            term += oacc[rows, :] * jnp.exp2((before - top) * rate2)
        oacc[rows, :] = term

    def await_half(half, block):
        @pl.when(core != half)
        def _():
            @pl.loop(0, rows_h)
            def _(at):
                other = lanes((1 - core) * rows_h + at)
                remote(
                    kv.at[block, :, other],
                    kv.at[block, :, other],
                    kvs_send.at[block, at],
                    kvs_recv.at[block, at],
                    sibling,
                ).wait_recv()

        if block == 0:

            @pl.when(core == half)
            def _():
                @pl.loop(0, rows_h)
                def _(at):
                    kv_place(at).wait()

    for unit, (half, block) in enumerate(units):
        await_half(half, block)
        natural(block, half)
        for i in range(tiles):
            forward_rows(unit, i)
            if i == middle_tile and block + 1 < rows_k:

                @pl.when(core == half)
                def _():
                    take(block + 1)

    for at, size in spans(span, q_tile):
        rows = pl.ds(at, size)
        total = oacc[rows, :]
        inverse = 1.0 / total[:, :1]
        mixed_values = (total * inverse).astype(BF16).astype(F32)
        ot[:, rows] = mixed_values.T.astype(BF16)
        delta[rows, :] = jnp.sum(gnat[rows, :] * mixed_values, -1, keepdims=True)
        last = tops[len(units) - 1, rows, :]
        for unit in range(len(units)):
            lift = jnp.exp2((tops[unit, rows, :] - last) * rate2)
            facs[unit, rows, :] = lift * inverse
        qacc[rows, :] = jnp.zeros((size, padded), F32)
    back_start(OUT, *o_pair)

    def backward_rows(half, block, i):
        rows = pl.ds(i * q_tile, q_tile)
        cols = pl.ds(half * half_span, half_span)
        factor = facs[units.index((half, block)), rows, :]
        grads = gnat[rows, :] * factor
        shift = delta[rows, :] * factor
        lifted = exps[block, rows, cols]
        back = dot(grads.astype(BF16), kv[block, depth - PAD :, cols]) - shift
        gscore = (lifted.astype(F32) * back).astype(BF16)
        qacc[rows, :] += dot(gscore, knat[block, cols, :])
        keys = dot(qt[:, rows], gscore)
        values = dot(grads.T.astype(BF16), lifted)
        if i > 0:
            keys += kvacc[:padded, :]
            values += kvacc[padded:, :]
        kvacc[:padded, :] = keys
        kvacc[padded:, :] = values

    def joined():
        keys = kvacc[:padded, :] * scale
        values = kvacc[padded:, :]
        middle = keys[depth - PAD :] + values[: 2 * PAD]
        return jnp.concatenate([keys[: depth - PAD], middle, values[2 * PAD :]], 0)

    def pass_on(block):
        dkvs_copy(block).wait_recv()
        total = keep[block] + dkvtake[block].astype(F32)
        dkvpart[block - 1] = total.astype(BF16)
        dkvx_copy(block).start()

    turns = [(half, block) for half in range(2) for block in (2, 3, 1, 0)]
    for n, (half, block) in enumerate(turns):
        for i in range(tiles):
            backward_rows(half, block, i)
            if n > 0 and i == middle_tile and turns[n - 1][1] > 0:
                half_before, block_before = turns[n - 1]

                @pl.when(core == half_before)
                def _():
                    pass_on(block_before)

            if n == len(turns) - 1:
                rows = pl.ds(i * q_tile, q_tile)
                dqt[:, rows] = (qacc[rows, :] * scale).T.astype(BF16)
                for at in range(q_tile // CHUNK):
                    back_one(DQ, i * (q_tile // CHUNK) + at, *dq_pair)

        @pl.when(core != half)
        def _():
            dkvgive[block] = joined().astype(BF16)
            dkvs_copy(block).start()

        @pl.when(core == half)
        def _():
            keep[block] = joined()

    dkvs_copy(0).wait_recv()
    dkvx_copy(2).wait_recv()
    total = keep[0] + dkvtake[0].astype(F32) + dkvrecv[1].astype(F32)
    dkvown[0] = total.astype(BF16)
    dkv_start(0)

    back_arrived(OUT, *o_pair)
    for head in range(column):
        rows = pl.ds(head * depth, depth)
        projt[rows, :] = ofin[head].astype(F32)[PAD:]
    attended = projt[:head_width, :].T.astype(BF16)
    for at, size in spans(width, 512):
        cols = pl.ds(at, size)
        term = dot(attended, wout[:, cols])
        outv[:, cols] = (binput[:, cols].astype(F32) + term).astype(BF16)
    out_store = pltpu.make_async_copy(outv, out_hbm, store_sem.at[0])
    out_store.start()

    for offset in (1, 3):
        dkvx_copy(offset).wait_recv()
    dkvown[1] = (dkvrecv[0].astype(F32) + dkvrecv[2].astype(F32)).astype(BF16)
    dkv_start(1)

    def back_project(part):
        rows = pl.ds(part * head_width, head_width)
        gproj[part] = projt[rows, :].T.astype(BF16)

    back_arrived(DQ, *dq_pair)
    for head in range(column):
        projt[pl.ds(head * depth, depth), :] = dqfin[head].astype(F32)[:depth]
    back_project(0)
    for at, size in spans(width, 512):
        cols = pl.ds(at, size)
        ginput[:, cols] = dot(gproj[0], win[pl.ds(0, head_width), cols])
    dkv_arrived()
    for head in range(column):
        both = dkvfin[head].astype(F32)
        projt[pl.ds(head_width + head * depth, depth), :] = both[:depth]
        projt[pl.ds(2 * head_width + head * depth, depth), :] = both[depth:]
    for part in (1, 2):
        back_project(part)
    for at, size in spans(width, 512):
        cols = pl.ds(at, size)
        ginput[:, cols] += sum(
            dot(gproj[part], win[pl.ds(part * head_width, head_width), cols])
            for part in (1, 2)
        )

    def gm_copy(i):
        rows = pl.ds(*row_spans[i])
        return remote(
            gm_send.at[rows], gm_recv.at[rows], gm_ssem.at[i], gm_rsem.at[i], partner
        )

    for i, (at, size) in enumerate(row_spans):
        rows = pl.ds(at, size)
        hat, rate = stats(binput[rows, :].astype(F32))
        grad = ups[rows, :].astype(F32) + norm_back(hat, rate, ginput[rows, :])
        ginput[rows, :] = grad

        @pl.when(is_upper)
        def _():
            hat, rate = stats(mixed[rows, :])
            gm_send[rows, :] = norm_back(hat, rate, ginput[rows, :]).astype(BF16)
            gm_copy(i).start()

    @pl.when(is_upper)
    def _():
        ginput[...] = jnp.zeros_like(ginput)
        for i in range(width // CHUNK):
            turn(gm_send, i)

    @pl.when(is_lower)
    def _():
        for i in range(len(row_spans)):
            gm_copy(i).wait_recv()
        for i in range(width // CHUNK):
            turn(gm_recv, i)

    half = width // 2

    @pl.loop(0, 2)
    def _(i):
        rows = pl.ds(pl.multiple_of(i * half, 16), half)
        gnt[rows, :] = dot(skipw[rows, :], flip[...])

    out_store.wait()
    for i in range(width // CHUNK):
        cols = pl.ds(i * CHUNK, CHUNK)
        term = ginput[:, cols] + gnt[pl.ds(i * CHUNK, CHUNK), :].T
        outv[:, cols] = term.astype(BF16)
    glat_store = pltpu.make_async_copy(outv, glat_hbm, store_sem.at[1])
    glat_store.start()

    head_sent(GRAD, *g_pair)
    head_sent(QUERY, *q_pair)
    back_sent(OUT, *o_pair)
    back_sent(DQ, *dq_pair)
    kv_sent()
    dkv_sent(0)
    dkv_sent(1)

    @pl.loop(0, rows_h)
    def _(at):
        kvs_copy(0, at).wait_send()
        for offset in range(1, rows_k):
            kvx_copy(offset, at).wait_send()
            kvs_copy(offset, at).wait_send()

    dkvs_copy(0).wait_send()
    for offset in range(1, rows_k):
        dkvx_copy(offset).wait_send()
        dkvs_copy(offset).wait_send()

    @pl.when(is_lower & (core == 0))
    def _():
        skip_copy(len(skip_spans) - 1).wait_send()

    @pl.when(is_lower & (core == 1))
    def _():
        for i in range(len(skip_spans)):
            skip_copy(i).wait_send()

    @pl.when(is_upper)
    def _():
        for i in range(len(row_spans)):
            gm_copy(i).wait_send()

    glat_store.wait()


def settle(out, glat, out_hbm, glat_hbm, held, sem):
    ins = [
        pltpu.make_async_copy(out, held.at[0], sem.at[0]),
        pltpu.make_async_copy(glat, held.at[1], sem.at[1]),
    ]
    outs = [
        pltpu.make_async_copy(held.at[0], out_hbm, sem.at[2]),
        pltpu.make_async_copy(held.at[1], glat_hbm, sem.at[3]),
    ]
    for copy in ins:
        copy.start()
    for copy, onward in zip(ins, outs):
        copy.wait()
        onward.start()
    for copy in outs:
        copy.wait()


def body(rows_h, rows_k, latents, skip_weight, project_in, project_out, upstream):
    tok, width = latents.shape[1:]
    head_width = project_out.shape[1]
    column = rows_h * CORES
    depth = head_width // column
    padded = depth + PAD
    span = column * tok
    part = span // 2
    n_skip = len(spans(width, 512))
    n_rows = len(spans(tok, 32))
    wide = (tok, width)
    vmem = pltpu.VMEM
    dma = pltpu.SemaphoreType.DMA
    scratch = [
        vmem(wide, BF16),
        vmem((width, width), BF16),
        vmem((3 * head_width, width), BF16),
        vmem((head_width, width), BF16),
        vmem(wide, BF16),
        vmem(wide, BF16),
        vmem(wide, BF16),
        vmem(wide, F32),
        vmem(wide, BF16),
        vmem(wide, BF16),
        vmem((width, tok), BF16),
        vmem((3 * head_width, tok), F32),
        vmem((column, padded, tok), BF16),
        vmem((column, 2 * depth, tok), BF16),
        vmem((column, padded, tok), BF16),
        vmem((padded, span), BF16),
        vmem((padded, span), BF16),
        vmem((rows_k, 2 * depth, span), BF16),
        vmem((rows_k, span, padded), BF16),
        vmem((rows_k, span, padded), BF16),
        vmem((span, padded), BF16),
        vmem((span, padded), F32),
        vmem((rows_k, span, span), BF16),
        vmem((2 * rows_k, span, 1), F32),
        vmem((2 * rows_k, span, 1), F32),
        vmem((span, 1), F32),
        vmem((span, padded), F32),
        vmem((span, padded), F32),
        vmem((2 * padded, part), F32),
        vmem((padded, span), BF16),
        vmem((padded, span), BF16),
        vmem((2, 2 * depth, part), BF16),
        vmem((rows_k, 2 * depth, part), F32),
        vmem((rows_k, 2 * depth, part), BF16),
        vmem((rows_k, 2 * depth, part), BF16),
        vmem((rows_k - 1, 2 * depth, part), BF16),
        vmem((rows_k - 1, 2 * depth, part), BF16),
        vmem((2, 2 * depth, part), BF16),
        vmem((column, padded, tok), BF16),
        vmem((column, padded, tok), BF16),
        vmem((column, 2 * depth, tok), BF16),
        vmem((3, tok, head_width), BF16),
        vmem((width, tok), F32),
        vmem(wide, F32),
        vmem(wide, BF16),
        vmem(wide, BF16),
        vmem(wide, BF16),
        dma((4 + n_skip,)),
        dma((2,)),
        dma((4, column)),
        dma((4, column)),
        dma((rows_h,)),
        dma((column // 2,)),
        dma((rows_k - 1, column // 2)),
        dma((rows_k - 1, column // 2)),
        dma((rows_k, column // 2)),
        dma((rows_k, column // 2)),
        dma((column // 2,)),
        dma((rows_k,)),
        dma((rows_k,)),
        dma((2, column // 2)),
        dma((column,)),
        dma((rows_k - 1,)),
        dma((rows_k - 1,)),
        pltpu.SemaphoreType.REGULAR,
        dma((n_skip,)),
        dma((n_skip,)),
        dma((n_rows,)),
        dma((n_rows,)),
    ]
    out, glat = pl.pallas_call(
        functools.partial(kernel, rows_h, rows_k),
        out_shape=[jax.ShapeDtypeStruct(wide, BF16)] * 2,
        in_specs=[pl.BlockSpec(memory_space=pl.ANY)] * 5,
        out_specs=[pl.BlockSpec(memory_space=pl.ANY)] * 2,
        scratch_shapes=scratch,
        compiler_params=pltpu.CompilerParams(
            collective_id=0, has_side_effects=True, vmem_limit_bytes=56 * 2**20
        ),
    )(latents[0], skip_weight[0], project_in[0].T, project_out[0], upstream[0])
    out, glat = pl.pallas_call(
        settle,
        out_shape=[jax.ShapeDtypeStruct(wide, BF16)] * 2,
        in_specs=[pl.BlockSpec(memory_space=pl.ANY)] * 2,
        out_specs=[pl.BlockSpec(memory_space=pl.ANY)] * 2,
        scratch_shapes=[vmem((2,) + wide, BF16), dma((4,))],
        compiler_params=pltpu.CompilerParams(vmem_limit_bytes=56 * 2**20),
    )(out, glat)
    return out[None], glat[None]


def solution(mesh):
    rows_h = HEADS // 2
    rows_k = mesh.shape["seq"] // HEADS
    return jax.shard_map(
        functools.partial(body, rows_h, rows_k),
        mesh=mesh,
        in_specs=(
            P("section", "seq", None),
            P("section", None, None),
            P("section", None, None),
            P("section", None, None),
            P("section", "seq", None),
        ),
        out_specs=(P("section", "seq", None), P("section", "seq", None)),
        check_vma=False,
    )
```

```python
import functools
import math

import jax
import jax.numpy as jnp
from jax import lax
from jax.experimental import pallas as pl
from jax.experimental.pallas import tpu as pltpu
from jax.sharding import PartitionSpec as P

HEADS = 8
EPSILON = 1e-06
CORES = 2
CHUNK = 128
PAD = 8

MESH = pl.DeviceIdType.MESH
F32 = jnp.float32
BF16 = jnp.bfloat16

GRAD, QUERY, OUT, DQ = range(4)


def dot(a, b):
    return jnp.dot(a, b, preferred_element_type=F32)


def spans(extent, width):
    return [(at, min(width, extent - at)) for at in range(0, extent, width)]


def stats(value):
    center = value - jnp.mean(value, -1, keepdims=True)
    rate = lax.rsqrt(jnp.mean(center * center, -1, keepdims=True) + EPSILON)
    return center * rate, rate


def norm_back(hat, rate, grad):
    inner = jnp.mean(grad * hat, -1, keepdims=True)
    return rate * (grad - jnp.mean(grad, -1, keepdims=True) - hat * inner)


def kernel(
    rows_h,
    rows_k,
    lat_hbm,
    skipw_hbm,
    win_hbm,
    wout_hbm,
    ups_hbm,
    out_hbm,
    glat_hbm,
    lat,
    skipw,
    win,
    wout,
    ups,
    skip_send,
    skip_recv,
    mixed,
    binput,
    normed,
    flip,
    projt,
    gsend,
    kvsend,
    qsend,
    gt,
    qt,
    kv,
    knat,
    vnat,
    qnat,
    gnat,
    exps,
    tops,
    facs,
    delta,
    oacc,
    qacc,
    kvacc,
    ot,
    dqt,
    kvin,
    keep,
    dkvgive,
    dkvtake,
    dkvpart,
    dkvrecv,
    dkvown,
    ofin,
    dqfin,
    dkvfin,
    gproj,
    gnt,
    ginput,
    gm_send,
    gm_recv,
    outv,
    load_sem,
    store_sem,
    col_send,
    col_recv,
    kv_send,
    kv_recv,
    kvx_send,
    kvx_recv,
    kvs_send,
    kvs_recv,
    place_sem,
    dkvs_send,
    dkvs_recv,
    dkv_send,
    dkv_recv,
    dkvx_send,
    dkvx_recv,
    skip_ssem,
    skip_rsem,
    gm_ssem,
    gm_rsem,
):
    sections = lax.axis_size("section")
    section = lax.axis_index("section")
    place = lax.axis_index("seq")
    row = place // (rows_k * CORES)
    line = lax.rem(place // CORES, rows_k)
    core = lax.rem(place, CORES)
    is_upper = section >= sections // 2
    is_lower = jnp.logical_not(is_upper)
    column = rows_h * CORES
    part_size = column // 2
    me = row * CORES + core
    even = lax.rem(line, 2)
    pair = line // 2
    own_head = 2 * row + even
    query_line = 2 * pair + core

    tok, width = lat.shape
    head_width = wout.shape[0]
    depth = head_width // column
    padded = depth + PAD
    span = column * CHUNK
    scale = 1.0 / math.sqrt(depth)
    rate2 = scale * math.log2(math.e)
    q_tile = 256

    def device(at_row, at_line, at_core):
        return {
            "section": section,
            "seq": (at_row * rows_k + at_line) * CORES + at_core,
        }

    def owner(index, at_line):
        return device(index // CORES, at_line, lax.rem(index, CORES))

    def across(offset):
        there = (line, line + 1 - 2 * even, lax.rem(line + 2, rows_k), rows_k - 1 - line)[offset]
        return device(row, there, core)

    sibling = device(row, line, 1 - core)
    partner = {"section": sections - 1 - section, "seq": place}

    def remote(src, dst, send, recv, device):
        return pltpu.make_async_remote_copy(
            src_ref=src,
            dst_ref=dst,
            send_sem=send,
            recv_sem=recv,
            device_id=device,
            device_id_type=MESH,
        )

    def lanes(index):
        return pl.ds(pl.multiple_of(index * CHUNK, CHUNK), CHUNK)

    def head_copy(kind, head, src, dst):
        there = device(head // 2, 2 * pair + lax.rem(head, 2), even)
        return remote(
            src.at[head],
            dst.at[:, lanes(me)],
            col_send.at[kind, head],
            col_recv.at[kind, me],
            there,
        )

    def back_copy(kind, index, src, dst):
        return remote(
            src.at[:, lanes(index)],
            dst.at[own_head],
            col_send.at[kind, index],
            col_recv.at[kind, own_head],
            owner(index, query_line),
        )

    def head_start(kind, src, dst):
        @pl.loop(0, column)
        def _(step):
            head = lax.rem(own_head + step, column)
            mine = (step == 0) & (even == core)

            @pl.when(mine)
            def _():
                pltpu.make_async_copy(
                    src.at[head], dst.at[:, lanes(me)], col_recv.at[kind, me]
                ).start()

            @pl.when(jnp.logical_not(mine))
            def _():
                head_copy(kind, head, src, dst).start()

    def head_arrived(kind, src, dst):
        @pl.loop(0, column)
        def _(index):
            pltpu.make_async_copy(
                src.at[0], dst.at[:, lanes(index)], col_recv.at[kind, index]
            ).wait()

    def head_sent(kind, src, dst):
        @pl.loop(0, column)
        def _(step):
            head = lax.rem(own_head + step, column)

            @pl.when((step > 0) | (even != core))
            def _():
                head_copy(kind, head, src, dst).wait_send()

    def back_one(kind, index, src, dst):
        mine = (index == me) & (even == core)

        @pl.when(mine)
        def _():
            pltpu.make_async_copy(
                src.at[:, lanes(index)], dst.at[own_head], col_recv.at[kind, own_head]
            ).start()

        @pl.when(jnp.logical_not(mine))
        def _():
            back_copy(kind, index, src, dst).start()

    def back_start(kind, src, dst):
        @pl.loop(0, column)
        def _(index):
            back_one(kind, index, src, dst)

    def back_arrived(kind, src, dst):
        @pl.loop(0, column)
        def _(head):
            pltpu.make_async_copy(
                src.at[:, lanes(0)], dst.at[head], col_recv.at[kind, head]
            ).wait()

    def back_sent(kind, src, dst):
        @pl.loop(0, column)
        def _(step):
            index = lax.rem(me + step, column)

            @pl.when((step > 0) | (even != core))
            def _():
                back_copy(kind, index, src, dst).wait_send()

    half_core = me // part_size
    half_at = lax.rem(me, part_size)
    kv_mine = half_core == core

    def kv_copy(step):
        at_row = lax.rem(row + step, rows_h)
        return remote(
            kvsend.at[pl.ds(2 * at_row, 2)],
            kvin.at[:, :, lanes(half_at)],
            kv_send.at[step],
            kv_recv.at[half_at],
            device(at_row, line, half_core),
        )

    def kv_own():
        return pltpu.make_async_copy(
            kvsend.at[pl.ds(2 * row, 2)],
            kvin.at[:, :, lanes(half_at)],
            kv_recv.at[half_at],
        )

    def kv_start():
        @pl.when(kv_mine)
        def _():
            kv_own().start()

        @pl.when(jnp.logical_not(kv_mine))
        def _():
            kv_copy(0).start()

        @pl.loop(1, rows_h)
        def _(step):
            kv_copy(step).start()

    def kv_arrived(at):
        pltpu.make_async_copy(
            kvsend.at[pl.ds(0, 2)], kvin.at[:, :, lanes(at)], kv_recv.at[at]
        ).wait()

    def kv_sent():
        @pl.when(jnp.logical_not(kv_mine))
        def _():
            kv_copy(0).wait_send()

        @pl.loop(1, rows_h)
        def _(step):
            kv_copy(step).wait_send()

    def half_lanes(at):
        return lanes(core * part_size + at)

    def kvx_copy(offset, at):
        head = even if offset == 2 else 1 - even
        return remote(
            kvin.at[head, :, lanes(at)],
            kv.at[offset, :, half_lanes(at)],
            kvx_send.at[offset - 1, at],
            kvx_recv.at[offset - 1, at],
            across(offset),
        )

    def kvs_copy(offset, at):
        there = kv.at[offset, :, half_lanes(at)]
        here = kvin.at[even, :, lanes(at)] if offset == 0 else there
        return remote(
            here, there, kvs_send.at[offset, at], kvs_recv.at[offset, at], sibling
        )

    def kv_place(at):
        return pltpu.make_async_copy(
            kvin.at[even, :, lanes(at)], kv.at[0, :, half_lanes(at)], place_sem.at[at]
        )

    def dkvs_copy(block):
        return remote(
            dkvgive.at[block],
            dkvtake.at[block],
            dkvs_send.at[block],
            dkvs_recv.at[block],
            sibling,
        )

    def dkvx_copy(offset):
        return remote(
            dkvpart.at[offset - 1],
            dkvrecv.at[offset - 1],
            dkvx_send.at[offset - 1],
            dkvx_recv.at[offset - 1],
            across(offset),
        )

    def dkv_copy(which, at):
        head = 2 * row + (even if which == 0 else 1 - even)
        return remote(
            dkvown.at[which, :, lanes(at)],
            dkvfin.at[head],
            dkv_send.at[which, at],
            dkv_recv.at[head],
            owner(core * part_size + at, line),
        )

    def dkv_start(which):
        head = 2 * row + (even if which == 0 else 1 - even)

        @pl.loop(0, part_size)
        def _(step):
            at = lax.rem(half_at + step, part_size)
            mine = (step == 0) & kv_mine

            @pl.when(mine)
            def _():
                pltpu.make_async_copy(
                    dkvown.at[which, :, lanes(at)], dkvfin.at[head], dkv_recv.at[head]
                ).start()

            @pl.when(jnp.logical_not(mine))
            def _():
                dkv_copy(which, at).start()

    def dkv_sent(which):
        @pl.loop(0, part_size)
        def _(step):
            at = lax.rem(half_at + step, part_size)

            @pl.when((step > 0) | jnp.logical_not(kv_mine))
            def _():
                dkv_copy(which, at).wait_send()

    def dkv_arrived():
        @pl.loop(0, column)
        def _(head):
            pltpu.make_async_copy(
                dkvown.at[0, :, lanes(0)], dkvfin.at[head], dkv_recv.at[head]
            ).wait()

    g_pair = (gsend, gt)
    q_pair = (qsend, qt)
    o_pair = (ot, ofin)
    dq_pair = (dqt, dqfin)

    skip_spans = spans(width, 512)
    pieces = [(lat_hbm, lat)]
    for at, size in skip_spans:
        cols = pl.ds(at, size)
        pieces.append((skipw_hbm.at[:, cols], skipw.at[:, cols]))
    pieces += [(ups_hbm, ups), (wout_hbm, wout), (win_hbm, win)]
    loads = [
        pltpu.make_async_copy(src, dst, load_sem.at[i])
        for i, (src, dst) in enumerate(pieces)
    ]
    lat_load, *skip_loads, ups_load, wout_load, win_load = loads
    for load in loads:
        load.start()

    barrier = pltpu.get_barrier_semaphore()
    peers = [owner(lax.rem(me + step, column), line) for step in range(1, column)]
    peers += [owner(index, line + 1 - 2 * even) for index in range(column)]
    peers += [across(offset) for offset in range(2, rows_k)]
    peers.append(partner)
    for peer in peers:
        pl.semaphore_signal(barrier, inc=1, device_id=peer, device_id_type=MESH)

    def skip_copy(i):
        at, size = skip_spans[i]
        cols = pl.ds(at, size)
        return remote(
            skip_send.at[:, cols],
            skip_recv.at[:, cols],
            skip_ssem.at[i],
            skip_rsem.at[i],
            partner,
        )

    lat_load.wait()
    for i, (at, size) in enumerate(skip_spans):
        skip_loads[i].wait()
        product = dot(lat[...], skipw[:, pl.ds(at, size)])
        mixed[:, pl.ds(at, size)] = product
        skip_send[:, pl.ds(at, size)] = product.astype(BF16)
        if i == 0:
            pl.semaphore_wait(barrier, len(peers))

        @pl.when(is_lower)
        def _():
            skip_copy(i).start()

    def turn(source, i):
        block = source[:, pl.ds(i * CHUNK, CHUNK)]
        flip[pl.ds(i * CHUNK, CHUNK), :] = block.astype(F32).T.astype(BF16)

    ups_load.wait()
    for i in range(width // CHUNK):
        turn(ups, i)
    wout_load.wait()
    blank = jnp.zeros((PAD, CHUNK), F32)

    @pl.loop(0, column // 2)
    def _(i):
        rows = pl.ds(pl.multiple_of(i * 2 * depth, 16), 2 * depth)
        two = dot(wout[rows, :], flip[...])
        gsend[2 * i] = jnp.concatenate([blank, two[:depth]], 0).astype(BF16)
        gsend[2 * i + 1] = jnp.concatenate([blank, two[depth:]], 0).astype(BF16)

    @pl.when(is_lower)
    def _():
        for i in range(len(skip_spans)):
            skip_copy(i).wait_send()

    row_spans = spans(tok, 32)

    @pl.when(is_upper)
    def _():
        for i in range(len(skip_spans)):
            skip_copy(i).wait_recv()
        for at, size in row_spans:
            rows = pl.ds(at, size)
            total = mixed[rows, :] + skip_recv[rows, :].astype(F32)
            mixed[rows, :] = total
            binput[rows, :] = stats(total)[0].astype(BF16)

    @pl.when(is_lower)
    def _():
        binput[...] = lat[...]

    for at, size in row_spans:
        rows = pl.ds(at, size)
        normed[rows, :] = stats(binput[rows, :].astype(F32))[0].astype(BF16)

    for i in range(width // CHUNK):
        turn(normed, i)
    win_load.wait()

    def project(part):
        rows = pl.ds(pl.multiple_of(part * head_width, 16), head_width)
        projt[rows, :] = dot(win[rows, :], flip[...])

    @pl.loop(1, 3)
    def _(part):
        project(part)

    for head in range(column):
        keys = projt[pl.ds(head_width + head * depth, depth), :]
        values = projt[pl.ds(2 * head_width + head * depth, depth), :]
        kvsend[head] = jnp.concatenate([keys, values], 0).astype(BF16)
    kv_start()
    project(0)
    for head in range(column):
        queries = projt[pl.ds(head * depth, depth), :]
        qsend[head] = jnp.concatenate([queries, blank], 0).astype(BF16)
    head_start(QUERY, *q_pair)
    head_start(GRAD, *g_pair)

    @pl.loop(0, part_size)
    def _(at):
        kv_arrived(at)
        kvs_copy(0, at).start()
        kv_place(at).start()

    for offset in range(1, rows_k):

        @pl.loop(0, part_size)
        def _(at):
            kvx_copy(offset, at).start()

    def take(block):
        @pl.loop(0, part_size)
        def _(at):
            kvx_copy(block, at).wait_recv()
            kvs_copy(block, at).start()

    def natural(block):
        lane = lax.broadcasted_iota(jnp.int32, (q_tile, padded), 1)
        for at, size in spans(span, q_tile):
            cols = pl.ds(at, size)
            keys = kv[block, :padded, cols].astype(F32).T
            values = kv[block, depth - PAD :, cols].astype(F32).T
            knat[block, cols, :] = keys.astype(BF16)
            vnat[block, cols, :] = jnp.where(lane < PAD, 1.0, values).astype(BF16)

    head_arrived(QUERY, *q_pair)
    for at, size in spans(span, q_tile):
        rows = pl.ds(at, size)
        qnat[rows, :] = qt[:, rows].astype(F32).T.astype(BF16)

    order = [0, 1, 2, 3]
    tiles = span // q_tile
    middle_tile = (tiles - 1) // 2

    def forward_rows(block, i):
        rows = pl.ds(i * q_tile, q_tile)
        scores = dot(qnat[rows, :], kv[block, :padded, :])
        top = jnp.max(scores, -1, keepdims=True)
        if block > 0:
            before = tops[block - 1, rows, :]
            top = jnp.maximum(top, before)
        tops[block, rows, :] = top
        lifted = jnp.exp2((scores - top) * rate2).astype(BF16)
        exps[block, rows, :] = lifted
        term = dot(lifted, vnat[block])
        if block > 0:
            term += oacc[rows, :] * jnp.exp2((before - top) * rate2)
        oacc[rows, :] = term

    for block in order:

        @pl.loop(0, part_size)
        def _(at):
            kvs_copy(block, at).wait_recv()
            if block == 0:
                kv_place(at).wait()

        natural(block)
        for i in range(tiles):
            forward_rows(block, i)
            if i == middle_tile and block + 1 < rows_k:
                take(block + 1)

    head_arrived(GRAD, *g_pair)
    for at, size in spans(span, q_tile):
        rows = pl.ds(at, size)
        gnat[rows, :] = gt[:, rows].astype(F32).T
        total = oacc[rows, :]
        inverse = 1.0 / total[:, :1]
        mixed_values = (total * inverse).astype(BF16).astype(F32)
        ot[:, rows] = mixed_values.T.astype(BF16)
        delta[rows, :] = jnp.sum(gnat[rows, :] * mixed_values, -1, keepdims=True)
        last = tops[order[-1], rows, :]
        for block in range(rows_k):
            lift = jnp.exp2((tops[block, rows, :] - last) * rate2)
            facs[block, rows, :] = lift * inverse
        qacc[rows, :] = jnp.zeros((size, padded), F32)
    back_start(OUT, *o_pair)

    def backward_rows(block, i):
        rows = pl.ds(i * q_tile, q_tile)
        factor = facs[block, rows, :]
        grads = gnat[rows, :] * factor
        shift = delta[rows, :] * factor
        lifted = exps[block, rows, :]
        back = dot(grads.astype(BF16), kv[block, depth - PAD :, :]) - shift
        gscore = (lifted.astype(F32) * back).astype(BF16)
        qacc[rows, :] += dot(gscore, knat[block])
        keys = dot(qt[:, rows], gscore)
        values = dot(grads.T.astype(BF16), lifted)
        if i > 0:
            keys += kvacc[:padded, :]
            values += kvacc[padded:, :]
        kvacc[:padded, :] = keys
        kvacc[padded:, :] = values

    half_span = span // 2

    def joined(which):
        cols = pl.ds(pl.multiple_of(which * half_span, CHUNK), half_span)
        keys = kvacc[:padded, cols] * scale
        values = kvacc[padded:, cols]
        middle = keys[depth - PAD :] + values[: 2 * PAD]
        return jnp.concatenate([keys[: depth - PAD], middle, values[2 * PAD :]], 0)

    def pass_on(block):
        dkvs_copy(block).wait_recv()
        total = keep[block] + dkvtake[block].astype(F32)
        dkvpart[block - 1] = total.astype(BF16)
        dkvx_copy(block).start()

    turns = [2, 3, 1, 0]
    for n, block in enumerate(turns):
        for i in range(tiles):
            backward_rows(block, i)
            if n > 0 and i == middle_tile:
                pass_on(turns[n - 1])
            if block == 0:
                rows = pl.ds(i * q_tile, q_tile)
                dqt[:, rows] = (qacc[rows, :] * scale).T.astype(BF16)
                for at in range(q_tile // CHUNK):
                    back_one(DQ, i * (q_tile // CHUNK) + at, *dq_pair)
        dkvgive[block] = joined(1 - core).astype(BF16)
        dkvs_copy(block).start()
        keep[block] = joined(core)

    dkvs_copy(0).wait_recv()
    dkvx_copy(2).wait_recv()
    total = keep[0] + dkvtake[0].astype(F32) + dkvrecv[1].astype(F32)
    dkvown[0] = total.astype(BF16)
    dkv_start(0)

    back_arrived(OUT, *o_pair)
    for head in range(column):
        rows = pl.ds(head * depth, depth)
        projt[rows, :] = ofin[head].astype(F32)[PAD:]
    attended = projt[:head_width, :].T.astype(BF16)
    for at, size in spans(width, 512):
        cols = pl.ds(at, size)
        term = dot(attended, wout[:, cols])
        outv[:, cols] = (binput[:, cols].astype(F32) + term).astype(BF16)
    out_store = pltpu.make_async_copy(outv, out_hbm, store_sem.at[0])
    out_store.start()

    for offset in (1, 3):
        dkvx_copy(offset).wait_recv()
    dkvown[1] = (dkvrecv[0].astype(F32) + dkvrecv[2].astype(F32)).astype(BF16)
    dkv_start(1)

    def back_project(part):
        rows = pl.ds(part * head_width, head_width)
        gproj[part] = projt[rows, :].T.astype(BF16)

    back_arrived(DQ, *dq_pair)
    for head in range(column):
        projt[pl.ds(head * depth, depth), :] = dqfin[head].astype(F32)[:depth]
    back_project(0)
    for at, size in spans(width, 512):
        cols = pl.ds(at, size)
        ginput[:, cols] = dot(gproj[0], win[pl.ds(0, head_width), cols])
    dkv_arrived()
    for head in range(column):
        both = dkvfin[head].astype(F32)
        projt[pl.ds(head_width + head * depth, depth), :] = both[:depth]
        projt[pl.ds(2 * head_width + head * depth, depth), :] = both[depth:]
    for part in (1, 2):
        back_project(part)
    for at, size in spans(width, 512):
        cols = pl.ds(at, size)
        ginput[:, cols] += sum(
            dot(gproj[part], win[pl.ds(part * head_width, head_width), cols])
            for part in (1, 2)
        )

    def gm_copy(i):
        rows = pl.ds(*row_spans[i])
        return remote(
            gm_send.at[rows], gm_recv.at[rows], gm_ssem.at[i], gm_rsem.at[i], partner
        )

    for i, (at, size) in enumerate(row_spans):
        rows = pl.ds(at, size)
        hat, rate = stats(binput[rows, :].astype(F32))
        grad = ups[rows, :].astype(F32) + norm_back(hat, rate, ginput[rows, :])
        ginput[rows, :] = grad

        @pl.when(is_upper)
        def _():
            hat, rate = stats(mixed[rows, :])
            gm_send[rows, :] = norm_back(hat, rate, ginput[rows, :]).astype(BF16)
            gm_copy(i).start()

    @pl.when(is_upper)
    def _():
        ginput[...] = jnp.zeros_like(ginput)
        for i in range(width // CHUNK):
            turn(gm_send, i)

    @pl.when(is_lower)
    def _():
        for i in range(len(row_spans)):
            gm_copy(i).wait_recv()
        for i in range(width // CHUNK):
            turn(gm_recv, i)

    half = width // 2

    @pl.loop(0, 2)
    def _(i):
        rows = pl.ds(pl.multiple_of(i * half, 16), half)
        gnt[rows, :] = dot(skipw[rows, :], flip[...])

    out_store.wait()
    for i in range(width // CHUNK):
        cols = pl.ds(i * CHUNK, CHUNK)
        term = ginput[:, cols] + gnt[pl.ds(i * CHUNK, CHUNK), :].T
        outv[:, cols] = term.astype(BF16)
    glat_store = pltpu.make_async_copy(outv, glat_hbm, store_sem.at[1])
    glat_store.start()

    head_sent(GRAD, *g_pair)
    head_sent(QUERY, *q_pair)
    back_sent(OUT, *o_pair)
    back_sent(DQ, *dq_pair)
    kv_sent()
    dkv_sent(0)
    dkv_sent(1)

    @pl.loop(0, part_size)
    def _(at):
        kvs_copy(0, at).wait_send()
        for offset in range(1, rows_k):
            kvx_copy(offset, at).wait_send()
            kvs_copy(offset, at).wait_send()

    dkvs_copy(0).wait_send()
    for offset in range(1, rows_k):
        dkvx_copy(offset).wait_send()
        dkvs_copy(offset).wait_send()

    @pl.when(is_upper)
    def _():
        for i in range(len(row_spans)):
            gm_copy(i).wait_send()

    glat_store.wait()


def settle(out, glat, out_hbm, glat_hbm, held, sem):
    ins = [
        pltpu.make_async_copy(out, held.at[0], sem.at[0]),
        pltpu.make_async_copy(glat, held.at[1], sem.at[1]),
    ]
    outs = [
        pltpu.make_async_copy(held.at[0], out_hbm, sem.at[2]),
        pltpu.make_async_copy(held.at[1], glat_hbm, sem.at[3]),
    ]
    for copy in ins:
        copy.start()
    for copy, onward in zip(ins, outs):
        copy.wait()
        onward.start()
    for copy in outs:
        copy.wait()


def body(rows_h, rows_k, latents, skip_weight, project_in, project_out, upstream):
    tok, width = latents.shape[1:]
    head_width = project_out.shape[1]
    column = rows_h * CORES
    depth = head_width // column
    padded = depth + PAD
    span = column * tok
    part = span // 2
    n_skip = len(spans(width, 512))
    n_rows = len(spans(tok, 32))
    wide = (tok, width)
    vmem = pltpu.VMEM
    dma = pltpu.SemaphoreType.DMA
    scratch = [
        vmem(wide, BF16),
        vmem((width, width), BF16),
        vmem((3 * head_width, width), BF16),
        vmem((head_width, width), BF16),
        vmem(wide, BF16),
        vmem(wide, BF16),
        vmem(wide, BF16),
        vmem(wide, F32),
        vmem(wide, BF16),
        vmem(wide, BF16),
        vmem((width, tok), BF16),
        vmem((3 * head_width, tok), F32),
        vmem((column, padded, tok), BF16),
        vmem((column, 2 * depth, tok), BF16),
        vmem((column, padded, tok), BF16),
        vmem((padded, span), BF16),
        vmem((padded, span), BF16),
        vmem((rows_k, 2 * depth, span), BF16),
        vmem((rows_k, span, padded), BF16),
        vmem((rows_k, span, padded), BF16),
        vmem((span, padded), BF16),
        vmem((span, padded), F32),
        vmem((rows_k, span, span), BF16),
        vmem((rows_k, span, 1), F32),
        vmem((rows_k, span, 1), F32),
        vmem((span, 1), F32),
        vmem((span, padded), F32),
        vmem((span, padded), F32),
        vmem((2 * padded, span), F32),
        vmem((padded, span), BF16),
        vmem((padded, span), BF16),
        vmem((2, 2 * depth, part), BF16),
        vmem((rows_k, 2 * depth, part), F32),
        vmem((rows_k, 2 * depth, part), BF16),
        vmem((rows_k, 2 * depth, part), BF16),
        vmem((rows_k - 1, 2 * depth, part), BF16),
        vmem((rows_k - 1, 2 * depth, part), BF16),
        vmem((2, 2 * depth, part), BF16),
        vmem((column, padded, tok), BF16),
        vmem((column, padded, tok), BF16),
        vmem((column, 2 * depth, tok), BF16),
        vmem((3, tok, head_width), BF16),
        vmem((width, tok), F32),
        vmem(wide, F32),
        vmem(wide, BF16),
        vmem(wide, BF16),
        vmem(wide, BF16),
        dma((4 + n_skip,)),
        dma((2,)),
        dma((4, column)),
        dma((4, column)),
        dma((rows_h,)),
        dma((column // 2,)),
        dma((rows_k - 1, column // 2)),
        dma((rows_k - 1, column // 2)),
        dma((rows_k, column // 2)),
        dma((rows_k, column // 2)),
        dma((column // 2,)),
        dma((rows_k,)),
        dma((rows_k,)),
        dma((2, column // 2)),
        dma((column,)),
        dma((rows_k - 1,)),
        dma((rows_k - 1,)),
        dma((n_skip,)),
        dma((n_skip,)),
        dma((n_rows,)),
        dma((n_rows,)),
    ]
    out, glat = pl.pallas_call(
        functools.partial(kernel, rows_h, rows_k),
        out_shape=[jax.ShapeDtypeStruct(wide, BF16)] * 2,
        in_specs=[pl.BlockSpec(memory_space=pl.ANY)] * 5,
        out_specs=[pl.BlockSpec(memory_space=pl.ANY)] * 2,
        scratch_shapes=scratch,
        compiler_params=pltpu.CompilerParams(
            collective_id=0, has_side_effects=True, vmem_limit_bytes=56 * 2**20
        ),
    )(latents[0], skip_weight[0], project_in[0].T, project_out[0], upstream[0])
    out, glat = pl.pallas_call(
        settle,
        out_shape=[jax.ShapeDtypeStruct(wide, BF16)] * 2,
        in_specs=[pl.BlockSpec(memory_space=pl.ANY)] * 2,
        out_specs=[pl.BlockSpec(memory_space=pl.ANY)] * 2,
        scratch_shapes=[vmem((2,) + wide, BF16), dma((4,))],
        compiler_params=pltpu.CompilerParams(vmem_limit_bytes=56 * 2**20),
    )(out, glat)
    return out[None], glat[None]


def solution(mesh):
    rows_h = HEADS // 2
    rows_k = mesh.shape["seq"] // HEADS
    return jax.shard_map(
        functools.partial(body, rows_h, rows_k),
        mesh=mesh,
        in_specs=(
            P("section", "seq", None),
            P("section", None, None),
            P("section", None, None),
            P("section", None, None),
            P("section", "seq", None),
        ),
        out_specs=(P("section", "seq", None), P("section", "seq", None)),
        check_vma=False,
    )
```

```python
import functools
import math

import jax
import jax.numpy as jnp
from jax import lax
from jax.experimental import pallas as pl
from jax.experimental.pallas import tpu as pltpu
from jax.sharding import PartitionSpec as P

HEADS = 8
EPSILON = 1e-06
CORES = 2
CHUNK = 128
PAD = 8

MESH = pl.DeviceIdType.MESH
F32 = jnp.float32
BF16 = jnp.bfloat16

GRAD, QUERY, OUT, DQ = range(4)


def dot(a, b):
    return jnp.dot(a, b, preferred_element_type=F32)


def spans(extent, width):
    return [(at, min(width, extent - at)) for at in range(0, extent, width)]


def stats(value):
    center = value - jnp.mean(value, -1, keepdims=True)
    rate = lax.rsqrt(jnp.mean(center * center, -1, keepdims=True) + EPSILON)
    return center * rate, rate


def norm_back(hat, rate, grad):
    inner = jnp.mean(grad * hat, -1, keepdims=True)
    return rate * (grad - jnp.mean(grad, -1, keepdims=True) - hat * inner)


def kernel(
    rows_h,
    rows_k,
    lat_hbm,
    skipw_hbm,
    win_hbm,
    wout_hbm,
    ups_hbm,
    out_hbm,
    glat_hbm,
    lat,
    skipw,
    win,
    wout,
    ups,
    skip_send,
    skip_recv,
    mixed,
    binput,
    normed,
    flip,
    projt,
    gsend,
    kvsend,
    qsend,
    gt,
    qt,
    kv,
    knat,
    vnat,
    qnat,
    gnat,
    exps,
    tops,
    facs,
    delta,
    oacc,
    qacc,
    kvacc,
    ot,
    dqt,
    kvin,
    keep,
    dkvgive,
    dkvtake,
    dkvpart,
    dkvrecv,
    dkvown,
    ofin,
    dqfin,
    dkvfin,
    gproj,
    gnt,
    ginput,
    gm_send,
    gm_recv,
    outv,
    load_sem,
    store_sem,
    col_send,
    col_recv,
    kv_send,
    kv_recv,
    kvx_send,
    kvx_recv,
    kvs_send,
    kvs_recv,
    place_sem,
    dkvs_send,
    dkvs_recv,
    dkv_send,
    dkv_recv,
    dkvx_send,
    dkvx_recv,
    skip_ssem,
    skip_rsem,
    gm_ssem,
    gm_rsem,
):
    sections = lax.axis_size("section")
    section = lax.axis_index("section")
    place = lax.axis_index("seq")
    row = place // (rows_k * CORES)
    line = lax.rem(place // CORES, rows_k)
    core = lax.rem(place, CORES)
    is_upper = section >= sections // 2
    is_lower = jnp.logical_not(is_upper)
    column = rows_h * CORES
    part_size = column // 2
    me = row * CORES + core
    even = lax.rem(line, 2)
    pair = line // 2
    own_head = 2 * row + even
    query_line = 2 * pair + core

    tok, width = lat.shape
    head_width = wout.shape[0]
    depth = head_width // column
    padded = depth + PAD
    span = column * CHUNK
    scale = 1.0 / math.sqrt(depth)
    rate2 = scale * math.log2(math.e)
    q_tile = 256

    def device(at_row, at_line, at_core):
        return {
            "section": section,
            "seq": (at_row * rows_k + at_line) * CORES + at_core,
        }

    def owner(index, at_line):
        return device(index // CORES, at_line, lax.rem(index, CORES))

    def across(offset):
        there = (line, line + 1 - 2 * even, lax.rem(line + 2, rows_k), rows_k - 1 - line)[offset]
        return device(row, there, core)

    sibling = device(row, line, 1 - core)
    partner = {"section": sections - 1 - section, "seq": place}

    def remote(src, dst, send, recv, device):
        return pltpu.make_async_remote_copy(
            src_ref=src,
            dst_ref=dst,
            send_sem=send,
            recv_sem=recv,
            device_id=device,
            device_id_type=MESH,
        )

    def lanes(index):
        return pl.ds(pl.multiple_of(index * CHUNK, CHUNK), CHUNK)

    def head_copy(kind, head, src, dst):
        there = device(head // 2, 2 * pair + lax.rem(head, 2), even)
        return remote(
            src.at[head],
            dst.at[:, lanes(me)],
            col_send.at[kind, head],
            col_recv.at[kind, me],
            there,
        )

    def back_copy(kind, index, src, dst):
        return remote(
            src.at[:, lanes(index)],
            dst.at[own_head],
            col_send.at[kind, index],
            col_recv.at[kind, own_head],
            owner(index, query_line),
        )

    def head_start(kind, src, dst):
        @pl.loop(0, column)
        def _(step):
            head = lax.rem(own_head + step, column)
            mine = (step == 0) & (even == core)

            @pl.when(mine)
            def _():
                pltpu.make_async_copy(
                    src.at[head], dst.at[:, lanes(me)], col_recv.at[kind, me]
                ).start()

            @pl.when(jnp.logical_not(mine))
            def _():
                head_copy(kind, head, src, dst).start()

    def head_arrived(kind, src, dst):
        @pl.loop(0, column)
        def _(index):
            pltpu.make_async_copy(
                src.at[0], dst.at[:, lanes(index)], col_recv.at[kind, index]
            ).wait()

    def head_sent(kind, src, dst):
        @pl.loop(0, column)
        def _(step):
            head = lax.rem(own_head + step, column)

            @pl.when((step > 0) | (even != core))
            def _():
                head_copy(kind, head, src, dst).wait_send()

    def back_one(kind, index, src, dst):
        mine = (index == me) & (even == core)

        @pl.when(mine)
        def _():
            pltpu.make_async_copy(
                src.at[:, lanes(index)], dst.at[own_head], col_recv.at[kind, own_head]
            ).start()

        @pl.when(jnp.logical_not(mine))
        def _():
            back_copy(kind, index, src, dst).start()

    def back_start(kind, src, dst):
        @pl.loop(0, column)
        def _(index):
            back_one(kind, index, src, dst)

    def back_arrived(kind, src, dst):
        @pl.loop(0, column)
        def _(head):
            pltpu.make_async_copy(
                src.at[:, lanes(0)], dst.at[head], col_recv.at[kind, head]
            ).wait()

    def back_sent(kind, src, dst):
        @pl.loop(0, column)
        def _(step):
            index = lax.rem(me + step, column)

            @pl.when((step > 0) | (even != core))
            def _():
                back_copy(kind, index, src, dst).wait_send()

    half_core = me // part_size
    half_at = lax.rem(me, part_size)
    kv_mine = half_core == core

    def kv_copy(step):
        at_row = lax.rem(row + step, rows_h)
        return remote(
            kvsend.at[pl.ds(2 * at_row, 2)],
            kvin.at[:, :, lanes(half_at)],
            kv_send.at[step],
            kv_recv.at[half_at],
            device(at_row, line, half_core),
        )

    def kv_own():
        return pltpu.make_async_copy(
            kvsend.at[pl.ds(2 * row, 2)],
            kvin.at[:, :, lanes(half_at)],
            kv_recv.at[half_at],
        )

    def kv_start():
        @pl.when(kv_mine)
        def _():
            kv_own().start()

        @pl.when(jnp.logical_not(kv_mine))
        def _():
            kv_copy(0).start()

        @pl.loop(1, rows_h)
        def _(step):
            kv_copy(step).start()

    def kv_arrived(at):
        pltpu.make_async_copy(
            kvsend.at[pl.ds(0, 2)], kvin.at[:, :, lanes(at)], kv_recv.at[at]
        ).wait()

    def kv_sent():
        @pl.when(jnp.logical_not(kv_mine))
        def _():
            kv_copy(0).wait_send()

        @pl.loop(1, rows_h)
        def _(step):
            kv_copy(step).wait_send()

    def half_lanes(at):
        return lanes(core * part_size + at)

    def kvx_copy(offset, at):
        head = even if offset == 2 else 1 - even
        return remote(
            kvin.at[head, :, lanes(at)],
            kv.at[offset, :, half_lanes(at)],
            kvx_send.at[offset - 1, at],
            kvx_recv.at[offset - 1, at],
            across(offset),
        )

    def kvs_copy(offset, at):
        there = kv.at[offset, :, half_lanes(at)]
        here = kvin.at[even, :, lanes(at)] if offset == 0 else there
        return remote(
            here, there, kvs_send.at[offset, at], kvs_recv.at[offset, at], sibling
        )

    def kv_place(at):
        return pltpu.make_async_copy(
            kvin.at[even, :, lanes(at)], kv.at[0, :, half_lanes(at)], place_sem.at[at]
        )

    def dkvs_copy(block):
        return remote(
            dkvgive.at[block],
            dkvtake.at[block],
            dkvs_send.at[block],
            dkvs_recv.at[block],
            sibling,
        )

    def dkvx_copy(offset):
        return remote(
            dkvpart.at[offset - 1],
            dkvrecv.at[offset - 1],
            dkvx_send.at[offset - 1],
            dkvx_recv.at[offset - 1],
            across(offset),
        )

    def dkv_copy(which, at):
        head = 2 * row + (even if which == 0 else 1 - even)
        return remote(
            dkvown.at[which, :, lanes(at)],
            dkvfin.at[head],
            dkv_send.at[which, at],
            dkv_recv.at[head],
            owner(core * part_size + at, line),
        )

    def dkv_start(which):
        head = 2 * row + (even if which == 0 else 1 - even)

        @pl.loop(0, part_size)
        def _(step):
            at = lax.rem(half_at + step, part_size)
            mine = (step == 0) & kv_mine

            @pl.when(mine)
            def _():
                pltpu.make_async_copy(
                    dkvown.at[which, :, lanes(at)], dkvfin.at[head], dkv_recv.at[head]
                ).start()

            @pl.when(jnp.logical_not(mine))
            def _():
                dkv_copy(which, at).start()

    def dkv_sent(which):
        @pl.loop(0, part_size)
        def _(step):
            at = lax.rem(half_at + step, part_size)

            @pl.when((step > 0) | jnp.logical_not(kv_mine))
            def _():
                dkv_copy(which, at).wait_send()

    def dkv_arrived():
        @pl.loop(0, column)
        def _(head):
            pltpu.make_async_copy(
                dkvown.at[0, :, lanes(0)], dkvfin.at[head], dkv_recv.at[head]
            ).wait()

    g_pair = (gsend, gt)
    q_pair = (qsend, qt)
    o_pair = (ot, ofin)
    dq_pair = (dqt, dqfin)

    skip_spans = spans(width, 512)
    pieces = [(lat_hbm, lat)]
    for at, size in skip_spans:
        cols = pl.ds(at, size)
        pieces.append((skipw_hbm.at[:, cols], skipw.at[:, cols]))
    pieces += [(ups_hbm, ups), (wout_hbm, wout), (win_hbm, win)]
    loads = [
        pltpu.make_async_copy(src, dst, load_sem.at[i])
        for i, (src, dst) in enumerate(pieces)
    ]
    lat_load, *skip_loads, ups_load, wout_load, win_load = loads
    for load in loads:
        load.start()

    barrier = pltpu.get_barrier_semaphore()
    peers = [owner(lax.rem(me + step, column), line) for step in range(1, column)]
    peers += [owner(index, line + 1 - 2 * even) for index in range(column)]
    peers += [across(offset) for offset in range(2, rows_k)]
    peers.append(partner)
    for peer in peers:
        pl.semaphore_signal(barrier, inc=1, device_id=peer, device_id_type=MESH)

    def skip_copy(i):
        at, size = skip_spans[i]
        cols = pl.ds(at, size)
        return remote(
            skip_send.at[:, cols],
            skip_recv.at[:, cols],
            skip_ssem.at[i],
            skip_rsem.at[i],
            partner,
        )

    lat_load.wait()
    for i, (at, size) in enumerate(skip_spans):
        skip_loads[i].wait()
        product = dot(lat[...], skipw[:, pl.ds(at, size)])
        mixed[:, pl.ds(at, size)] = product
        skip_send[:, pl.ds(at, size)] = product.astype(BF16)
        if i == 0:
            pl.semaphore_wait(barrier, len(peers))

        @pl.when(is_lower)
        def _():
            skip_copy(i).start()

    def turn(source, i):
        block = source[:, pl.ds(i * CHUNK, CHUNK)]
        flip[pl.ds(i * CHUNK, CHUNK), :] = block.astype(F32).T.astype(BF16)

    ups_load.wait()
    for i in range(width // CHUNK):
        turn(ups, i)
    wout_load.wait()
    blank = jnp.zeros((PAD, CHUNK), F32)

    @pl.loop(0, column // 2)
    def _(i):
        rows = pl.ds(pl.multiple_of(i * 2 * depth, 16), 2 * depth)
        two = dot(wout[rows, :], flip[...])
        gsend[2 * i] = jnp.concatenate([blank, two[:depth]], 0).astype(BF16)
        gsend[2 * i + 1] = jnp.concatenate([blank, two[depth:]], 0).astype(BF16)

    @pl.when(is_lower)
    def _():
        for i in range(len(skip_spans)):
            skip_copy(i).wait_send()

    row_spans = spans(tok, 32)

    @pl.when(is_upper)
    def _():
        for i in range(len(skip_spans)):
            skip_copy(i).wait_recv()
        for at, size in row_spans:
            rows = pl.ds(at, size)
            total = mixed[rows, :] + skip_recv[rows, :].astype(F32)
            mixed[rows, :] = total
            binput[rows, :] = stats(total)[0].astype(BF16)

    @pl.when(is_lower)
    def _():
        binput[...] = lat[...]

    for at, size in row_spans:
        rows = pl.ds(at, size)
        normed[rows, :] = stats(binput[rows, :].astype(F32))[0].astype(BF16)

    for i in range(width // CHUNK):
        turn(normed, i)
    win_load.wait()

    def project(part):
        rows = pl.ds(pl.multiple_of(part * head_width, 16), head_width)
        projt[rows, :] = dot(win[rows, :], flip[...])

    @pl.loop(1, 3)
    def _(part):
        project(part)

    for head in range(column):
        keys = projt[pl.ds(head_width + head * depth, depth), :]
        values = projt[pl.ds(2 * head_width + head * depth, depth), :]
        kvsend[head] = jnp.concatenate([keys, values], 0).astype(BF16)
    kv_start()
    project(0)
    for head in range(column):
        queries = projt[pl.ds(head * depth, depth), :]
        qsend[head] = jnp.concatenate([queries, blank], 0).astype(BF16)
    head_start(QUERY, *q_pair)
    head_start(GRAD, *g_pair)

    @pl.loop(0, part_size)
    def _(at):
        kv_arrived(at)
        kvs_copy(0, at).start()
        kv_place(at).start()

    for offset in range(1, rows_k):

        @pl.loop(0, part_size)
        def _(at):
            kvx_copy(offset, at).start()

    def take(block):
        @pl.loop(0, part_size)
        def _(at):
            kvx_copy(block, at).wait_recv()
            kvs_copy(block, at).start()

    def natural(block):
        lane = lax.broadcasted_iota(jnp.int32, (q_tile, padded), 1)
        for at, size in spans(span, q_tile):
            cols = pl.ds(at, size)
            keys = kv[block, :padded, cols].astype(F32).T
            values = kv[block, depth - PAD :, cols].astype(F32).T
            knat[block, cols, :] = keys.astype(BF16)
            vnat[block, cols, :] = jnp.where(lane < PAD, 1.0, values).astype(BF16)

    head_arrived(QUERY, *q_pair)
    for at, size in spans(span, q_tile):
        rows = pl.ds(at, size)
        qnat[rows, :] = qt[:, rows].astype(F32).T.astype(BF16)

    order = [0, 1, 3, 2]
    tiles = span // q_tile
    middle_tile = (tiles - 1) // 2

    def forward_rows(block, i):
        rows = pl.ds(i * q_tile, q_tile)
        scores = dot(qnat[rows, :], kv[block, :padded, :])
        top = jnp.max(scores, -1, keepdims=True)
        if block > 0:
            before = tops[order[order.index(block) - 1], rows, :]
            top = jnp.maximum(top, before)
        tops[block, rows, :] = top
        lifted = jnp.exp2((scores - top) * rate2).astype(BF16)
        exps[block, rows, :] = lifted
        term = dot(lifted, vnat[block])
        if block > 0:
            term += oacc[rows, :] * jnp.exp2((before - top) * rate2)
        oacc[rows, :] = term

    for block in order:

        @pl.loop(0, part_size)
        def _(at):
            kvs_copy(block, at).wait_recv()
            if block == 0:
                kv_place(at).wait()

        natural(block)
        for i in range(tiles):
            forward_rows(block, i)
            if i == middle_tile and block != order[-1]:
                take(order[order.index(block) + 1])

    head_arrived(GRAD, *g_pair)
    for at, size in spans(span, q_tile):
        rows = pl.ds(at, size)
        gnat[rows, :] = gt[:, rows].astype(F32).T
        total = oacc[rows, :]
        inverse = 1.0 / total[:, :1]
        mixed_values = (total * inverse).astype(BF16).astype(F32)
        ot[:, rows] = mixed_values.T.astype(BF16)
        delta[rows, :] = jnp.sum(gnat[rows, :] * mixed_values, -1, keepdims=True)
        last = tops[order[-1], rows, :]
        for block in range(rows_k):
            lift = jnp.exp2((tops[block, rows, :] - last) * rate2)
            facs[block, rows, :] = lift * inverse
        qacc[rows, :] = jnp.zeros((size, padded), F32)
    back_start(OUT, *o_pair)

    def backward_rows(block, i):
        rows = pl.ds(i * q_tile, q_tile)
        factor = facs[block, rows, :]
        grads = gnat[rows, :] * factor
        shift = delta[rows, :] * factor
        lifted = exps[block, rows, :]
        back = dot(grads.astype(BF16), kv[block, depth - PAD :, :]) - shift
        gscore = (lifted.astype(F32) * back).astype(BF16)
        qacc[rows, :] += dot(gscore, knat[block])
        keys = dot(qt[:, rows], gscore)
        values = dot(grads.T.astype(BF16), lifted)
        if i > 0:
            keys += kvacc[:padded, :]
            values += kvacc[padded:, :]
        kvacc[:padded, :] = keys
        kvacc[padded:, :] = values

    half_span = span // 2

    def joined(which):
        cols = pl.ds(pl.multiple_of(which * half_span, CHUNK), half_span)
        keys = kvacc[:padded, cols] * scale
        values = kvacc[padded:, cols]
        middle = keys[depth - PAD :] + values[: 2 * PAD]
        return jnp.concatenate([keys[: depth - PAD], middle, values[2 * PAD :]], 0)

    def pass_on(block):
        dkvs_copy(block).wait_recv()
        total = keep[block] + dkvtake[block].astype(F32)
        dkvpart[block - 1] = total.astype(BF16)
        dkvx_copy(block).start()

    turns = [2, 3, 1, 0]
    for n, block in enumerate(turns):
        for i in range(tiles):
            backward_rows(block, i)
            if n > 0 and i == middle_tile:
                pass_on(turns[n - 1])
            if block == 0:
                rows = pl.ds(i * q_tile, q_tile)
                dqt[:, rows] = (qacc[rows, :] * scale).T.astype(BF16)
                for at in range(q_tile // CHUNK):
                    back_one(DQ, i * (q_tile // CHUNK) + at, *dq_pair)
        dkvgive[block] = joined(1 - core).astype(BF16)
        dkvs_copy(block).start()
        keep[block] = joined(core)

    dkvs_copy(0).wait_recv()
    dkvx_copy(2).wait_recv()
    total = keep[0] + dkvtake[0].astype(F32) + dkvrecv[1].astype(F32)
    dkvown[0] = total.astype(BF16)
    dkv_start(0)

    back_arrived(OUT, *o_pair)
    for head in range(column):
        rows = pl.ds(head * depth, depth)
        projt[rows, :] = ofin[head].astype(F32)[PAD:]
    attended = projt[:head_width, :].T.astype(BF16)
    for at, size in spans(width, 512):
        cols = pl.ds(at, size)
        term = dot(attended, wout[:, cols])
        outv[:, cols] = (binput[:, cols].astype(F32) + term).astype(BF16)
    out_store = pltpu.make_async_copy(outv, out_hbm, store_sem.at[0])
    out_store.start()

    for offset in (1, 3):
        dkvx_copy(offset).wait_recv()
    dkvown[1] = (dkvrecv[0].astype(F32) + dkvrecv[2].astype(F32)).astype(BF16)
    dkv_start(1)

    def back_project(part):
        rows = pl.ds(part * head_width, head_width)
        gproj[part] = projt[rows, :].T.astype(BF16)

    back_arrived(DQ, *dq_pair)
    for head in range(column):
        projt[pl.ds(head * depth, depth), :] = dqfin[head].astype(F32)[:depth]
    back_project(0)
    for at, size in spans(width, 512):
        cols = pl.ds(at, size)
        ginput[:, cols] = dot(gproj[0], win[pl.ds(0, head_width), cols])
    dkv_arrived()
    for head in range(column):
        both = dkvfin[head].astype(F32)
        projt[pl.ds(head_width + head * depth, depth), :] = both[:depth]
        projt[pl.ds(2 * head_width + head * depth, depth), :] = both[depth:]
    for part in (1, 2):
        back_project(part)
    for at, size in spans(width, 512):
        cols = pl.ds(at, size)
        ginput[:, cols] += sum(
            dot(gproj[part], win[pl.ds(part * head_width, head_width), cols])
            for part in (1, 2)
        )

    def gm_copy(i):
        rows = pl.ds(*row_spans[i])
        return remote(
            gm_send.at[rows], gm_recv.at[rows], gm_ssem.at[i], gm_rsem.at[i], partner
        )

    for i, (at, size) in enumerate(row_spans):
        rows = pl.ds(at, size)
        hat, rate = stats(binput[rows, :].astype(F32))
        grad = ups[rows, :].astype(F32) + norm_back(hat, rate, ginput[rows, :])
        ginput[rows, :] = grad

        @pl.when(is_upper)
        def _():
            hat, rate = stats(mixed[rows, :])
            gm_send[rows, :] = norm_back(hat, rate, ginput[rows, :]).astype(BF16)
            gm_copy(i).start()

    @pl.when(is_upper)
    def _():
        ginput[...] = jnp.zeros_like(ginput)
        for i in range(width // CHUNK):
            turn(gm_send, i)

    @pl.when(is_lower)
    def _():
        for i in range(len(row_spans)):
            gm_copy(i).wait_recv()
        for i in range(width // CHUNK):
            turn(gm_recv, i)

    half = width // 2

    @pl.loop(0, 2)
    def _(i):
        rows = pl.ds(pl.multiple_of(i * half, 16), half)
        gnt[rows, :] = dot(skipw[rows, :], flip[...])

    out_store.wait()
    for i in range(width // CHUNK):
        cols = pl.ds(i * CHUNK, CHUNK)
        term = ginput[:, cols] + gnt[pl.ds(i * CHUNK, CHUNK), :].T
        outv[:, cols] = term.astype(BF16)
    glat_store = pltpu.make_async_copy(outv, glat_hbm, store_sem.at[1])
    glat_store.start()

    head_sent(GRAD, *g_pair)
    head_sent(QUERY, *q_pair)
    back_sent(OUT, *o_pair)
    back_sent(DQ, *dq_pair)
    kv_sent()
    dkv_sent(0)
    dkv_sent(1)

    @pl.loop(0, part_size)
    def _(at):
        kvs_copy(0, at).wait_send()
        for offset in range(1, rows_k):
            kvx_copy(offset, at).wait_send()
            kvs_copy(offset, at).wait_send()

    dkvs_copy(0).wait_send()
    for offset in range(1, rows_k):
        dkvx_copy(offset).wait_send()
        dkvs_copy(offset).wait_send()

    @pl.when(is_upper)
    def _():
        for i in range(len(row_spans)):
            gm_copy(i).wait_send()

    glat_store.wait()


def settle(out, glat, out_hbm, glat_hbm, held, sem):
    ins = [
        pltpu.make_async_copy(out, held.at[0], sem.at[0]),
        pltpu.make_async_copy(glat, held.at[1], sem.at[1]),
    ]
    outs = [
        pltpu.make_async_copy(held.at[0], out_hbm, sem.at[2]),
        pltpu.make_async_copy(held.at[1], glat_hbm, sem.at[3]),
    ]
    for copy in ins:
        copy.start()
    for copy, onward in zip(ins, outs):
        copy.wait()
        onward.start()
    for copy in outs:
        copy.wait()


def body(rows_h, rows_k, latents, skip_weight, project_in, project_out, upstream):
    tok, width = latents.shape[1:]
    head_width = project_out.shape[1]
    column = rows_h * CORES
    depth = head_width // column
    padded = depth + PAD
    span = column * tok
    part = span // 2
    n_skip = len(spans(width, 512))
    n_rows = len(spans(tok, 32))
    wide = (tok, width)
    vmem = pltpu.VMEM
    dma = pltpu.SemaphoreType.DMA
    scratch = [
        vmem(wide, BF16),
        vmem((width, width), BF16),
        vmem((3 * head_width, width), BF16),
        vmem((head_width, width), BF16),
        vmem(wide, BF16),
        vmem(wide, BF16),
        vmem(wide, BF16),
        vmem(wide, F32),
        vmem(wide, BF16),
        vmem(wide, BF16),
        vmem((width, tok), BF16),
        vmem((3 * head_width, tok), F32),
        vmem((column, padded, tok), BF16),
        vmem((column, 2 * depth, tok), BF16),
        vmem((column, padded, tok), BF16),
        vmem((padded, span), BF16),
        vmem((padded, span), BF16),
        vmem((rows_k, 2 * depth, span), BF16),
        vmem((rows_k, span, padded), BF16),
        vmem((rows_k, span, padded), BF16),
        vmem((span, padded), BF16),
        vmem((span, padded), F32),
        vmem((rows_k, span, span), BF16),
        vmem((rows_k, span, 1), F32),
        vmem((rows_k, span, 1), F32),
        vmem((span, 1), F32),
        vmem((span, padded), F32),
        vmem((span, padded), F32),
        vmem((2 * padded, span), F32),
        vmem((padded, span), BF16),
        vmem((padded, span), BF16),
        vmem((2, 2 * depth, part), BF16),
        vmem((rows_k, 2 * depth, part), F32),
        vmem((rows_k, 2 * depth, part), BF16),
        vmem((rows_k, 2 * depth, part), BF16),
        vmem((rows_k - 1, 2 * depth, part), BF16),
        vmem((rows_k - 1, 2 * depth, part), BF16),
        vmem((2, 2 * depth, part), BF16),
        vmem((column, padded, tok), BF16),
        vmem((column, padded, tok), BF16),
        vmem((column, 2 * depth, tok), BF16),
        vmem((3, tok, head_width), BF16),
        vmem((width, tok), F32),
        vmem(wide, F32),
        vmem(wide, BF16),
        vmem(wide, BF16),
        vmem(wide, BF16),
        dma((4 + n_skip,)),
        dma((2,)),
        dma((4, column)),
        dma((4, column)),
        dma((rows_h,)),
        dma((column // 2,)),
        dma((rows_k - 1, column // 2)),
        dma((rows_k - 1, column // 2)),
        dma((rows_k, column // 2)),
        dma((rows_k, column // 2)),
        dma((column // 2,)),
        dma((rows_k,)),
        dma((rows_k,)),
        dma((2, column // 2)),
        dma((column,)),
        dma((rows_k - 1,)),
        dma((rows_k - 1,)),
        dma((n_skip,)),
        dma((n_skip,)),
        dma((n_rows,)),
        dma((n_rows,)),
    ]
    out, glat = pl.pallas_call(
        functools.partial(kernel, rows_h, rows_k),
        out_shape=[jax.ShapeDtypeStruct(wide, BF16)] * 2,
        in_specs=[pl.BlockSpec(memory_space=pl.ANY)] * 5,
        out_specs=[pl.BlockSpec(memory_space=pl.ANY)] * 2,
        scratch_shapes=scratch,
        compiler_params=pltpu.CompilerParams(
            collective_id=0, has_side_effects=True, vmem_limit_bytes=56 * 2**20
        ),
    )(latents[0], skip_weight[0], project_in[0].T, project_out[0], upstream[0])
    out, glat = pl.pallas_call(
        settle,
        out_shape=[jax.ShapeDtypeStruct(wide, BF16)] * 2,
        in_specs=[pl.BlockSpec(memory_space=pl.ANY)] * 2,
        out_specs=[pl.BlockSpec(memory_space=pl.ANY)] * 2,
        scratch_shapes=[vmem((2,) + wide, BF16), dma((4,))],
        compiler_params=pltpu.CompilerParams(vmem_limit_bytes=56 * 2**20),
    )(out, glat)
    return out[None], glat[None]


def solution(mesh):
    rows_h = HEADS // 2
    rows_k = mesh.shape["seq"] // HEADS
    return jax.shard_map(
        functools.partial(body, rows_h, rows_k),
        mesh=mesh,
        in_specs=(
            P("section", "seq", None),
            P("section", None, None),
            P("section", None, None),
            P("section", None, None),
            P("section", "seq", None),
        ),
        out_specs=(P("section", "seq", None), P("section", "seq", None)),
        check_vma=False,
    )
```

```python
import functools
import math

import jax
import jax.numpy as jnp
from jax import lax
from jax.experimental import pallas as pl
from jax.experimental.pallas import tpu as pltpu
from jax.sharding import PartitionSpec as P

HEADS = 8
EPSILON = 1e-06
CORES = 2
CHUNK = 128
PAD = 8

MESH = pl.DeviceIdType.MESH
F32 = jnp.float32
BF16 = jnp.bfloat16

GRAD, QUERY, OUT, DQ = range(4)


def dot(a, b):
    return jnp.dot(a, b, preferred_element_type=F32)


def spans(extent, width):
    return [(at, min(width, extent - at)) for at in range(0, extent, width)]


def stats(value):
    center = value - jnp.mean(value, -1, keepdims=True)
    rate = lax.rsqrt(jnp.mean(center * center, -1, keepdims=True) + EPSILON)
    return center * rate, rate


def norm_back(hat, rate, grad):
    inner = jnp.mean(grad * hat, -1, keepdims=True)
    return rate * (grad - jnp.mean(grad, -1, keepdims=True) - hat * inner)


def kernel(
    rows_h,
    rows_k,
    lat_hbm,
    skipw_hbm,
    win_hbm,
    wout_hbm,
    ups_hbm,
    out_hbm,
    glat_hbm,
    lat,
    skipw,
    win,
    wout,
    ups,
    skip_send,
    skip_recv,
    mixed,
    binput,
    normed,
    flip,
    projt,
    gsend,
    kvsend,
    qsend,
    gt,
    qt,
    kv,
    knat,
    vnat,
    qnat,
    gnat,
    exps,
    tops,
    facs,
    delta,
    oacc,
    qacc,
    kvacc,
    ot,
    dqt,
    kvin,
    keep,
    dkvgive,
    dkvtake,
    dkvpart,
    dkvrecv,
    dkvown,
    ofin,
    dqfin,
    dkvfin,
    gproj,
    gnt,
    ginput,
    gm_send,
    gm_recv,
    outv,
    load_sem,
    store_sem,
    col_send,
    col_recv,
    kv_send,
    kv_recv,
    kvx_send,
    kvx_recv,
    kvs_send,
    kvs_recv,
    place_sem,
    dkvs_send,
    dkvs_recv,
    dkv_send,
    dkv_recv,
    dkvx_send,
    dkvx_recv,
    skip_ssem,
    skip_rsem,
    gm_ssem,
    gm_rsem,
):
    sections = lax.axis_size("section")
    section = lax.axis_index("section")
    place = lax.axis_index("seq")
    row = place // (rows_k * CORES)
    line = lax.rem(place // CORES, rows_k)
    core = lax.rem(place, CORES)
    is_upper = section >= sections // 2
    is_lower = jnp.logical_not(is_upper)
    column = rows_h * CORES
    part_size = column // 2
    me = row * CORES + core
    even = lax.rem(line, 2)
    pair = line // 2
    own_head = 2 * row + even
    query_line = 2 * pair + core

    tok, width = lat.shape
    head_width = wout.shape[0]
    depth = head_width // column
    padded = depth + PAD
    span = column * CHUNK
    scale = 1.0 / math.sqrt(depth)
    rate2 = scale * math.log2(math.e)
    q_tile = 256

    def device(at_row, at_line, at_core):
        return {
            "section": section,
            "seq": (at_row * rows_k + at_line) * CORES + at_core,
        }

    def owner(index, at_line):
        return device(index // CORES, at_line, lax.rem(index, CORES))

    def across(offset):
        there = (line, line + 1 - 2 * even, lax.rem(line + 2, rows_k), rows_k - 1 - line)[offset]
        return device(row, there, core)

    sibling = device(row, line, 1 - core)
    partner = {"section": sections - 1 - section, "seq": place}

    def remote(src, dst, send, recv, device):
        return pltpu.make_async_remote_copy(
            src_ref=src,
            dst_ref=dst,
            send_sem=send,
            recv_sem=recv,
            device_id=device,
            device_id_type=MESH,
        )

    def lanes(index):
        return pl.ds(pl.multiple_of(index * CHUNK, CHUNK), CHUNK)

    def head_copy(kind, head, src, dst):
        there = device(head // 2, 2 * pair + lax.rem(head, 2), even)
        return remote(
            src.at[head],
            dst.at[:, lanes(me)],
            col_send.at[kind, head],
            col_recv.at[kind, me],
            there,
        )

    def back_copy(kind, index, src, dst):
        return remote(
            src.at[:, lanes(index)],
            dst.at[own_head],
            col_send.at[kind, index],
            col_recv.at[kind, own_head],
            owner(index, query_line),
        )

    def head_start(kind, src, dst):
        @pl.loop(0, column)
        def _(step):
            head = lax.rem(own_head + step, column)
            mine = (step == 0) & (even == core)

            @pl.when(mine)
            def _():
                pltpu.make_async_copy(
                    src.at[head], dst.at[:, lanes(me)], col_recv.at[kind, me]
                ).start()

            @pl.when(jnp.logical_not(mine))
            def _():
                head_copy(kind, head, src, dst).start()

    def head_arrived(kind, src, dst):
        @pl.loop(0, column)
        def _(index):
            pltpu.make_async_copy(
                src.at[0], dst.at[:, lanes(index)], col_recv.at[kind, index]
            ).wait()

    def head_sent(kind, src, dst):
        @pl.loop(0, column)
        def _(step):
            head = lax.rem(own_head + step, column)

            @pl.when((step > 0) | (even != core))
            def _():
                head_copy(kind, head, src, dst).wait_send()

    def back_one(kind, index, src, dst):
        mine = (index == me) & (even == core)

        @pl.when(mine)
        def _():
            pltpu.make_async_copy(
                src.at[:, lanes(index)], dst.at[own_head], col_recv.at[kind, own_head]
            ).start()

        @pl.when(jnp.logical_not(mine))
        def _():
            back_copy(kind, index, src, dst).start()

    def back_start(kind, src, dst):
        @pl.loop(0, column)
        def _(index):
            back_one(kind, index, src, dst)

    def back_arrived(kind, src, dst):
        @pl.loop(0, column)
        def _(head):
            pltpu.make_async_copy(
                src.at[:, lanes(0)], dst.at[head], col_recv.at[kind, head]
            ).wait()

    def back_sent(kind, src, dst):
        @pl.loop(0, column)
        def _(step):
            index = lax.rem(me + step, column)

            @pl.when((step > 0) | (even != core))
            def _():
                back_copy(kind, index, src, dst).wait_send()

    half_core = me // part_size
    half_at = lax.rem(me, part_size)
    kv_mine = half_core == core

    def kv_copy(step):
        at_row = lax.rem(row + step, rows_h)
        return remote(
            kvsend.at[pl.ds(2 * at_row, 2)],
            kvin.at[:, :, lanes(half_at)],
            kv_send.at[step],
            kv_recv.at[half_at],
            device(at_row, line, half_core),
        )

    def kv_own():
        return pltpu.make_async_copy(
            kvsend.at[pl.ds(2 * row, 2)],
            kvin.at[:, :, lanes(half_at)],
            kv_recv.at[half_at],
        )

    def kv_start():
        @pl.when(kv_mine)
        def _():
            kv_own().start()

        @pl.when(jnp.logical_not(kv_mine))
        def _():
            kv_copy(0).start()

        @pl.loop(1, rows_h)
        def _(step):
            kv_copy(step).start()

    def kv_arrived(at):
        pltpu.make_async_copy(
            kvsend.at[pl.ds(0, 2)], kvin.at[:, :, lanes(at)], kv_recv.at[at]
        ).wait()

    def kv_sent():
        @pl.when(jnp.logical_not(kv_mine))
        def _():
            kv_copy(0).wait_send()

        @pl.loop(1, rows_h)
        def _(step):
            kv_copy(step).wait_send()

    def half_lanes(at):
        return lanes(core * part_size + at)

    def kvx_copy(offset, at):
        head = even if offset == 2 else 1 - even
        return remote(
            kvin.at[head, :, lanes(at)],
            kv.at[offset, :, half_lanes(at)],
            kvx_send.at[offset - 1, at],
            kvx_recv.at[offset - 1, at],
            across(offset),
        )

    def kvs_copy(offset, at):
        there = kv.at[offset, :, half_lanes(at)]
        here = kvin.at[even, :, lanes(at)] if offset == 0 else there
        return remote(
            here, there, kvs_send.at[offset, at], kvs_recv.at[offset, at], sibling
        )

    def kv_place(at):
        return pltpu.make_async_copy(
            kvin.at[even, :, lanes(at)], kv.at[0, :, half_lanes(at)], place_sem.at[at]
        )

    def dkvs_copy(block):
        return remote(
            dkvgive.at[block],
            dkvtake.at[block],
            dkvs_send.at[block],
            dkvs_recv.at[block],
            sibling,
        )

    def dkvx_copy(offset):
        return remote(
            dkvpart.at[offset - 1],
            dkvrecv.at[offset - 1],
            dkvx_send.at[offset - 1],
            dkvx_recv.at[offset - 1],
            across(offset),
        )

    def dkv_copy(which, at):
        head = 2 * row + (even if which == 0 else 1 - even)
        return remote(
            dkvown.at[which, :, lanes(at)],
            dkvfin.at[head],
            dkv_send.at[which, at],
            dkv_recv.at[head],
            owner(core * part_size + at, line),
        )

    def dkv_start(which):
        head = 2 * row + (even if which == 0 else 1 - even)

        @pl.loop(0, part_size)
        def _(step):
            at = lax.rem(half_at + step, part_size)
            mine = (step == 0) & kv_mine

            @pl.when(mine)
            def _():
                pltpu.make_async_copy(
                    dkvown.at[which, :, lanes(at)], dkvfin.at[head], dkv_recv.at[head]
                ).start()

            @pl.when(jnp.logical_not(mine))
            def _():
                dkv_copy(which, at).start()

    def dkv_sent(which):
        @pl.loop(0, part_size)
        def _(step):
            at = lax.rem(half_at + step, part_size)

            @pl.when((step > 0) | jnp.logical_not(kv_mine))
            def _():
                dkv_copy(which, at).wait_send()

    def dkv_arrived():
        @pl.loop(0, column)
        def _(head):
            pltpu.make_async_copy(
                dkvown.at[0, :, lanes(0)], dkvfin.at[head], dkv_recv.at[head]
            ).wait()

    g_pair = (gsend, gt)
    q_pair = (qsend, qt)
    o_pair = (ot, ofin)
    dq_pair = (dqt, dqfin)

    skip_spans = spans(width, 512)
    pieces = [(lat_hbm, lat)]
    for at, size in skip_spans:
        cols = pl.ds(at, size)
        pieces.append((skipw_hbm.at[:, cols], skipw.at[:, cols]))
    pieces += [(ups_hbm, ups), (wout_hbm, wout), (win_hbm, win)]
    loads = [
        pltpu.make_async_copy(src, dst, load_sem.at[i])
        for i, (src, dst) in enumerate(pieces)
    ]
    lat_load, *skip_loads, ups_load, wout_load, win_load = loads
    for load in loads:
        load.start()

    barrier = pltpu.get_barrier_semaphore()
    peers = [owner(lax.rem(me + step, column), line) for step in range(1, column)]
    peers += [owner(index, line + 1 - 2 * even) for index in range(column)]
    peers += [across(offset) for offset in range(2, rows_k)]
    peers.append(partner)
    for peer in peers:
        pl.semaphore_signal(barrier, inc=1, device_id=peer, device_id_type=MESH)

    def skip_copy(i):
        at, size = skip_spans[i]
        cols = pl.ds(at, size)
        return remote(
            skip_send.at[:, cols],
            skip_recv.at[:, cols],
            skip_ssem.at[i],
            skip_rsem.at[i],
            partner,
        )

    lat_load.wait()
    for i, (at, size) in enumerate(skip_spans):
        skip_loads[i].wait()
        product = dot(lat[...], skipw[:, pl.ds(at, size)])
        mixed[:, pl.ds(at, size)] = product
        skip_send[:, pl.ds(at, size)] = product.astype(BF16)
        if i == 0:
            pl.semaphore_wait(barrier, len(peers))

        @pl.when(is_lower)
        def _():
            skip_copy(i).start()

    def turn(source, i):
        block = source[:, pl.ds(i * CHUNK, CHUNK)]
        flip[pl.ds(i * CHUNK, CHUNK), :] = block.astype(F32).T.astype(BF16)

    ups_load.wait()
    for i in range(width // CHUNK):
        turn(ups, i)
    wout_load.wait()
    blank = jnp.zeros((PAD, CHUNK), F32)

    @pl.loop(0, column // 2)
    def _(i):
        rows = pl.ds(pl.multiple_of(i * 2 * depth, 16), 2 * depth)
        two = dot(wout[rows, :], flip[...])
        gsend[2 * i] = jnp.concatenate([blank, two[:depth]], 0).astype(BF16)
        gsend[2 * i + 1] = jnp.concatenate([blank, two[depth:]], 0).astype(BF16)

    @pl.when(is_lower)
    def _():
        for i in range(len(skip_spans)):
            skip_copy(i).wait_send()

    row_spans = spans(tok, 32)

    @pl.when(is_upper)
    def _():
        for i in range(len(skip_spans)):
            skip_copy(i).wait_recv()
        for at, size in row_spans:
            rows = pl.ds(at, size)
            total = mixed[rows, :] + skip_recv[rows, :].astype(F32)
            mixed[rows, :] = total
            binput[rows, :] = stats(total)[0].astype(BF16)

    @pl.when(is_lower)
    def _():
        binput[...] = lat[...]

    for at, size in row_spans:
        rows = pl.ds(at, size)
        normed[rows, :] = stats(binput[rows, :].astype(F32))[0].astype(BF16)

    for i in range(width // CHUNK):
        turn(normed, i)
    win_load.wait()

    def project(part):
        rows = pl.ds(pl.multiple_of(part * head_width, 16), head_width)
        projt[rows, :] = dot(win[rows, :], flip[...])

    @pl.loop(1, 3)
    def _(part):
        project(part)

    for head in range(column):
        keys = projt[pl.ds(head_width + head * depth, depth), :]
        values = projt[pl.ds(2 * head_width + head * depth, depth), :]
        kvsend[head] = jnp.concatenate([keys, values], 0).astype(BF16)
    kv_start()
    project(0)
    for head in range(column):
        queries = projt[pl.ds(head * depth, depth), :]
        qsend[head] = jnp.concatenate([queries, blank], 0).astype(BF16)
    head_start(QUERY, *q_pair)
    head_start(GRAD, *g_pair)

    @pl.loop(0, part_size)
    def _(at):
        kv_arrived(at)
        kvs_copy(0, at).start()
        kv_place(at).start()

    for offset in range(1, rows_k):

        @pl.loop(0, part_size)
        def _(at):
            kvx_copy(offset, at).start()

    def take(block):
        @pl.loop(0, part_size)
        def _(at):
            kvx_copy(block, at).wait_recv()
            kvs_copy(block, at).start()

    def natural(block):
        lane = lax.broadcasted_iota(jnp.int32, (q_tile, padded), 1)
        for at, size in spans(span, q_tile):
            cols = pl.ds(at, size)
            keys = kv[block, :padded, cols].astype(F32).T
            values = kv[block, depth - PAD :, cols].astype(F32).T
            knat[block, cols, :] = keys.astype(BF16)
            vnat[block, cols, :] = jnp.where(lane < PAD, 1.0, values).astype(BF16)

    head_arrived(QUERY, *q_pair)
    for at, size in spans(span, q_tile):
        rows = pl.ds(at, size)
        qnat[rows, :] = qt[:, rows].astype(F32).T.astype(BF16)

    order = [0, 1, 3, 2]
    tiles = span // q_tile
    middle_tile = tiles // 2

    def forward_rows(block, i):
        rows = pl.ds(i * q_tile, q_tile)
        scores = dot(qnat[rows, :], kv[block, :padded, :])
        top = jnp.max(scores, -1, keepdims=True)
        if block > 0:
            before = tops[order[order.index(block) - 1], rows, :]
            top = jnp.maximum(top, before)
        tops[block, rows, :] = top
        lifted = jnp.exp2((scores - top) * rate2).astype(BF16)
        exps[block, rows, :] = lifted
        term = dot(lifted, vnat[block])
        if block > 0:
            term += oacc[rows, :] * jnp.exp2((before - top) * rate2)
        oacc[rows, :] = term

    for block in order:

        @pl.loop(0, part_size)
        def _(at):
            kvs_copy(block, at).wait_recv()
            if block == 0:
                kv_place(at).wait()

        natural(block)
        for i in range(tiles):
            forward_rows(block, i)
            if i == middle_tile and block != order[-1]:
                take(order[order.index(block) + 1])

    head_arrived(GRAD, *g_pair)
    for at, size in spans(span, q_tile):
        rows = pl.ds(at, size)
        gnat[rows, :] = gt[:, rows].astype(F32).T
        total = oacc[rows, :]
        inverse = 1.0 / total[:, :1]
        mixed_values = (total * inverse).astype(BF16).astype(F32)
        ot[:, rows] = mixed_values.T.astype(BF16)
        delta[rows, :] = jnp.sum(gnat[rows, :] * mixed_values, -1, keepdims=True)
        last = tops[order[-1], rows, :]
        for block in range(rows_k):
            lift = jnp.exp2((tops[block, rows, :] - last) * rate2)
            facs[block, rows, :] = lift * inverse
        qacc[rows, :] = jnp.zeros((size, padded), F32)
    back_start(OUT, *o_pair)

    def backward_rows(block, i):
        rows = pl.ds(i * q_tile, q_tile)
        factor = facs[block, rows, :]
        grads = gnat[rows, :] * factor
        shift = delta[rows, :] * factor
        lifted = exps[block, rows, :]
        back = dot(grads.astype(BF16), kv[block, depth - PAD :, :]) - shift
        gscore = (lifted.astype(F32) * back).astype(BF16)
        qacc[rows, :] += dot(gscore, knat[block])
        keys = dot(qt[:, rows], gscore)
        values = dot(grads.T.astype(BF16), lifted)
        if i > 0:
            keys += kvacc[:padded, :]
            values += kvacc[padded:, :]
        kvacc[:padded, :] = keys
        kvacc[padded:, :] = values

    half_span = span // 2

    def joined(which):
        cols = pl.ds(pl.multiple_of(which * half_span, CHUNK), half_span)
        keys = kvacc[:padded, cols] * scale
        values = kvacc[padded:, cols]
        middle = keys[depth - PAD :] + values[: 2 * PAD]
        return jnp.concatenate([keys[: depth - PAD], middle, values[2 * PAD :]], 0)

    def pass_on(block):
        dkvs_copy(block).wait_recv()
        total = keep[block] + dkvtake[block].astype(F32)
        dkvpart[block - 1] = total.astype(BF16)
        dkvx_copy(block).start()

    turns = [2, 3, 1, 0]
    for n, block in enumerate(turns):
        for i in range(tiles):
            backward_rows(block, i)
            if n > 0 and i == middle_tile:
                pass_on(turns[n - 1])
            if block == 0:
                rows = pl.ds(i * q_tile, q_tile)
                dqt[:, rows] = (qacc[rows, :] * scale).T.astype(BF16)
                for at in range(q_tile // CHUNK):
                    back_one(DQ, i * (q_tile // CHUNK) + at, *dq_pair)
        dkvgive[block] = joined(1 - core).astype(BF16)
        dkvs_copy(block).start()
        keep[block] = joined(core)

    dkvs_copy(0).wait_recv()
    dkvx_copy(2).wait_recv()
    total = keep[0] + dkvtake[0].astype(F32) + dkvrecv[1].astype(F32)
    dkvown[0] = total.astype(BF16)
    dkv_start(0)

    back_arrived(OUT, *o_pair)
    for head in range(column):
        rows = pl.ds(head * depth, depth)
        projt[rows, :] = ofin[head].astype(F32)[PAD:]
    attended = projt[:head_width, :].T.astype(BF16)
    for at, size in spans(width, 512):
        cols = pl.ds(at, size)
        term = dot(attended, wout[:, cols])
        outv[:, cols] = (binput[:, cols].astype(F32) + term).astype(BF16)
    out_store = pltpu.make_async_copy(outv, out_hbm, store_sem.at[0])
    out_store.start()

    for offset in (1, 3):
        dkvx_copy(offset).wait_recv()
    dkvown[1] = (dkvrecv[0].astype(F32) + dkvrecv[2].astype(F32)).astype(BF16)
    dkv_start(1)

    def back_project(part):
        rows = pl.ds(part * head_width, head_width)
        gproj[part] = projt[rows, :].T.astype(BF16)

    back_arrived(DQ, *dq_pair)
    for head in range(column):
        projt[pl.ds(head * depth, depth), :] = dqfin[head].astype(F32)[:depth]
    back_project(0)
    for at, size in spans(width, 512):
        cols = pl.ds(at, size)
        ginput[:, cols] = dot(gproj[0], win[pl.ds(0, head_width), cols])
    dkv_arrived()
    for head in range(column):
        both = dkvfin[head].astype(F32)
        projt[pl.ds(head_width + head * depth, depth), :] = both[:depth]
        projt[pl.ds(2 * head_width + head * depth, depth), :] = both[depth:]
    for part in (1, 2):
        back_project(part)
    for at, size in spans(width, 512):
        cols = pl.ds(at, size)
        ginput[:, cols] += sum(
            dot(gproj[part], win[pl.ds(part * head_width, head_width), cols])
            for part in (1, 2)
        )

    def gm_copy(i):
        rows = pl.ds(*row_spans[i])
        return remote(
            gm_send.at[rows], gm_recv.at[rows], gm_ssem.at[i], gm_rsem.at[i], partner
        )

    for i, (at, size) in enumerate(row_spans):
        rows = pl.ds(at, size)
        hat, rate = stats(binput[rows, :].astype(F32))
        grad = ups[rows, :].astype(F32) + norm_back(hat, rate, ginput[rows, :])
        ginput[rows, :] = grad

        @pl.when(is_upper)
        def _():
            hat, rate = stats(mixed[rows, :])
            gm_send[rows, :] = norm_back(hat, rate, ginput[rows, :]).astype(BF16)
            gm_copy(i).start()

    @pl.when(is_upper)
    def _():
        ginput[...] = jnp.zeros_like(ginput)
        for i in range(width // CHUNK):
            turn(gm_send, i)

    @pl.when(is_lower)
    def _():
        for i in range(len(row_spans)):
            gm_copy(i).wait_recv()
        for i in range(width // CHUNK):
            turn(gm_recv, i)

    half = width // 2

    @pl.loop(0, 2)
    def _(i):
        rows = pl.ds(pl.multiple_of(i * half, 16), half)
        gnt[rows, :] = dot(skipw[rows, :], flip[...])

    out_store.wait()
    for i in range(width // CHUNK):
        cols = pl.ds(i * CHUNK, CHUNK)
        term = ginput[:, cols] + gnt[pl.ds(i * CHUNK, CHUNK), :].T
        outv[:, cols] = term.astype(BF16)
    glat_store = pltpu.make_async_copy(outv, glat_hbm, store_sem.at[1])
    glat_store.start()

    head_sent(GRAD, *g_pair)
    head_sent(QUERY, *q_pair)
    back_sent(OUT, *o_pair)
    back_sent(DQ, *dq_pair)
    kv_sent()
    dkv_sent(0)
    dkv_sent(1)

    @pl.loop(0, part_size)
    def _(at):
        kvs_copy(0, at).wait_send()
        for offset in range(1, rows_k):
            kvx_copy(offset, at).wait_send()
            kvs_copy(offset, at).wait_send()

    dkvs_copy(0).wait_send()
    for offset in range(1, rows_k):
        dkvx_copy(offset).wait_send()
        dkvs_copy(offset).wait_send()

    @pl.when(is_upper)
    def _():
        for i in range(len(row_spans)):
            gm_copy(i).wait_send()

    glat_store.wait()


def settle(out, glat, out_hbm, glat_hbm, held, sem):
    ins = [
        pltpu.make_async_copy(out, held.at[0], sem.at[0]),
        pltpu.make_async_copy(glat, held.at[1], sem.at[1]),
    ]
    outs = [
        pltpu.make_async_copy(held.at[0], out_hbm, sem.at[2]),
        pltpu.make_async_copy(held.at[1], glat_hbm, sem.at[3]),
    ]
    for copy in ins:
        copy.start()
    for copy, onward in zip(ins, outs):
        copy.wait()
        onward.start()
    for copy in outs:
        copy.wait()


def body(rows_h, rows_k, latents, skip_weight, project_in, project_out, upstream):
    tok, width = latents.shape[1:]
    head_width = project_out.shape[1]
    column = rows_h * CORES
    depth = head_width // column
    padded = depth + PAD
    span = column * tok
    part = span // 2
    n_skip = len(spans(width, 512))
    n_rows = len(spans(tok, 32))
    wide = (tok, width)
    vmem = pltpu.VMEM
    dma = pltpu.SemaphoreType.DMA
    scratch = [
        vmem(wide, BF16),
        vmem((width, width), BF16),
        vmem((3 * head_width, width), BF16),
        vmem((head_width, width), BF16),
        vmem(wide, BF16),
        vmem(wide, BF16),
        vmem(wide, BF16),
        vmem(wide, F32),
        vmem(wide, BF16),
        vmem(wide, BF16),
        vmem((width, tok), BF16),
        vmem((3 * head_width, tok), F32),
        vmem((column, padded, tok), BF16),
        vmem((column, 2 * depth, tok), BF16),
        vmem((column, padded, tok), BF16),
        vmem((padded, span), BF16),
        vmem((padded, span), BF16),
        vmem((rows_k, 2 * depth, span), BF16),
        vmem((rows_k, span, padded), BF16),
        vmem((rows_k, span, padded), BF16),
        vmem((span, padded), BF16),
        vmem((span, padded), F32),
        vmem((rows_k, span, span), BF16),
        vmem((rows_k, span, 1), F32),
        vmem((rows_k, span, 1), F32),
        vmem((span, 1), F32),
        vmem((span, padded), F32),
        vmem((span, padded), F32),
        vmem((2 * padded, span), F32),
        vmem((padded, span), BF16),
        vmem((padded, span), BF16),
        vmem((2, 2 * depth, part), BF16),
        vmem((rows_k, 2 * depth, part), F32),
        vmem((rows_k, 2 * depth, part), BF16),
        vmem((rows_k, 2 * depth, part), BF16),
        vmem((rows_k - 1, 2 * depth, part), BF16),
        vmem((rows_k - 1, 2 * depth, part), BF16),
        vmem((2, 2 * depth, part), BF16),
        vmem((column, padded, tok), BF16),
        vmem((column, padded, tok), BF16),
        vmem((column, 2 * depth, tok), BF16),
        vmem((3, tok, head_width), BF16),
        vmem((width, tok), F32),
        vmem(wide, F32),
        vmem(wide, BF16),
        vmem(wide, BF16),
        vmem(wide, BF16),
        dma((4 + n_skip,)),
        dma((2,)),
        dma((4, column)),
        dma((4, column)),
        dma((rows_h,)),
        dma((column // 2,)),
        dma((rows_k - 1, column // 2)),
        dma((rows_k - 1, column // 2)),
        dma((rows_k, column // 2)),
        dma((rows_k, column // 2)),
        dma((column // 2,)),
        dma((rows_k,)),
        dma((rows_k,)),
        dma((2, column // 2)),
        dma((column,)),
        dma((rows_k - 1,)),
        dma((rows_k - 1,)),
        dma((n_skip,)),
        dma((n_skip,)),
        dma((n_rows,)),
        dma((n_rows,)),
    ]
    out, glat = pl.pallas_call(
        functools.partial(kernel, rows_h, rows_k),
        out_shape=[jax.ShapeDtypeStruct(wide, BF16)] * 2,
        in_specs=[pl.BlockSpec(memory_space=pl.ANY)] * 5,
        out_specs=[pl.BlockSpec(memory_space=pl.ANY)] * 2,
        scratch_shapes=scratch,
        compiler_params=pltpu.CompilerParams(
            collective_id=0, has_side_effects=True, vmem_limit_bytes=56 * 2**20
        ),
    )(latents[0], skip_weight[0], project_in[0].T, project_out[0], upstream[0])
    out, glat = pl.pallas_call(
        settle,
        out_shape=[jax.ShapeDtypeStruct(wide, BF16)] * 2,
        in_specs=[pl.BlockSpec(memory_space=pl.ANY)] * 2,
        out_specs=[pl.BlockSpec(memory_space=pl.ANY)] * 2,
        scratch_shapes=[vmem((2,) + wide, BF16), dma((4,))],
        compiler_params=pltpu.CompilerParams(vmem_limit_bytes=56 * 2**20),
    )(out, glat)
    return out[None], glat[None]


def solution(mesh):
    rows_h = HEADS // 2
    rows_k = mesh.shape["seq"] // HEADS
    return jax.shard_map(
        functools.partial(body, rows_h, rows_k),
        mesh=mesh,
        in_specs=(
            P("section", "seq", None),
            P("section", None, None),
            P("section", None, None),
            P("section", None, None),
            P("section", "seq", None),
        ),
        out_specs=(P("section", "seq", None), P("section", "seq", None)),
        check_vma=False,
    )
```
